32 devices in a mesh: row: 4 (over y, core), seq: 8 (over z, x).
Axes of the slice: x: 2, y: 2, z: 4, core: 2. Of those that a mesh axis runs over, the one named last changes fastest.
Arguments:
- tokens: bfloat16 [2, 4, 1024, 1024], P(None, 'row', 'seq'), may hold values from -6 to 6
- cotangent: bfloat16 [2, 4, 1024, 1024], P(None, 'row', 'seq'), may hold values from -6 to 6
- row_lengths: int32 [2, 4], P(None, 'row'), may hold values from 256 to 1024, as said below
- norm1_gain: float32 [1024], replicated, may hold values from 0.5 to 1.5
- w_in: bfloat16 [1024, 6144], P('seq'), may hold values from -0.1875 to 0.1875
- w_router: bfloat16 [1024, 24], replicated, may hold values from -0.25 to 0.25
- conv_weight: float32 [4, 5120], replicated, may hold values from -3 to 3
- a_log: float32 [8], replicated, as said below
- dt_bias: float32 [8], replicated, may hold values from -1 to 1
- head_gain: float32 [128], replicated, may hold values from 0.5 to 1.5
- w_out: bfloat16 [1024, 1024], P('seq'), may hold values from -0.375 to 0.375
- norm2_gain: float32 [1024], replicated, may hold values from 0.5 to 1.5
- w_gu: bfloat16 [1024, 5632], P('seq'), may hold values from -0.1875 to 0.1875
- w_down: bfloat16 [2816, 1024], P('seq'), may hold values from -0.109375 to 0.109375
Outputs:
- out: bfloat16 [2, 4, 1024, 1024], P(None, 'row', 'seq')
- grad_tokens: float32 [2, 4, 1024, 1024], P(None, 'row', 'seq')
- grad_norm1: float32 [1024], replicated
- grad_w_in: float32 [1024, 6144], P('seq')
- grad_w_router: float32 [1024, 24], replicated
- grad_conv: float32 [4, 5120], replicated
- grad_a_log: float32 [8], replicated
- grad_dt_bias: float32 [8], replicated
- grad_head_gain: float32 [128], replicated
- grad_w_out: float32 [1024, 1024], P('seq')
- grad_norm2: float32 [1024], replicated
- grad_w_gu: float32 [1024, 5632], P('seq')
- grad_w_down: float32 [2816, 1024], P('seq')
The draws below stay inside these ranges and needn't reach their ends.
Inputs may be any that keep to these rules, and one draw needn't show every extreme that they name: `row_lengths`: each length is 1024 or 256; for every index of the rows, some micro-batch's row there has 1024. `a_log`: each entry lies between log(0.05 / 1024) and log(0.05).
All inputs are finite; a program needn't handle non-finite values.
Results may differ from the reference program's by a relative error of at most 0.02.
The reference program's roundings to bfloat16 on the way count: a program that leaves them out, or rounds other values in their place, can miss the bound.
Values may be sent and summed in bfloat16 or wider, within the bound.
No kernel may reach another device: no remote copies, remote signals or barrier semaphores. Data moves between devices by JAX's collectives and lax.ppermute only.
A program may use at most 448 MiB of HBM per device.

```python
import math
import jax
import jax.numpy as jnp
from jax import lax

D = 1024
H = 8
HD = 128
FF = 2816
NH = 2
KS = 4
GROUP = 64
MICRO = 2
BROWS = 4
LMAX = 1024
CIN = 6144
CONV = 5120
BA = 24


def draw_row_lengths(key, part):
    key = jax.random.fold_in(key, 11)
    first_key, second_key = jax.random.split(key)
    coin_flip = jax.random.randint(first_key, (MICRO, BROWS), 0, 2)
    chosen = jax.random.randint(second_key, (BROWS,), 0, MICRO)
    full_row = (coin_flip == 0) | (jnp.arange(MICRO)[:, None] == chosen[None, :])
    return jnp.where(full_row, LMAX, LMAX // 4).astype(jnp.int32)


def draw_a_log(key, part):
    key = jax.random.fold_in(key, 7)
    low_end = math.log(0.3 / LMAX)
    high_end = math.log(0.05)
    return jax.random.uniform(key, (H,), jnp.float32, low_end, high_end)


def level_of(stream_key, shape, cuts, least, largest):
    def one(axis_at, blocks):
        draws = jax.random.uniform(jax.random.fold_in(jax.random.fold_in(stream_key, 6), axis_at), (blocks,), jnp.float32, least / len(cuts), largest / len(cuts))
        return jnp.repeat(jnp.exp(draws), shape[axis_at] // blocks).reshape((-1,) + (1,) * (len(shape) - axis_at - 1))

    factor_of = one(*cuts[0])
    for cut in cuts[1:]:
        factor_of = factor_of * one(*cut)
    return factor_of


def centred(stream_key, dims, width, reach, cuts=(), kind=jnp.bfloat16):
    array = jax.random.normal(stream_key, dims, jnp.float32) * width
    if len(cuts) > 0:
        array = level_of(stream_key, dims, cuts, -0.22, 0.18) * array
    return jnp.clip(array, min=-reach, max=reach).astype(kind)


def setup_inputs(seed: int = 0) -> dict:
    seeds = jax.random.split(jax.random.key(seed), 15)
    return {
        "tokens": centred(seeds[0], (MICRO, BROWS, LMAX, D), 1.0, 6.0, ((1, 4), (2, 8))),
        "cotangent": centred(seeds[1], (MICRO, BROWS, LMAX, D), 1.0, 6.0, ((1, 4), (2, 8))),
        "row_lengths": draw_row_lengths(jax.random.fold_in(seeds[14], 71), 0),
        "norm1_gain": jnp.clip(1.0 + 0.1 * jax.random.normal(seeds[3], (D,), jnp.float32), 0.5, 1.5),
        "w_in": centred(seeds[4], (D, CIN), D ** -0.5, 0.1875, ((0, 8),)),
        "w_router": centred(seeds[5], (D, BA), (D // 2) ** -0.5, 0.25),
        "conv_weight": centred(seeds[6], (KS, CONV), KS ** -0.5, 3.0, (), jnp.float32),
        "a_log": draw_a_log(jax.random.fold_in(seeds[14], 71), 0),
        "dt_bias": jnp.clip(jax.random.uniform(seeds[8], (H,), jnp.float32, -1.0, 1.0), -1.0, 1.0),
        "head_gain": jnp.clip(1.0 + 0.1 * jax.random.normal(seeds[9], (HD,), jnp.float32), 0.5, 1.5),
        "w_out": centred(seeds[10], (D, D), (D // 4) ** -0.5, 0.375, ((0, 8),)),
        "norm2_gain": jnp.clip(1.0 + 0.1 * jax.random.normal(seeds[11], (D,), jnp.float32), 0.5, 1.5),
        "w_gu": centred(seeds[12], (D, 2 * FF), D ** -0.5, 0.1875, ((0, 8),)),
        "w_down": centred(seeds[13], (FF, D), FF ** -0.5, 0.109375, ((0, 8),)),
    }


HIGH = lax.Precision.HIGHEST
EPS_NORM = 1e-05
EPS_UNIT = 1e-06

@jax.custom_vjp
def low(v):
    return lax.optimization_barrier(v.astype(jnp.bfloat16)).astype(jnp.float32)

@jax.custom_vjp
def low_back(v):
    return v

def low_keep(v):
    return (low(v), None)

def low_pass(kept, grad):
    return (grad,)

def back_keep(v):
    return (v, None)

def back_low(kept, grad):
    return (low(grad),)
low.defvjp(low_keep, low_pass)
low_back.defvjp(back_keep, back_low)

def rms_scale(values):
    return lax.rsqrt(lax.optimization_barrier(jnp.mean(values * values, axis=-1, keepdims=True)) + EPS_NORM)

def mixer_inputs(extended, conv_weight, router, a_log, dt_bias, n_heads, head_dim, n_keys):
    n_taps = conv_weight.shape[0]
    n_rows = extended.shape[0] - n_taps + 1
    conv_sum = conv_weight[0] * extended[0:n_rows]
    for offset in range(1, n_taps):
        conv_sum = conv_sum + conv_weight[offset] * extended[offset:offset + n_rows]
    activated = jax.nn.silu(conv_sum)
    model_width = n_heads * head_dim
    queries = activated[:, :model_width].reshape(n_rows, n_heads, head_dim)
    key_vecs = activated[:, model_width:model_width + n_keys * model_width].reshape(n_rows, n_keys, n_heads, head_dim)
    val_vecs = activated[:, model_width + n_keys * model_width:].reshape(n_rows, n_keys, n_heads, head_dim)
    queries = queries * lax.rsqrt(lax.optimization_barrier(jnp.sum(queries * queries, axis=-1, keepdims=True)) + EPS_UNIT)
    key_vecs = key_vecs * lax.rsqrt(lax.optimization_barrier(jnp.sum(key_vecs * key_vecs, axis=-1, keepdims=True)) + EPS_UNIT)
    beta_vals = jax.nn.sigmoid(router[:, :n_keys * n_heads]).reshape(n_rows, n_keys, n_heads)
    decays = -jnp.exp(a_log) * jax.nn.softplus(router[:, n_keys * n_heads:] + dt_bias)
    return (queries, key_vecs, val_vecs, beta_vals, decays)

def head_mix(mixed_out, gate_pre, head_gain):
    n_rows = mixed_out.shape[0]
    normed = mixed_out * lax.rsqrt(lax.optimization_barrier(jnp.mean(mixed_out * mixed_out, axis=-1, keepdims=True)) + EPS_NORM) * head_gain
    return normed.reshape(n_rows, -1) * jax.nn.silu(gate_pre)

def recurrence(queries, key_vecs, val_vecs, beta_vals, decays):
    n_tok, n_heads, head_dim = queries.shape
    n_keys = key_vecs.shape[1]

    def token_step(carried, inputs_now):
        q_now, k_now, v_now, b_now, g_now = inputs_now
        carried = jnp.exp(g_now)[:, None, None] * carried
        for key_num in range(n_keys):
            guess = jnp.einsum('hvk,hk->hv', carried, k_now[key_num], precision=HIGH)
            carried = carried + b_now[key_num][:, None, None] * (v_now[key_num] - guess)[:, :, None] * k_now[key_num][:, None, :]
        return (carried, jnp.einsum('hvk,hk->hv', carried, q_now, precision=HIGH))

    def block_step(carried, block_in):
        return lax.scan(token_step, carried, block_in)
    blocks = jax.tree.map(lambda array_in: array_in.reshape((n_tok // GROUP, GROUP) + array_in.shape[1:]), (queries, key_vecs, val_vecs, beta_vals, decays))
    start_state = jnp.zeros((n_heads, head_dim, head_dim), jnp.float32)
    _, block_outs = lax.scan(jax.checkpoint(block_step), start_state, blocks)
    return block_outs.reshape(n_tok, n_heads, head_dim)

def layer_row(params, x_row):
    norm1_gain, w_in, w_router, conv_weight, a_log, dt_bias, head_gain, w_out, norm2_gain, w_gu, w_down = params
    n_taps = conv_weight.shape[0]
    conv_width = conv_weight.shape[1]
    normed_in = low(x_row * rms_scale(x_row) * norm1_gain)
    projected = low(low_back(jnp.dot(normed_in, w_in, precision=HIGH)))
    router = low_back(jnp.dot(normed_in, w_router, precision=HIGH))
    extended = jnp.pad(projected[:, :conv_width], ((n_taps - 1, 0), (0, 0)))
    queries, key_vecs, val_vecs, beta_vals, decays = mixer_inputs(extended, conv_weight, router, a_log, dt_bias, H, HD, NH)
    mixed_out = recurrence(low(queries), low(key_vecs), low(val_vecs), beta_vals, decays)
    gated_out = low(head_mix(mixed_out, projected[:, conv_width:], head_gain))
    residual = x_row + low_back(jnp.dot(gated_out, w_out, precision=HIGH))
    normed_mid = low(residual * rms_scale(residual) * norm2_gain)
    gate_up = low_back(jnp.dot(normed_mid, w_gu, precision=HIGH))
    act_low = low(jax.nn.silu(gate_up[:, :FF]) * gate_up[:, FF:])
    return residual + low_back(jnp.dot(act_low, w_down, precision=HIGH))

def reference(tokens, cotangent, row_lengths, norm1_gain, w_in, w_router, conv_weight, a_log, dt_bias, head_gain, w_out, norm2_gain, w_gu, w_down):
    params = (norm1_gain, w_in.astype(jnp.float32), w_router.astype(jnp.float32), conv_weight, a_log, dt_bias, head_gain, w_out.astype(jnp.float32), norm2_gain, w_gu.astype(jnp.float32), w_down.astype(jnp.float32))
    row_set = tokens.astype(jnp.float32).reshape(-1, LMAX, D)

    def forward(param_set, rows_in):
        return lax.map(jax.checkpoint(lambda one_row: layer_row(param_set, one_row)), rows_in)
    result, pull_back = jax.vjp(forward, params, row_set)
    places = jnp.arange(LMAX, dtype=jnp.int32)
    live_mask = (places[None, :] < row_lengths.reshape(-1).astype(jnp.int32)[:, None]).astype(jnp.float32)
    seed_grad = cotangent.astype(jnp.float32).reshape(-1, LMAX, D) * live_mask[:, :, None]
    param_grads, d_rows = pull_back(seed_grad)
    full_shape = tokens.shape
    return (result.reshape(full_shape).astype(jnp.bfloat16), d_rows.reshape(full_shape), param_grads[0], param_grads[1], param_grads[2], param_grads[3], param_grads[4], param_grads[5], param_grads[6], param_grads[7], param_grads[8], param_grads[9], param_grads[10])
```

```python
from functools import partial

import jax
import jax.numpy as jnp
from jax import lax
from jax.experimental import pallas as pl
from jax.experimental.pallas import tpu as pltpu
from jax.sharding import PartitionSpec as P

BF = jnp.bfloat16
F32 = jnp.float32
EPS_NORM = 1e-05
EPS_UNIT = 1e-06
CH = 64
ST = 128
HALO = 16
LANES = 128
VMEM_BYTES = 50 * 1024 * 1024


def halves(value):
    high = value.astype(BF)
    return (high, (value - high.astype(F32)).astype(BF))


def dot(left, right, over_left=1, over_right=0):
    return lax.dot_general(
        left, right, (((over_left,), (over_right,)), ((), ())), preferred_element_type=F32
    )


def mm(left, right, over_left=1, over_right=0):
    left = left if isinstance(left, tuple) else (left,)
    right = right if isinstance(right, tuple) else (right,)
    total = dot(left[0], right[0], over_left, over_right)
    if len(right) > 1:
        total = total + dot(left[0], right[1], over_left, over_right)
    if len(left) > 1:
        total = total + dot(left[1], right[0], over_left, over_right)
    return total


def exact_sum(ones, value):
    high = value.astype(BF)
    rest = value - high.astype(F32)
    mid = rest.astype(BF)
    low = (rest - mid.astype(F32)).astype(BF)
    return dot(ones, high) + dot(ones, mid) + dot(ones, low)


def step_orders():
    row = lax.broadcasted_iota(jnp.int32, (ST, ST), 0)
    col = lax.broadcasted_iota(jnp.int32, (ST, ST), 1)
    order = lambda i: 2 * (i & (CH - 1)) + (i >> 6)
    return order(row), order(col)


def sees():
    row = lax.broadcasted_iota(jnp.int32, (CH, ST), 0)
    col = lax.broadcasted_iota(jnp.int32, (CH, ST), 1)
    return (col & (CH - 1)) <= row


def twice(value):
    return jnp.concatenate([value, value], axis=0)


def log_decays(router, par):
    lane = lax.broadcasted_iota(jnp.int32, (CH, LANES), 1)
    pre = router + par[2:3]
    soft = jnp.maximum(pre, 0.0) + jnp.log1p(jnp.exp(-jnp.abs(pre)))
    decay = -jnp.exp(par[1:2]) * soft
    row = lax.broadcasted_iota(jnp.int32, (CH, CH), 0)
    col = lax.broadcasted_iota(jnp.int32, (CH, CH), 1)
    below = jnp.where(col <= row, 1.0, 0.0).astype(BF)
    total = exact_sum(below, jnp.where(lane == 2, decay, 0.0))
    return decay, total


def gate_columns(router, par):
    strength = jax.nn.sigmoid(router)
    decay, total = log_decays(router, par)
    beta = jnp.concatenate([strength[:, 0:1], strength[:, 1:2]], axis=0)
    doubled = twice(total)
    g_col = doubled[:, 2:3]
    g_row = doubled.T[2:3, :]
    g_last = total[CH - 1 : CH, 2:3]
    return beta, g_col, g_row, g_last, decay


def seen_decay(g_col, g_row, visible):
    return jnp.where(visible, jnp.exp(jnp.where(visible, g_col[:CH] - g_row, 0.0)), 0.0)


def unit(value):
    scale = lax.rsqrt(jnp.sum(value * value, axis=-1, keepdims=True) + EPS_UNIT)
    return value * scale, scale


def taps_sum(window, weight, start):
    total = weight[0:1] * window[pl.ds(start + 5, CH), :]
    for tap in range(1, 4):
        total = total + weight[tap : tap + 1] * window[pl.ds(start + 5 + tap, CH), :]
    return total


def fill_window(window, proj_ref, halo_ref, is_first):
    width = window.shape[1]
    edge = halo_ref[0, :, :width].astype(F32)[HALO - 8 :]
    window[0:8, :] = jnp.where(is_first, 0.0, edge)
    window[8:, :] = proj_ref[0, :, :width].astype(F32)


def prep_kernel(
    count, proj_ref, halo_ref, router_ref, taps_ref, par_ref,
    solve_ref, wmat_ref, umat_ref, seen_ref, q_ref, k_ref, window,
):
    fill_window(window, proj_ref, halo_ref, pl.program_id(1) == 0)
    weight = taps_ref[...]
    par = par_ref[...]
    o_row, o_col = step_orders()
    strict = o_row > o_col
    eye = jnp.where(o_row == o_col, 1.0, 0.0)
    visible = sees()
    many = range(count)
    lower, rights = [], []
    for n in many:
        conv = taps_sum(window, weight, n * CH)
        act = conv * jax.nn.sigmoid(conv)
        q = unit(act[:, 0:128])[0].astype(BF)
        k = jnp.concatenate(
            [unit(act[:, 128:256])[0], unit(act[:, 256:384])[0]], axis=0
        ).astype(BF)
        v = jnp.concatenate([act[:, 384:512], act[:, 512:640]], axis=0).astype(BF)
        beta, g_col, g_row, _, _ = gate_columns(
            router_ref[0, n * CH : (n + 1) * CH, :], par
        )
        gaps = seen_decay(g_col, g_row, visible)
        lower.append(jnp.where(strict, beta * twice(gaps) * dot(k, k, 1, 1), 0.0))
        kf = k.astype(F32)
        rights.append(
            jnp.concatenate([beta * jnp.exp(g_col) * kf, beta * v.astype(F32)], axis=1)
        )
        seen_ref[0, n] = gaps * dot(q, k, 1, 1)
        q_ref[0, n] = q
        k_ref[0, n] = k
    inverse = [eye - jnp.where((o_row >> 1) == (o_col >> 1), part, 0.0) for part in lower]
    for level in range(1, 7):
        at = ((o_row >> level) ^ (o_col >> level)) == 1
        parts = [halves(jnp.where(at, part, 0.0)) for part in lower]
        known = [halves(value) for value in inverse]
        inner = [halves(mm(parts[n], known[n])) for n in many]
        inverse = [inverse[n] - mm(known[n], inner[n]) for n in many]
    for n in many:
        solve_ref[0, n] = inverse[n]
        both = mm(halves(inverse[n]), halves(rights[n]))
        wmat_ref[0, n] = both[:, :128]
        umat_ref[0, n] = both[:, 128:]


def head_norm(mixed):
    return lax.rsqrt(jnp.mean(mixed * mixed, axis=-1, keepdims=True) + EPS_NORM)


def scan_kernel(
    n_micro, count, wmat_ref, umat_ref, seen_ref, q_ref, k_ref, router_ref, gate_ref, par_ref,
    out_ref, mixed_ref, news_ref, state_ref, state,
):
    @pl.when(pl.program_id(0) == 0)
    def _():
        state[...] = jnp.zeros_like(state)

    par = par_ref[...]
    now = [state[m] for m in range(n_micro)]
    for n in range(count):
        rows = slice(n * CH, (n + 1) * CH)
        for m in range(n_micro):
            _, g_col, _, g_last, _ = gate_columns(router_ref[m, rows, :], par)
            held = halves(now[m])
            state_ref[m, n] = now[m]
            news = umat_ref[m, n] - mm(halves(wmat_ref[m, n]), held)
            news_ref[m, n] = news
            news_h = halves(news)
            ends = halves(jnp.exp(g_last - g_col) * k_ref[m, n].astype(F32))
            now[m] = jnp.exp(g_last) * now[m] + mm(ends, news_h, 0, 0)
            mixed = jnp.exp(g_col[:CH]) * mm(q_ref[m, n], held) + mm(halves(seen_ref[m, n]), news_h)
            mixed_ref[m, n] = mixed
            gate = gate_ref[m, rows, :].astype(F32)
            out_ref[m, rows, :] = (
                mixed * head_norm(mixed) * par[0:1] * (gate * jax.nn.sigmoid(gate))
            ).astype(BF)
    for m in range(n_micro):
        state[m] = now[m]


def scan_back_kernel(
    n_micro, count, wmat_ref, seen_ref, q_ref, k_ref, router_ref, gate_ref, par_ref, mixed_ref, d_out_ref,
    d_mixed_ref, d_news_ref, d_state_ref, d_gate_ref, gain_ref, state,
):
    @pl.when(pl.program_id(0) == 0)
    def _():
        state[...] = jnp.zeros_like(state)
        gain_ref[...] = jnp.zeros_like(gain_ref)

    par = par_ref[...]
    now = [state[m] for m in range(n_micro)]
    gain = jnp.zeros((1, LANES), F32)
    for n in reversed(range(count)):
        rows = slice(n * CH, (n + 1) * CH)
        for m in range(n_micro):
            _, g_col, _, g_last, _ = gate_columns(router_ref[m, rows, :], par)
            mixed = mixed_ref[m, n]
            gate = gate_ref[m, rows, :].astype(F32)
            d_out = d_out_ref[m, rows, :].astype(F32)
            scale = head_norm(mixed)
            normed = mixed * scale
            sig = jax.nn.sigmoid(gate)
            silu = gate * sig
            gain = gain + jnp.sum(d_out * normed * silu, axis=0, keepdims=True)
            d_gate = d_out * normed * par[0:1] * (sig * (1.0 + gate * (1.0 - sig)))
            d_gate_ref[m, rows, :] = d_gate.astype(BF)
            d_normed = d_out * par[0:1] * silu
            d_mixed = scale * d_normed - mixed * scale**3 * jnp.mean(
                d_normed * mixed, axis=-1, keepdims=True
            )
            d_mixed_ref[m, n] = d_mixed
            d_mixed_h = halves(d_mixed)
            d_state_ref[m, n] = now[m]
            ends = halves(jnp.exp(g_last - g_col) * k_ref[m, n].astype(F32))
            d_news = mm(halves(seen_ref[m, n]), d_mixed_h, 0, 0) + mm(ends, halves(now[m]))
            d_news_ref[m, n] = d_news
            q_eff = halves(jnp.exp(g_col[:CH]) * q_ref[m, n].astype(F32))
            now[m] = (
                jnp.exp(g_last) * now[m]
                + mm(q_eff, d_mixed_h, 0, 0)
                - mm(halves(wmat_ref[m, n]), halves(d_news), 0, 0)
            )
    gain_ref[0:1, :] += gain
    for m in range(n_micro):
        state[m] = now[m]


def unit_back(grad, value, scale):
    return scale * grad - value * scale**3 * jnp.sum(grad * value, axis=-1, keepdims=True)


def grads_kernel(
    count, proj_ref, halo_ref, router_ref, taps_ref, par_ref, solve_ref, seen_ref, news_ref, state_ref,
    d_mixed_ref, d_news_ref, d_state_ref, d_gate_ref,
    d_ext_ref, g_taps_ref, g_par_ref, window, d_window,
):
    step = pl.program_id(1)
    size = count * CH
    fill_window(window, proj_ref, halo_ref, step == pl.num_programs(1) - 1)

    @pl.when((step == 0) & (pl.program_id(0) == 0))
    def _():
        g_taps_ref[...] = jnp.zeros_like(g_taps_ref)
        g_par_ref[...] = jnp.zeros_like(g_par_ref)

    @pl.when(step == 0)
    def _():
        d_window[size:, :] = jnp.zeros((8, d_window.shape[1]), F32)

    @pl.when(step > 0)
    def _():
        d_window[size:, :] = d_window[0:8, :]

    weight = taps_ref[...]
    par = par_ref[...]
    o_row, o_col = step_orders()
    strict = o_row > o_col
    visible = sees()
    row = lax.broadcasted_iota(jnp.int32, (CH, CH), 0)
    col = lax.broadcasted_iota(jnp.int32, (CH, CH), 1)
    above = jnp.where(col >= row, 1.0, 0.0).astype(BF)
    lane = lax.broadcasted_iota(jnp.int32, (CH, LANES), 1)
    last = lax.broadcasted_iota(jnp.int32, (CH, LANES), 0) == CH - 1
    g_alog = jnp.zeros((1, LANES), F32)
    g_dt = jnp.zeros((1, LANES), F32)
    for n in range(count):
        rows = slice(n * CH, (n + 1) * CH)
        conv = taps_sum(window, weight, n * CH)
        sig = jax.nn.sigmoid(conv)
        act = conv * sig
        qn, q_scale = unit(act[:, 0:128])
        k0n, k0_scale = unit(act[:, 128:256])
        k1n, k1_scale = unit(act[:, 256:384])
        q = qn.astype(BF)
        k = jnp.concatenate([k0n, k1n], axis=0).astype(BF)
        kf, qf = k.astype(F32), q.astype(F32)
        router = router_ref[0, rows, :]
        beta, g_col, g_row, g_last, decay = gate_columns(router, par)
        gaps = seen_decay(g_col, g_row, visible)
        ratio = jnp.where(strict, twice(gaps), 0.0)
        grown = jnp.exp(g_col)
        left = jnp.exp(g_last - g_col)
        gram = dot(k, k, 1, 1)
        state = state_ref[0, n]
        state_h = halves(state)
        news = news_ref[0, n]
        news_h = halves(news)
        d_mixed_h = halves(d_mixed_ref[0, n])
        d_state = d_state_ref[0, n]
        d_right = mm(halves(solve_ref[0, n]), halves(d_news_ref[0, n]), 0, 0)
        d_right_h = halves(d_right)
        d_lower = jnp.where(strict, -mm(d_right_h, news_h, 1, 1), 0.0)
        d_pre = (1.0 - beta) * jnp.sum(d_right * news, axis=-1, keepdims=True)
        d_v = beta * d_right
        d_grown_k = -beta * mm(d_right_h, state_h, 1, 1)
        d_k = grown * d_grown_k
        d_gram = beta * ratio * d_lower
        both = d_gram * gram
        d_g = jnp.sum(both, axis=-1, keepdims=True) + jnp.sum(d_k * kf, axis=-1, keepdims=True)
        d_g_row = -jnp.sum(both, axis=0, keepdims=True)
        d_k = d_k + mm(halves(d_gram + d_gram.T), k)
        d_seen = mm(d_mixed_h, news_h, 1, 1)
        d_scores = halves(d_seen * gaps)
        seen_both = d_seen * seen_ref[0, n]
        d_q_grown = grown[:CH] * mm(d_mixed_h, state_h, 1, 1)
        d_q = d_q_grown + mm(d_scores, k)
        d_k = d_k + mm(d_scores, q, 0, 0)
        d_g_q = jnp.sum(seen_both + d_q_grown * qf, axis=-1, keepdims=True)
        d_g_row = d_g_row - jnp.sum(seen_both, axis=0, keepdims=True)
        d_ends = left * mm(news_h, halves(d_state), 1, 1)
        d_k = d_k + d_ends
        ends_sum = jnp.sum(d_ends * kf, axis=-1, keepdims=True)
        d_g = d_g - ends_sum
        d_last = jnp.sum(ends_sum, axis=0, keepdims=True) + jnp.exp(g_last) * jnp.sum(
            jnp.sum(d_state * state, axis=-1, keepdims=True), axis=0, keepdims=True
        )
        d_g_rows = jnp.broadcast_to(d_g_row, (LANES, ST)).T
        d_g_tok = d_g_q + d_g[:CH] + d_g[CH:] + d_g_rows[:CH] + d_g_rows[CH:]
        d_g_tok = d_g_tok + jnp.where(last, d_last, 0.0)
        d_decay = exact_sum(above, d_g_tok)
        d_soft = -jnp.exp(par[1:2]) * jax.nn.sigmoid(router + par[2:3]) * d_decay
        d_router = jnp.where(
            lane == 0,
            d_pre[:CH],
            jnp.where(lane == 1, d_pre[CH:], jnp.where(lane == 2, d_soft, 0.0)),
        )
        width = window.shape[1]
        d_ext_ref[0, rows, width : width + LANES] = d_gate_ref[0, rows, :]
        d_ext_ref[0, rows, width + LANES :] = d_router.astype(BF)
        g_alog = g_alog + jnp.sum(
            jnp.where(lane == 2, d_decay * decay, 0.0), axis=0, keepdims=True
        )
        g_dt = g_dt + jnp.sum(jnp.where(lane == 2, d_soft, 0.0), axis=0, keepdims=True)
        d_act = jnp.concatenate(
            [
                unit_back(d_q, act[:, 0:128], q_scale),
                unit_back(d_k[:CH], act[:, 128:256], k0_scale),
                unit_back(d_k[CH:], act[:, 256:384], k1_scale),
                d_v[:CH],
                d_v[CH:],
            ],
            axis=1,
        )
        d_window[rows, :] = d_act * (sig * (1.0 + conv * (1.0 - sig)))
    g_par_ref[1:2, :] += g_alog
    g_par_ref[2:3, :] += g_dt
    for n in range(count):
        start = n * CH
        here = d_window[pl.ds(start, CH), :]
        total = weight[3:4] * here
        for tap in range(3):
            total = total + weight[tap : tap + 1] * d_window[pl.ds(start + 3 - tap, CH), :]
        d_ext_ref[0, pl.ds(start, CH), : total.shape[1]] = total.astype(BF)
        for tap in range(4):
            g_taps_ref[tap : tap + 1, :] += jnp.sum(
                here * window[pl.ds(start + 5 + tap, CH), :], axis=0, keepdims=True
            )


def params(*semantics):
    return pltpu.CompilerParams(dimension_semantics=semantics, vmem_limit_bytes=VMEM_BYTES)


def cost(chunks, dots, size):
    return pl.CostEstimate(
        flops=chunks * dots * 2 * 128**3, transcendentals=chunks * 128 * 1024, bytes_accessed=size
    )


def whole(shape):
    return pl.BlockSpec(shape, lambda *_: (0,) * len(shape))


def prepare(projected, router, taps, par, width, count=8):
    n_micro, length, full = projected.shape
    steps = length // (count * CH)
    chunks = length // CH
    size = count * CH
    per = lambda *tail: pl.BlockSpec((1, count) + tail, lambda m, i: (m, i, 0, 0))
    made = lambda kind, *tail: jax.ShapeDtypeStruct((n_micro, chunks) + tail, kind)
    return pl.pallas_call(
        partial(prep_kernel, count),
        grid=(n_micro, steps),
        in_specs=[
            pl.BlockSpec((1, size, full), lambda m, i: (m, i, 0)),
            pl.BlockSpec((1, HALO, full), lambda m, i: (m, jnp.maximum(i * (size // HALO) - 1, 0), 0)),
            pl.BlockSpec((1, size, LANES), lambda m, i: (m, i, 0)),
            whole(taps.shape),
            whole(par.shape),
        ],
        out_specs=[per(ST, ST), per(ST, 128), per(ST, 128), per(CH, ST), per(CH, 128), per(ST, 128)],
        out_shape=[
            made(F32, ST, ST), made(F32, ST, 128), made(F32, ST, 128), made(F32, CH, ST),
            made(BF, CH, 128), made(BF, ST, 128),
        ],
        scratch_shapes=[pltpu.VMEM((size + 8, width), F32)],
        compiler_params=params("arbitrary", "arbitrary"),
        cost_estimate=cost(n_micro * chunks, 44, n_micro * chunks * 400 * 1024),
        name="mixer_prepare",
    )(projected, projected, router, taps, par)


def scan_states(prep, router, projected, par, gate_at, count=4):
    _, wmat, umat, seen, q, k = prep
    n_micro, chunks = wmat.shape[:2]
    length = chunks * CH
    size = count * CH
    per = lambda *tail: pl.BlockSpec((n_micro, count) + tail, lambda i: (0, i, 0, 0))
    made = lambda kind, *tail: jax.ShapeDtypeStruct((n_micro, chunks) + tail, kind)
    return pl.pallas_call(
        partial(scan_kernel, n_micro, count),
        grid=(chunks // count,),
        in_specs=[
            per(ST, 128), per(ST, 128), per(CH, ST), per(CH, 128), per(ST, 128),
            pl.BlockSpec((n_micro, size, LANES), lambda i: (0, i, 0)),
            pl.BlockSpec((n_micro, size, 128), lambda i: (0, i, gate_at)),
            whole(par.shape),
        ],
        out_specs=[
            pl.BlockSpec((n_micro, size, 128), lambda i: (0, i, 0)),
            per(CH, 128), per(ST, 128), per(128, 128),
        ],
        out_shape=[
            jax.ShapeDtypeStruct((n_micro, length, 128), BF),
            made(F32, CH, 128), made(F32, ST, 128), made(F32, 128, 128),
        ],
        scratch_shapes=[pltpu.VMEM((n_micro, 128, 128), F32)],
        compiler_params=params("arbitrary"),
        cost_estimate=cost(n_micro * chunks, 12, n_micro * chunks * 420 * 1024),
        name="mixer_scan",
    )(wmat, umat, seen, q, k, router, projected, par)


def scan_back(prep, router, projected, par, gate_at, mixed, d_out, count=4):
    _, wmat, _, seen, q, k = prep
    n_micro, chunks = wmat.shape[:2]
    length = chunks * CH
    size = count * CH
    blocks = chunks // count
    per = lambda *tail: pl.BlockSpec((n_micro, count) + tail, lambda i: (0, blocks - 1 - i, 0, 0))
    made = lambda kind, *tail: jax.ShapeDtypeStruct((n_micro, chunks) + tail, kind)
    return pl.pallas_call(
        partial(scan_back_kernel, n_micro, count),
        grid=(blocks,),
        in_specs=[
            per(ST, 128), per(CH, ST), per(CH, 128), per(ST, 128),
            pl.BlockSpec((n_micro, size, LANES), lambda i: (0, blocks - 1 - i, 0)),
            pl.BlockSpec((n_micro, size, 128), lambda i: (0, blocks - 1 - i, gate_at)),
            whole(par.shape),
            per(CH, 128),
            pl.BlockSpec((n_micro, size, 128), lambda i: (0, blocks - 1 - i, 0)),
        ],
        out_specs=[
            per(CH, 128), per(ST, 128), per(128, 128),
            pl.BlockSpec((n_micro, size, 128), lambda i: (0, blocks - 1 - i, 0)),
            whole((8, LANES)),
        ],
        out_shape=[
            made(F32, CH, 128), made(F32, ST, 128), made(F32, 128, 128),
            jax.ShapeDtypeStruct((n_micro, length, 128), BF),
            jax.ShapeDtypeStruct((8, LANES), F32),
        ],
        scratch_shapes=[pltpu.VMEM((n_micro, 128, 128), F32)],
        compiler_params=params("arbitrary"),
        cost_estimate=cost(n_micro * chunks, 12, n_micro * chunks * 420 * 1024),
        name="mixer_scan_back",
    )(wmat, seen, q, k, router, projected, par, mixed, d_out)


def mixer_grads(prep, router, projected, taps, par, width, news, state, d_mixed, d_news, d_state, d_gate, count=4):
    solve, _, _, seen, _, _ = prep
    n_micro, chunks = solve.shape[:2]
    length = chunks * CH
    size = count * CH
    blocks = chunks // count
    full = projected.shape[2]
    per = lambda *tail: pl.BlockSpec((1, count) + tail, lambda m, i: (m, blocks - 1 - i, 0, 0))
    rows = lambda n: pl.BlockSpec((1, size, n), lambda m, i: (m, blocks - 1 - i, 0))
    before = lambda m, i: (m, jnp.maximum((blocks - 1 - i) * (size // HALO) - 1, 0), 0)
    return pl.pallas_call(
        partial(grads_kernel, count),
        grid=(n_micro, blocks),
        in_specs=[
            rows(full), pl.BlockSpec((1, HALO, full), before), rows(LANES),
            whole(taps.shape), whole(par.shape),
            per(ST, ST), per(CH, ST), per(ST, 128), per(128, 128),
            per(CH, 128), per(ST, 128), per(128, 128), rows(LANES),
        ],
        out_specs=[rows(width + 2 * LANES), whole((8, width)), whole((8, LANES))],
        out_shape=[
            jax.ShapeDtypeStruct((n_micro, length, width + 2 * LANES), BF),
            jax.ShapeDtypeStruct((8, width), F32),
            jax.ShapeDtypeStruct((8, LANES), F32),
        ],
        scratch_shapes=[pltpu.VMEM((size + 8, width), F32), pltpu.VMEM((size + 8, width), F32)],
        compiler_params=params("arbitrary", "arbitrary"),
        cost_estimate=cost(n_micro * chunks, 32, n_micro * chunks * 600 * 1024),
        name="mixer_grads",
    )(projected, projected, router, taps, par, solve, seen, news, state, d_mixed, d_news, d_state, d_gate)


def exchange(value, bit):
    count = lax.axis_size("row")
    return lax.ppermute(value, "row", [(i, i ^ bit) for i in range(count)])


def row_bits():
    count = lax.axis_size("row")
    return [1 << b for b in range(count.bit_length() - 1)]


def row_gather(value):
    parts = {0: value}
    for bit in reversed(row_bits()):
        places = sorted(parts)
        got = exchange(jnp.stack([parts[j] for j in places]), bit)
        parts.update({j ^ bit: got[n] for n, j in enumerate(places)})
    return [parts[j] for j in range(len(parts))]


def row_scatter(parts):
    parts = dict(enumerate(parts))
    for bit in row_bits():
        away = [j for j in sorted(parts) if j & bit]
        got = exchange(jnp.stack([parts[j].astype(BF) for j in away]), bit).astype(F32)
        parts = {
            j ^ bit: parts[j ^ bit].astype(F32) + got[n] for n, j in enumerate(away)
        }
    return parts[0]


def row_sum(value):
    for bit in row_bits():
        value = value + exchange(value, bit)
    return value


def rms_scale(values):
    return lax.rsqrt(jnp.mean(values * values, axis=-1, keepdims=True) + EPS_NORM)


def rms_back(grad_norm, values, inv_scale):
    return inv_scale * grad_norm - values * inv_scale**3 * jnp.mean(
        grad_norm * values, axis=-1, keepdims=True
    )


def matmul(spec, left, right, kind=F32):
    return jnp.einsum(spec, left, right, preferred_element_type=F32).astype(kind)


def local(
    tokens,
    cotangent,
    row_lengths,
    norm1_gain,
    w_in,
    w_router,
    conv_weight,
    a_log,
    dt_bias,
    head_gain,
    w_out,
    norm2_gain,
    w_gu,
    w_down,
):
    n_seq, n_row = lax.axis_size("seq"), lax.axis_size("row")
    seq, row = lax.axis_index("seq"), lax.axis_index("row")
    n_micro, _, n_tok, model = tokens.shape
    n_heads = a_log.shape[0]
    head_dim = head_gain.shape[0]
    n_taps, conv_width = conv_weight.shape
    slots = w_in.shape[1] // (n_heads * head_dim)
    width = conv_width // n_heads
    length = n_tok * n_seq
    copies = n_seq // n_heads
    head = seq // copies
    gate_at = slots - 1

    def to_heads(value):
        return lax.all_to_all(jnp.repeat(value, copies, axis=0), "seq", 0, 0, tiled=True)

    def from_heads(value):
        got = lax.all_to_all(value, "seq", 0, 0, tiled=True)
        return got if copies == 1 else got[::copies]

    tokens_all = lax.all_gather(tokens[:, 0], "seq", axis=0)
    cut = w_in.shape[0] // n_row
    w_piece = lax.dynamic_index_in_dim(
        w_in.reshape(n_row, cut, slots, n_heads, head_dim), row, 0, False
    )
    w_piece = w_piece.transpose(2, 0, 1, 3).reshape(n_heads, cut, slots * head_dim)
    w_pieces = jnp.stack(row_gather(to_heads(w_piece)))
    w_head = jnp.stack(
        [lax.dynamic_index_in_dim(w_pieces, row ^ j, 0, False) for j in range(n_row)], axis=1
    ).reshape(model, slots * head_dim)
    w_rt = lax.dynamic_index_in_dim(w_router.reshape(model, -1, n_heads), head, 2, False)
    n_rt = w_rt.shape[1]
    w_rt = jnp.pad(w_rt, ((0, 0), (0, LANES - n_rt)))
    taps = lax.dynamic_index_in_dim(
        conv_weight.reshape(n_taps, gate_at, n_heads, head_dim), head, 2, False
    ).reshape(n_taps, width)
    taps = jnp.pad(taps, ((0, 8 - n_taps), (0, 0)))
    par = jnp.concatenate(
        [
            head_gain[None],
            jnp.broadcast_to(lax.dynamic_index_in_dim(a_log, head, 0), (1, LANES)),
            jnp.broadcast_to(lax.dynamic_index_in_dim(dt_bias, head, 0), (1, LANES)),
            jnp.zeros((5, LANES), F32),
        ]
    )
    hidden = w_gu.shape[1] // 2
    unit_cut = hidden // n_seq // n_row
    n_units = unit_cut * n_seq
    gu_piece = lax.dynamic_index_in_dim(
        w_gu.reshape(-1, 2, n_seq, n_row, unit_cut), row, 3, False
    ).reshape(-1, 2 * n_units)
    down_piece = lax.dynamic_slice_in_dim(w_down, row * unit_cut, unit_cut, 0)
    full_out = lax.all_gather(w_out, "seq", axis=0, tiled=True)
    gu = lax.all_gather(gu_piece, "seq", axis=0, tiled=True)
    down = lax.all_gather(down_piece, "seq", axis=0, tiled=True)

    position = seq * n_tok + jnp.arange(n_tok, dtype=jnp.int32)
    live = (position[None, :] < row_lengths[:, :1]).astype(F32)[:, :, None]
    d_top = cotangent[:, 0].astype(F32) * live
    d_top_low = d_top.astype(BF)
    d_top_rows = jnp.concatenate(
        [part.reshape(-1, model) for part in row_gather(d_top_low)], axis=0
    )
    d_act = matmul("td,fd->tf", d_top_rows, down)

    x_all = tokens_all.transpose(1, 0, 2, 3).reshape(n_micro, length, model).astype(F32)
    scale_all = rms_scale(x_all)
    normed_in = (x_all * scale_all * norm1_gain).astype(BF)
    projected = matmul("mtd,dc->mtc", normed_in, w_head, BF)
    router = matmul("mtd,dc->mtc", normed_in, w_rt)
    prep = prepare(projected, router, taps, par, width)
    gated, mixed, news, state = scan_states(prep, router, projected, par, gate_at)

    gated_out = from_heads(
        gated.reshape(n_micro, n_seq, n_tok, head_dim).transpose(1, 0, 2, 3)
    )
    gated_out = gated_out.transpose(1, 2, 0, 3).reshape(n_micro * n_tok, model)
    x_vals = tokens[:, 0].reshape(-1, model).astype(F32)
    residual = x_vals + matmul("tc,cd->td", gated_out, full_out)
    scale_mid = rms_scale(residual)
    normed_mid = (residual * scale_mid * norm2_gain).astype(BF)
    mid_rows = jnp.concatenate(row_gather(normed_mid), axis=0)
    gate_up = matmul("td,dc->tc", mid_rows, gu)
    gate_part = gate_up[:, :n_units]
    up_part = gate_up[:, n_units:]
    gate_sig = jax.nn.sigmoid(gate_part)
    act_low = (gate_part * gate_sig * up_part).astype(BF)
    d_gate = d_act * up_part * gate_sig * (1.0 + gate_part * (1.0 - gate_sig))
    d_up = d_act * gate_part * gate_sig
    d_gu_low = jnp.concatenate([d_gate, d_up], axis=1).astype(BF)
    d_mid = row_scatter(list(matmul("tc,dc->td", d_gu_low, gu).reshape(n_row, -1, model)))
    d_residual = d_top.reshape(-1, model) + rms_back(d_mid * norm2_gain, residual, scale_mid)
    d_res_low = d_residual.astype(BF)
    d_gated = matmul("td,cd->tc", d_res_low, full_out, BF)
    d_gated = d_gated.reshape(n_micro, n_tok, n_heads, head_dim).transpose(2, 0, 1, 3)
    d_gated = to_heads(d_gated).transpose(1, 0, 2, 3).reshape(n_micro, length, head_dim)

    mlp_out = row_scatter(list(matmul("tf,fd->td", act_low, down).reshape(n_row, -1, model)))
    out = (residual + mlp_out).astype(BF).reshape(n_micro, 1, n_tok, model)

    d_mixed, d_news, d_state, d_gate_pre, g_head = scan_back(
        prep, router, projected, par, gate_at, mixed, d_gated
    )
    d_ext, g_taps, g_par = mixer_grads(
        prep, router, projected, taps, par, width, news, state, d_mixed, d_news, d_state, d_gate_pre
    )
    if copies > 1:
        mine = (seq % copies == 0).astype(F32)
        d_ext = d_ext * mine.astype(BF)
        g_taps, g_par, g_head = g_taps * mine, g_par * mine, g_head * mine
    w_ext = jnp.concatenate([w_head, w_rt], axis=1)
    d_in_part = matmul("mtc,dc->mtd", d_ext, w_ext)
    g_norm1 = jnp.sum(d_in_part * x_all * scale_all, axis=(0, 1))
    d_in_part = d_in_part.astype(BF).reshape(n_micro, n_seq, n_tok, model).transpose(1, 0, 2, 3)
    d_in = lax.psum_scatter(d_in_part, "seq", scatter_dimension=0).astype(F32)
    x_own = tokens[:, 0].astype(F32)
    grad_tokens = d_residual.reshape(n_micro, n_tok, model) + rms_back(
        d_in * norm1_gain, x_own, rms_scale(x_own)
    )

    g_ext = matmul("mtd,mtc->dc", normed_in, d_ext)
    g_in = g_ext[:, : slots * head_dim].reshape(n_seq, n_row, cut, slots * head_dim)
    g_in = row_scatter([lax.dynamic_index_in_dim(g_in, row ^ j, 1, False) for j in range(n_row)])
    g_in = from_heads(g_in.astype(BF)).reshape(n_heads, cut, slots, head_dim)
    g_in = g_in.transpose(1, 2, 0, 3).reshape(cut, -1)
    grad_in = lax.all_gather(g_in, "row", axis=0, tiled=True).astype(F32)

    g_out = matmul("tc,td->cd", gated_out, d_res_low).reshape(model, n_row, -1)
    g_out = row_scatter([lax.dynamic_index_in_dim(g_out, row ^ j, 1, False) for j in range(n_row)])
    g_gu = matmul("td,tc->dc", mid_rows, d_gu_low, BF)
    g_down = matmul("tf,td->fd", act_low, d_top_rows, BF)
    g_wide = jnp.concatenate([g_gu, g_out.astype(BF)], axis=1)
    g_wide = lax.psum_scatter(g_wide, "seq", scatter_dimension=0, tiled=True)
    g_down = lax.psum_scatter(g_down, "seq", scatter_dimension=0, tiled=True)
    g_wide = lax.all_gather(g_wide, "row", axis=0)
    grad_down = lax.all_gather(g_down, "row", axis=0, tiled=True).astype(F32)
    grad_gu = g_wide[:, :, : 2 * n_units].reshape(n_row, -1, 2, n_seq, unit_cut)
    grad_gu = grad_gu.transpose(1, 2, 3, 0, 4).reshape(-1, 2 * hidden).astype(F32)
    grad_out = g_wide[:, :, 2 * n_units :].transpose(1, 0, 2).reshape(-1, model).astype(F32)

    g_norm2 = jnp.sum(d_mid * residual * scale_mid, axis=0)
    shared = jnp.concatenate([g_norm1, g_norm2, g_head[0]])
    by_head = jnp.concatenate(
        [
            g_taps[:n_taps].reshape(-1),
            g_ext[:, slots * head_dim : slots * head_dim + n_rt].T.reshape(-1),
            g_par[1, 2:3],
            g_par[2, 2:3],
        ]
    )
    size = shared.shape[0] + by_head.shape[0]
    packed = jnp.pad(jnp.concatenate([shared, by_head]), (0, -size % 1024)).reshape(-1, 1024)
    packed = lax.all_gather(row_sum(packed), "seq", axis=0).reshape(n_seq, -1)
    total = jnp.sum(packed[:, : shared.shape[0]], axis=0)
    heads = packed[::copies, shared.shape[0] : size]
    n_conv = n_taps * width
    conv_sum = heads[:, :n_conv].reshape(n_heads, n_taps, gate_at, head_dim)
    conv_sum = conv_sum.transpose(1, 2, 0, 3).reshape(n_taps, conv_width)
    router_sum = heads[:, n_conv : n_conv + n_rt * model].reshape(n_heads, n_rt, model)
    router_sum = router_sum.transpose(2, 1, 0).reshape(model, n_rt * n_heads)
    return (
        out,
        grad_tokens[:, None],
        total[:model],
        grad_in,
        router_sum,
        conv_sum,
        heads[:, -2],
        heads[:, -1],
        total[2 * model :],
        grad_out,
        total[model : 2 * model],
        grad_gu,
        grad_down,
    )


def solution(mesh):
    by_rows = P("seq", None)
    by_tokens = P(None, "row", "seq", None)
    return jax.shard_map(
        local,
        mesh=mesh,
        in_specs=(
            by_tokens, by_tokens, P(None, "row"), P(), by_rows, P(), P(), P(), P(), P(),
            by_rows, P(), by_rows, by_rows,
        ),
        out_specs=(
            by_tokens, by_tokens, P(), by_rows, P(), P(), P(), P(), P(),
            by_rows, P(), by_rows, by_rows,
        ),
        check_vma=False,
    )
```

```python
from functools import partial

import jax
import jax.numpy as jnp
from jax import lax
from jax.experimental import pallas as pl
from jax.experimental.pallas import tpu as pltpu
from jax.sharding import PartitionSpec as P

BF = jnp.bfloat16
F32 = jnp.float32
EPS_NORM = 1e-05
EPS_UNIT = 1e-06
CH = 64
ST = 128
HALO = 16
LANES = 128
VMEM_BYTES = 50 * 1024 * 1024


def halves(value):
    high = value.astype(BF)
    return (high, (value - high.astype(F32)).astype(BF))


def dot(left, right, over_left=1, over_right=0):
    return lax.dot_general(
        left, right, (((over_left,), (over_right,)), ((), ())), preferred_element_type=F32
    )


def mm(left, right, over_left=1, over_right=0):
    left = left if isinstance(left, tuple) else (left,)
    right = right if isinstance(right, tuple) else (right,)
    total = dot(left[0], right[0], over_left, over_right)
    if len(right) > 1:
        total = total + dot(left[0], right[1], over_left, over_right)
    if len(left) > 1:
        total = total + dot(left[1], right[0], over_left, over_right)
    return total


def exact_sum(ones, value):
    high = value.astype(BF)
    rest = value - high.astype(F32)
    mid = rest.astype(BF)
    low = (rest - mid.astype(F32)).astype(BF)
    return dot(ones, high) + dot(ones, mid) + dot(ones, low)


def step_orders():
    row = lax.broadcasted_iota(jnp.int32, (ST, ST), 0)
    col = lax.broadcasted_iota(jnp.int32, (ST, ST), 1)
    order = lambda i: 2 * (i & (CH - 1)) + (i >> 6)
    return order(row), order(col)


def sees():
    row = lax.broadcasted_iota(jnp.int32, (CH, ST), 0)
    col = lax.broadcasted_iota(jnp.int32, (CH, ST), 1)
    return (col & (CH - 1)) <= row


def twice(value):
    return jnp.concatenate([value, value], axis=0)


def log_decays(router, par):
    lane = lax.broadcasted_iota(jnp.int32, (CH, LANES), 1)
    pre = router + par[2:3]
    soft = jnp.maximum(pre, 0.0) + jnp.log1p(jnp.exp(-jnp.abs(pre)))
    decay = -jnp.exp(par[1:2]) * soft
    row = lax.broadcasted_iota(jnp.int32, (CH, CH), 0)
    col = lax.broadcasted_iota(jnp.int32, (CH, CH), 1)
    below = jnp.where(col <= row, 1.0, 0.0).astype(BF)
    total = exact_sum(below, jnp.where(lane == 2, decay, 0.0))
    return decay, total


def gate_columns(router, par):
    strength = jax.nn.sigmoid(router)
    decay, total = log_decays(router, par)
    beta = jnp.concatenate([strength[:, 0:1], strength[:, 1:2]], axis=0)
    doubled = twice(total)
    g_col = doubled[:, 2:3]
    g_row = doubled.T[2:3, :]
    g_last = total[CH - 1 : CH, 2:3]
    return beta, g_col, g_row, g_last, decay


def seen_decay(g_col, g_row, visible):
    return jnp.where(visible, jnp.exp(jnp.where(visible, g_col[:CH] - g_row, 0.0)), 0.0)


def unit(value):
    scale = lax.rsqrt(jnp.sum(value * value, axis=-1, keepdims=True) + EPS_UNIT)
    return value * scale, scale


def taps_sum(window, weight, start):
    total = weight[0:1] * window[pl.ds(start + 5, CH), :]
    for tap in range(1, 4):
        total = total + weight[tap : tap + 1] * window[pl.ds(start + 5 + tap, CH), :]
    return total


def fill_window(window, proj_ref, halo_ref, is_first):
    width = window.shape[1]
    edge = halo_ref[0, :, :width].astype(F32)[HALO - 8 :]
    window[0:8, :] = jnp.where(is_first, 0.0, edge)
    window[8:, :] = proj_ref[0, :, :width].astype(F32)


def prep_kernel(
    count, proj_ref, halo_ref, router_ref, taps_ref, par_ref,
    solve_ref, wmat_ref, umat_ref, seen_ref, q_ref, k_ref, window,
):
    fill_window(window, proj_ref, halo_ref, pl.program_id(1) == 0)
    weight = taps_ref[...]
    par = par_ref[...]
    o_row, o_col = step_orders()
    strict = o_row > o_col
    eye = jnp.where(o_row == o_col, 1.0, 0.0)
    visible = sees()
    many = range(count)
    lower, rights = [], []
    for n in many:
        conv = taps_sum(window, weight, n * CH)
        act = conv * jax.nn.sigmoid(conv)
        q = unit(act[:, 0:128])[0].astype(BF)
        k = jnp.concatenate(
            [unit(act[:, 128:256])[0], unit(act[:, 256:384])[0]], axis=0
        ).astype(BF)
        v = jnp.concatenate([act[:, 384:512], act[:, 512:640]], axis=0).astype(BF)
        beta, g_col, g_row, _, _ = gate_columns(
            router_ref[0, n * CH : (n + 1) * CH, :], par
        )
        gaps = seen_decay(g_col, g_row, visible)
        lower.append(jnp.where(strict, beta * twice(gaps) * dot(k, k, 1, 1), 0.0))
        kf = k.astype(F32)
        rights.append(
            jnp.concatenate([beta * jnp.exp(g_col) * kf, beta * v.astype(F32)], axis=1)
        )
        seen_ref[0, n] = gaps * dot(q, k, 1, 1)
        q_ref[0, n] = q
        k_ref[0, n] = k
    inverse = [eye - jnp.where((o_row >> 1) == (o_col >> 1), part, 0.0) for part in lower]
    for level in range(1, 7):
        at = ((o_row >> level) ^ (o_col >> level)) == 1
        parts = [halves(jnp.where(at, part, 0.0)) for part in lower]
        known = [halves(value) for value in inverse]
        inner = [halves(mm(parts[n], known[n])) for n in many]
        inverse = [inverse[n] - mm(known[n], inner[n]) for n in many]
    for n in many:
        solve_ref[0, n] = inverse[n]
        both = mm(halves(inverse[n]), halves(rights[n]))
        wmat_ref[0, n] = both[:, :128]
        umat_ref[0, n] = both[:, 128:]


def head_norm(mixed):
    return lax.rsqrt(jnp.mean(mixed * mixed, axis=-1, keepdims=True) + EPS_NORM)


def scan_kernel(
    n_micro, count, wmat_ref, umat_ref, seen_ref, q_ref, k_ref, router_ref, gate_ref, par_ref,
    out_ref, mixed_ref, news_ref, state_ref, state,
):
    @pl.when(pl.program_id(0) == 0)
    def _():
        state[...] = jnp.zeros_like(state)

    par = par_ref[...]
    now = [state[m] for m in range(n_micro)]
    for n in range(count):
        rows = slice(n * CH, (n + 1) * CH)
        for m in range(n_micro):
            _, g_col, _, g_last, _ = gate_columns(router_ref[m, rows, :], par)
            held = halves(now[m])
            state_ref[m, n] = now[m]
            news = umat_ref[m, n] - mm(halves(wmat_ref[m, n]), held)
            news_ref[m, n] = news
            news_h = halves(news)
            ends = halves(jnp.exp(g_last - g_col) * k_ref[m, n].astype(F32))
            now[m] = jnp.exp(g_last) * now[m] + mm(ends, news_h, 0, 0)
            mixed = jnp.exp(g_col[:CH]) * mm(q_ref[m, n], held) + mm(halves(seen_ref[m, n]), news_h)
            mixed_ref[m, n] = mixed
            gate = gate_ref[m, rows, :].astype(F32)
            out_ref[m, rows, :] = (
                mixed * head_norm(mixed) * par[0:1] * (gate * jax.nn.sigmoid(gate))
            ).astype(BF)
    for m in range(n_micro):
        state[m] = now[m]


def scan_back_kernel(
    n_micro, count, wmat_ref, seen_ref, q_ref, k_ref, router_ref, gate_ref, par_ref, mixed_ref, d_out_ref,
    d_mixed_ref, d_news_ref, d_state_ref, d_gate_ref, gain_ref, state,
):
    @pl.when(pl.program_id(0) == 0)
    def _():
        state[...] = jnp.zeros_like(state)
        gain_ref[...] = jnp.zeros_like(gain_ref)

    par = par_ref[...]
    now = [state[m] for m in range(n_micro)]
    gain = jnp.zeros((1, LANES), F32)
    for n in reversed(range(count)):
        rows = slice(n * CH, (n + 1) * CH)
        for m in range(n_micro):
            _, g_col, _, g_last, _ = gate_columns(router_ref[m, rows, :], par)
            mixed = mixed_ref[m, n]
            gate = gate_ref[m, rows, :].astype(F32)
            d_out = d_out_ref[m, rows, :].astype(F32)
            scale = head_norm(mixed)
            normed = mixed * scale
            sig = jax.nn.sigmoid(gate)
            silu = gate * sig
            gain = gain + jnp.sum(d_out * normed * silu, axis=0, keepdims=True)
            d_gate = d_out * normed * par[0:1] * (sig * (1.0 + gate * (1.0 - sig)))
            d_gate_ref[m, rows, :] = d_gate.astype(BF)
            d_normed = d_out * par[0:1] * silu
            d_mixed = scale * d_normed - mixed * scale**3 * jnp.mean(
                d_normed * mixed, axis=-1, keepdims=True
            )
            d_mixed_ref[m, n] = d_mixed
            d_mixed_h = halves(d_mixed)
            d_state_ref[m, n] = now[m]
            ends = halves(jnp.exp(g_last - g_col) * k_ref[m, n].astype(F32))
            d_news = mm(halves(seen_ref[m, n]), d_mixed_h, 0, 0) + mm(ends, halves(now[m]))
            d_news_ref[m, n] = d_news
            q_eff = halves(jnp.exp(g_col[:CH]) * q_ref[m, n].astype(F32))
            now[m] = (
                jnp.exp(g_last) * now[m]
                + mm(q_eff, d_mixed_h, 0, 0)
                - mm(halves(wmat_ref[m, n]), halves(d_news), 0, 0)
            )
    gain_ref[0:1, :] += gain
    for m in range(n_micro):
        state[m] = now[m]


def unit_back(grad, value, scale):
    return scale * grad - value * scale**3 * jnp.sum(grad * value, axis=-1, keepdims=True)


def grads_kernel(
    count, proj_ref, halo_ref, router_ref, taps_ref, par_ref, solve_ref, seen_ref, news_ref, state_ref,
    d_mixed_ref, d_news_ref, d_state_ref, d_gate_ref,
    d_ext_ref, g_taps_ref, g_par_ref, window, d_window,
):
    step = pl.program_id(1)
    size = count * CH
    fill_window(window, proj_ref, halo_ref, step == pl.num_programs(1) - 1)

    @pl.when((step == 0) & (pl.program_id(0) == 0))
    def _():
        g_taps_ref[...] = jnp.zeros_like(g_taps_ref)
        g_par_ref[...] = jnp.zeros_like(g_par_ref)

    @pl.when(step == 0)
    def _():
        d_window[size:, :] = jnp.zeros((8, d_window.shape[1]), F32)

    @pl.when(step > 0)
    def _():
        d_window[size:, :] = d_window[0:8, :]

    weight = taps_ref[...]
    par = par_ref[...]
    o_row, o_col = step_orders()
    strict = o_row > o_col
    visible = sees()
    row = lax.broadcasted_iota(jnp.int32, (CH, CH), 0)
    col = lax.broadcasted_iota(jnp.int32, (CH, CH), 1)
    above = jnp.where(col >= row, 1.0, 0.0).astype(BF)
    lane = lax.broadcasted_iota(jnp.int32, (CH, LANES), 1)
    last = lax.broadcasted_iota(jnp.int32, (CH, LANES), 0) == CH - 1
    g_alog = jnp.zeros((1, LANES), F32)
    g_dt = jnp.zeros((1, LANES), F32)
    for n in range(count):
        rows = slice(n * CH, (n + 1) * CH)
        conv = taps_sum(window, weight, n * CH)
        sig = jax.nn.sigmoid(conv)
        act = conv * sig
        qn, q_scale = unit(act[:, 0:128])
        k0n, k0_scale = unit(act[:, 128:256])
        k1n, k1_scale = unit(act[:, 256:384])
        q = qn.astype(BF)
        k = jnp.concatenate([k0n, k1n], axis=0).astype(BF)
        kf, qf = k.astype(F32), q.astype(F32)
        router = router_ref[0, rows, :]
        beta, g_col, g_row, g_last, decay = gate_columns(router, par)
        gaps = seen_decay(g_col, g_row, visible)
        ratio = jnp.where(strict, twice(gaps), 0.0)
        grown = jnp.exp(g_col)
        left = jnp.exp(g_last - g_col)
        gram = dot(k, k, 1, 1)
        state = state_ref[0, n]
        state_h = halves(state)
        news = news_ref[0, n]
        news_h = halves(news)
        d_mixed_h = halves(d_mixed_ref[0, n])
        d_state = d_state_ref[0, n]
        d_right = mm(halves(solve_ref[0, n]), halves(d_news_ref[0, n]), 0, 0)
        d_right_h = halves(d_right)
        d_lower = jnp.where(strict, -mm(d_right_h, news_h, 1, 1), 0.0)
        d_pre = (1.0 - beta) * jnp.sum(d_right * news, axis=-1, keepdims=True)
        d_v = beta * d_right
        d_grown_k = -beta * mm(d_right_h, state_h, 1, 1)
        d_k = grown * d_grown_k
        d_gram = beta * ratio * d_lower
        both = d_gram * gram
        d_g = jnp.sum(both, axis=-1, keepdims=True) + jnp.sum(d_k * kf, axis=-1, keepdims=True)
        d_g_row = -jnp.sum(both, axis=0, keepdims=True)
        d_k = d_k + mm(halves(d_gram + d_gram.T), k)
        d_seen = mm(d_mixed_h, news_h, 1, 1)
        d_scores = halves(d_seen * gaps)
        seen_both = d_seen * seen_ref[0, n]
        d_q_grown = grown[:CH] * mm(d_mixed_h, state_h, 1, 1)
        d_q = d_q_grown + mm(d_scores, k)
        d_k = d_k + mm(d_scores, q, 0, 0)
        d_g_q = jnp.sum(seen_both + d_q_grown * qf, axis=-1, keepdims=True)
        d_g_row = d_g_row - jnp.sum(seen_both, axis=0, keepdims=True)
        d_ends = left * mm(news_h, halves(d_state), 1, 1)
        d_k = d_k + d_ends
        ends_sum = jnp.sum(d_ends * kf, axis=-1, keepdims=True)
        d_g = d_g - ends_sum
        d_last = jnp.sum(ends_sum, axis=0, keepdims=True) + jnp.exp(g_last) * jnp.sum(
            jnp.sum(d_state * state, axis=-1, keepdims=True), axis=0, keepdims=True
        )
        d_g_rows = jnp.broadcast_to(d_g_row, (LANES, ST)).T
        d_g_tok = d_g_q + d_g[:CH] + d_g[CH:] + d_g_rows[:CH] + d_g_rows[CH:]
        d_g_tok = d_g_tok + jnp.where(last, d_last, 0.0)
        d_decay = exact_sum(above, d_g_tok)
        d_soft = -jnp.exp(par[1:2]) * jax.nn.sigmoid(router + par[2:3]) * d_decay
        d_router = jnp.where(
            lane == 0,
            d_pre[:CH],
            jnp.where(lane == 1, d_pre[CH:], jnp.where(lane == 2, d_soft, 0.0)),
        )
        width = window.shape[1]
        d_ext_ref[0, rows, width : width + LANES] = d_gate_ref[0, rows, :]
        d_ext_ref[0, rows, width + LANES :] = d_router.astype(BF)
        g_alog = g_alog + jnp.sum(
            jnp.where(lane == 2, d_decay * decay, 0.0), axis=0, keepdims=True
        )
        g_dt = g_dt + jnp.sum(jnp.where(lane == 2, d_soft, 0.0), axis=0, keepdims=True)
        d_act = jnp.concatenate(
            [
                unit_back(d_q, act[:, 0:128], q_scale),
                unit_back(d_k[:CH], act[:, 128:256], k0_scale),
                unit_back(d_k[CH:], act[:, 256:384], k1_scale),
                d_v[:CH],
                d_v[CH:],
            ],
            axis=1,
        )
        d_window[rows, :] = d_act * (sig * (1.0 + conv * (1.0 - sig)))
    g_par_ref[1:2, :] += g_alog
    g_par_ref[2:3, :] += g_dt
    for n in range(count):
        start = n * CH
        here = d_window[pl.ds(start, CH), :]
        total = weight[3:4] * here
        for tap in range(3):
            total = total + weight[tap : tap + 1] * d_window[pl.ds(start + 3 - tap, CH), :]
        d_ext_ref[0, pl.ds(start, CH), : total.shape[1]] = total.astype(BF)
        for tap in range(4):
            g_taps_ref[tap : tap + 1, :] += jnp.sum(
                here * window[pl.ds(start + 5 + tap, CH), :], axis=0, keepdims=True
            )


def params(*semantics):
    return pltpu.CompilerParams(dimension_semantics=semantics, vmem_limit_bytes=VMEM_BYTES)


def cost(chunks, per_chunk):
    return pl.CostEstimate(
        flops=int(chunks * per_chunk * 1.1e9), transcendentals=0, bytes_accessed=1 << 20
    )


def launch(kernel, in_specs, earlier, **options):
    n_in = len(in_specs)

    def body(*refs):
        kernel(*refs[:n_in], *refs[n_in + len(earlier) :])

    specs = list(in_specs) + [pl.BlockSpec(memory_space=pl.ANY)] * len(earlier)
    called = pl.pallas_call(body, in_specs=specs, **options)
    return lambda *operands: called(*operands, *earlier)


def fence(value, *earlier):
    anywhere = pl.BlockSpec(memory_space=pl.ANY)
    return pl.pallas_call(
        lambda *refs: None,
        in_specs=[anywhere] * (1 + len(earlier)),
        out_specs=anywhere,
        out_shape=jax.ShapeDtypeStruct(value.shape, value.dtype),
        input_output_aliases={0: 0},
        name="fence",
    )(value, *earlier)


def whole(shape):
    return pl.BlockSpec(shape, lambda *_: (0,) * len(shape))


def prepare(projected, router, taps, par, width, earlier=(), count=8):
    n_micro, length, full = projected.shape
    steps = length // (count * CH)
    chunks = length // CH
    size = count * CH
    per = lambda *tail: pl.BlockSpec((1, count) + tail, lambda m, i: (m, i, 0, 0))
    made = lambda kind, *tail: jax.ShapeDtypeStruct((n_micro, chunks) + tail, kind)
    return launch(
        partial(prep_kernel, count),
        [
            pl.BlockSpec((1, size, full), lambda m, i: (m, i, 0)),
            pl.BlockSpec((1, HALO, full), lambda m, i: (m, jnp.maximum(i * (size // HALO) - 1, 0), 0)),
            pl.BlockSpec((1, size, LANES), lambda m, i: (m, i, 0)),
            whole(taps.shape),
            whole(par.shape),
        ],
        earlier,
        grid=(n_micro, steps),
        out_specs=[per(ST, ST), per(ST, 128), per(ST, 128), per(CH, ST), per(CH, 128), per(ST, 128)],
        out_shape=[
            made(F32, ST, ST), made(F32, ST, 128), made(F32, ST, 128), made(F32, CH, ST),
            made(BF, CH, 128), made(BF, ST, 128),
        ],
        scratch_shapes=[pltpu.VMEM((size + 8, width), F32)],
        compiler_params=params("arbitrary", "arbitrary"),
        cost_estimate=cost(n_micro * chunks, 0.75),
        name="mixer_prepare",
    )(projected, projected, router, taps, par)


def scan_states(prep, router, projected, par, gate_at, earlier=(), count=4):
    _, wmat, umat, seen, q, k = prep
    n_micro, chunks = wmat.shape[:2]
    length = chunks * CH
    size = count * CH
    per = lambda *tail: pl.BlockSpec((n_micro, count) + tail, lambda i: (0, i, 0, 0))
    made = lambda kind, *tail: jax.ShapeDtypeStruct((n_micro, chunks) + tail, kind)
    return launch(
        partial(scan_kernel, n_micro, count),
        [
            per(ST, 128), per(ST, 128), per(CH, ST), per(CH, 128), per(ST, 128),
            pl.BlockSpec((n_micro, size, LANES), lambda i: (0, i, 0)),
            pl.BlockSpec((n_micro, size, 128), lambda i: (0, i, gate_at)),
            whole(par.shape),
        ],
        earlier,
        grid=(chunks // count,),
        out_specs=[
            pl.BlockSpec((n_micro, size, 128), lambda i: (0, i, 0)),
            per(CH, 128), per(ST, 128), per(128, 128),
        ],
        out_shape=[
            jax.ShapeDtypeStruct((n_micro, length, 128), BF),
            made(F32, CH, 128), made(F32, ST, 128), made(F32, 128, 128),
        ],
        scratch_shapes=[pltpu.VMEM((n_micro, 128, 128), F32)],
        compiler_params=params("arbitrary"),
        cost_estimate=cost(n_micro * chunks, 0.5),
        name="mixer_scan",
    )(wmat, umat, seen, q, k, router, projected, par)


def scan_back(prep, router, projected, par, gate_at, mixed, d_out, earlier=(), count=4):
    _, wmat, _, seen, q, k = prep
    n_micro, chunks = wmat.shape[:2]
    length = chunks * CH
    size = count * CH
    blocks = chunks // count
    per = lambda *tail: pl.BlockSpec((n_micro, count) + tail, lambda i: (0, blocks - 1 - i, 0, 0))
    made = lambda kind, *tail: jax.ShapeDtypeStruct((n_micro, chunks) + tail, kind)
    return launch(
        partial(scan_back_kernel, n_micro, count),
        [
            per(ST, 128), per(CH, ST), per(CH, 128), per(ST, 128),
            pl.BlockSpec((n_micro, size, LANES), lambda i: (0, blocks - 1 - i, 0)),
            pl.BlockSpec((n_micro, size, 128), lambda i: (0, blocks - 1 - i, gate_at)),
            whole(par.shape),
            per(CH, 128),
            pl.BlockSpec((n_micro, size, 128), lambda i: (0, blocks - 1 - i, 0)),
        ],
        earlier,
        grid=(blocks,),
        out_specs=[
            per(CH, 128), per(ST, 128), per(128, 128),
            pl.BlockSpec((n_micro, size, 128), lambda i: (0, blocks - 1 - i, 0)),
            whole((8, LANES)),
        ],
        out_shape=[
            made(F32, CH, 128), made(F32, ST, 128), made(F32, 128, 128),
            jax.ShapeDtypeStruct((n_micro, length, 128), BF),
            jax.ShapeDtypeStruct((8, LANES), F32),
        ],
        scratch_shapes=[pltpu.VMEM((n_micro, 128, 128), F32)],
        compiler_params=params("arbitrary"),
        cost_estimate=cost(n_micro * chunks, 0.5),
        name="mixer_scan_back",
    )(wmat, seen, q, k, router, projected, par, mixed, d_out)


def mixer_grads(
    prep, router, projected, taps, par, width, news, state, d_mixed, d_news, d_state, d_gate,
    earlier=(), count=4,
):
    solve, _, _, seen, _, _ = prep
    n_micro, chunks = solve.shape[:2]
    length = chunks * CH
    size = count * CH
    blocks = chunks // count
    full = projected.shape[2]
    per = lambda *tail: pl.BlockSpec((1, count) + tail, lambda m, i: (m, blocks - 1 - i, 0, 0))
    rows = lambda n: pl.BlockSpec((1, size, n), lambda m, i: (m, blocks - 1 - i, 0))
    before = lambda m, i: (m, jnp.maximum((blocks - 1 - i) * (size // HALO) - 1, 0), 0)
    return launch(
        partial(grads_kernel, count),
        [
            rows(full), pl.BlockSpec((1, HALO, full), before), rows(LANES),
            whole(taps.shape), whole(par.shape),
            per(ST, ST), per(CH, ST), per(ST, 128), per(128, 128),
            per(CH, 128), per(ST, 128), per(128, 128), rows(LANES),
        ],
        earlier,
        grid=(n_micro, blocks),
        out_specs=[rows(width + 2 * LANES), whole((8, width)), whole((8, LANES))],
        out_shape=[
            jax.ShapeDtypeStruct((n_micro, length, width + 2 * LANES), BF),
            jax.ShapeDtypeStruct((8, width), F32),
            jax.ShapeDtypeStruct((8, LANES), F32),
        ],
        scratch_shapes=[pltpu.VMEM((size + 8, width), F32), pltpu.VMEM((size + 8, width), F32)],
        compiler_params=params("arbitrary", "arbitrary"),
        cost_estimate=cost(n_micro * chunks, 1.4),
        name="mixer_grads",
    )(projected, projected, router, taps, par, solve, seen, news, state, d_mixed, d_news, d_state, d_gate)


def project_kernel(x_ref, gain_ref, weight_ref, router_weight_ref, normed_ref, out_ref, router_ref):
    x = x_ref[0].astype(F32)
    scale = lax.rsqrt(jnp.mean(x * x, axis=-1, keepdims=True) + EPS_NORM)
    normed = (x * scale * gain_ref[...]).astype(BF)
    normed_ref[0] = normed
    out_ref[0] = dot(normed, weight_ref[...]).astype(BF)
    router_ref[0] = dot(normed, router_weight_ref[...])


def project(x, gain, weight, router_weight, earlier=(), size=256):
    n_micro, length, model = x.shape
    full = weight.shape[1]
    rows = lambda n: pl.BlockSpec((1, size, n), lambda m, i: (m, i, 0))
    return launch(
        project_kernel,
        [rows(model), whole((1, model)), whole(weight.shape), whole(router_weight.shape)],
        earlier,
        grid=(n_micro, length // size),
        out_specs=[rows(model), rows(full), rows(LANES)],
        out_shape=[
            jax.ShapeDtypeStruct((n_micro, length, model), BF),
            jax.ShapeDtypeStruct((n_micro, length, full), BF),
            jax.ShapeDtypeStruct((n_micro, length, LANES), F32),
        ],
        compiler_params=params("arbitrary", "arbitrary"),
        cost_estimate=cost(n_micro * length // CH, 0.35),
        name="project",
    )(x, gain[None], weight, router_weight)


def ring_add_kernel(table, ahead_ref, behind_ref, up_ref, low_ref, up_out, low_out):
    up_out[...] = (ahead_ref[...].astype(F32) + up_ref[0, 0].astype(F32)).astype(up_out.dtype)
    low_out[...] = (behind_ref[...].astype(F32) + low_ref[0, 0].astype(F32)).astype(low_out.dtype)


def ring_add(table, step, ahead, behind, parts, kind, earlier=()):
    rows, model = ahead.shape
    one = pl.BlockSpec((rows, model), lambda i, table: (0, 0))
    part = lambda m: pl.BlockSpec((1, 1, rows, model), lambda i, table: (m, table[2 * step + m], 0, 0))
    made = jax.ShapeDtypeStruct((rows, model), kind)
    n_in = 5

    def body(*refs):
        ring_add_kernel(*refs[:n_in], *refs[n_in + len(earlier) :])

    return pl.pallas_call(
        body,
        grid_spec=pltpu.PrefetchScalarGridSpec(
            num_scalar_prefetch=1,
            grid=(1,),
            in_specs=[one, one, part(0), part(1)] + [pl.BlockSpec(memory_space=pl.ANY)] * len(earlier),
            out_specs=[one, one],
        ),
        out_shape=[made, made],
        compiler_params=params("arbitrary"),
        cost_estimate=cost(1, 1.0),
        name="ring_add",
    )(table, ahead, behind, parts, parts, *earlier)


def input_grads_kernel(normed_ref, d_ext_ref, w_ext_ref, gain_ref, out_ref, lines_ref):
    total = dot(normed_ref[0], d_ext_ref[0], 0, 0)
    for m in range(1, normed_ref.shape[0]):
        total = total + dot(normed_ref[m], d_ext_ref[m], 0, 0)
    full = out_ref.shape[1]
    out_ref[...] = total[:, :full].astype(BF)
    norm = jnp.sum(total * w_ext_ref[...].astype(F32), axis=1, keepdims=True)
    lane = lax.broadcasted_iota(jnp.int32, (total.shape[0], LANES), 1)
    tail = jnp.where(lane == 3, norm, total[:, full:])
    lines = tail.T[:8]
    row = lax.broadcasted_iota(jnp.int32, lines.shape, 0)
    lines_ref[...] = jnp.where(row == 3, lines / gain_ref[...], lines)


def input_grads(normed, d_ext, w_ext, gain, full, earlier=(), size=128):
    n_micro, length, model = normed.shape
    wide = d_ext.shape[2]
    return launch(
        input_grads_kernel,
        [
            pl.BlockSpec((n_micro, length, size), lambda i: (0, 0, i)),
            whole(d_ext.shape),
            pl.BlockSpec((size, wide), lambda i: (i, 0)),
            pl.BlockSpec((1, size), lambda i: (0, i)),
        ],
        earlier,
        grid=(model // size,),
        out_specs=[
            pl.BlockSpec((size, full), lambda i: (i, 0)),
            pl.BlockSpec((8, size), lambda i: (0, i)),
        ],
        out_shape=[
            jax.ShapeDtypeStruct((model, full), BF),
            jax.ShapeDtypeStruct((8, model), F32),
        ],
        compiler_params=params("arbitrary"),
        cost_estimate=cost(1, 7.0),
        name="input_grads",
    )(normed, d_ext, w_ext, gain[None])


def place_heads_kernel(n_heads, slots, where, *refs):
    parts, out_ref = refs[:-1], refs[-1]
    for j, part in enumerate(parts):
        at = where[0] ^ j
        for slot in range(slots):
            for h in range(n_heads):
                to = (slot * n_heads + h) * LANES
                value = part[h, :, slot * LANES : (slot + 1) * LANES]
                out_ref[at, :, to : to + LANES] = value.astype(F32)


def place_heads(where, parts, slots):
    n_heads, cut, full = parts[0].shape
    shape = (len(parts), cut, full * n_heads)
    return pl.pallas_call(
        partial(place_heads_kernel, n_heads, slots),
        grid_spec=pltpu.PrefetchScalarGridSpec(
            num_scalar_prefetch=1,
            grid=(1,),
            in_specs=[pl.BlockSpec(part.shape, lambda i, where: (0, 0, 0)) for part in parts],
            out_specs=pl.BlockSpec(shape, lambda i, where: (0, 0, 0)),
        ),
        out_shape=jax.ShapeDtypeStruct(shape, F32),
        compiler_params=params("arbitrary"),
        cost_estimate=cost(1, 3.0),
        name="place_heads",
    )(where, *parts).reshape(-1, full * n_heads)


def place_units_kernel(unit_cut, unit_pad, n_seq, where, *refs):
    parts, out_ref = refs[:-1], refs[-1]
    n_row = len(parts)
    group = unit_cut * n_row
    hidden = group * n_seq
    for block in range(hidden // LANES):
        low = (block * LANES // group) * unit_pad // LANES * LANES
        high = ((block * LANES + LANES - 1) // group + 1) * unit_pad
        high = min(n_seq * unit_pad, -(-high // LANES) * LANES)
        col = lax.broadcasted_iota(jnp.int32, (high - low, LANES), 1) + block * LANES
        row = lax.broadcasted_iota(jnp.int32, (high - low, LANES), 0) + low
        inner = lax.rem(col, group)
        owner = lax.div(inner, unit_cut)
        unit = lax.div(col, group) * unit_pad + lax.rem(inner, unit_cut)
        total = [0.0, 0.0]
        for j, part in enumerate(parts):
            chosen = jnp.where((unit == row) & (owner == (where[0] ^ j)), 1.0, 0.0).astype(BF)
            for half in range(2):
                total[half] = total[half] + dot(part[half, :, low:high], chosen)
        for half in range(2):
            to = half * hidden + block * LANES
            out_ref[:, to : to + LANES] = total[half]


def place_units(where, parts, unit_cut, unit_pad, n_seq):
    rows = parts[0].shape[1]
    shape = (rows, 2 * unit_cut * n_seq * len(parts))
    return pl.pallas_call(
        partial(place_units_kernel, unit_cut, unit_pad, n_seq),
        grid_spec=pltpu.PrefetchScalarGridSpec(
            num_scalar_prefetch=1,
            grid=(1,),
            in_specs=[pl.BlockSpec(part.shape, lambda i, where: (0, 0, 0)) for part in parts],
            out_specs=pl.BlockSpec(shape, lambda i, where: (0, 0)),
        ),
        out_shape=jax.ShapeDtypeStruct(shape, F32),
        compiler_params=params("arbitrary"),
        cost_estimate=cost(1, 5.0),
        name="place_units",
    )(where, *parts)


def place_rows_kernel(where, *refs):
    parts, out_ref = refs[:-1], refs[-1]
    for j, part in enumerate(parts):
        out_ref[where[0] ^ j] = part[: out_ref.shape[1]].astype(F32)


def place_rows(where, parts, keep):
    width = parts[0].shape[1]
    shape = (len(parts), keep, width)
    return pl.pallas_call(
        place_rows_kernel,
        grid_spec=pltpu.PrefetchScalarGridSpec(
            num_scalar_prefetch=1,
            grid=(1,),
            in_specs=[pl.BlockSpec(part.shape, lambda i, where: (0, 0)) for part in parts],
            out_specs=pl.BlockSpec(shape, lambda i, where: (0, 0, 0)),
        ),
        out_shape=jax.ShapeDtypeStruct(shape, F32),
        compiler_params=params("arbitrary"),
        cost_estimate=cost(1, 2.0),
        name="place_rows",
    )(where, *parts).reshape(-1, width)


def feed_kernel(n_seq, first, mid_ref, d_top_ref, w_ref, act_ref, d_gu_ref, d_mid_ref, down_ref):
    n_units = act_ref.shape[1]
    model = mid_ref.shape[1]
    per = n_units // n_seq

    @pl.when(pl.program_id(0) == 0)
    def _():
        lines = w_ref[:, 2 * n_units :].reshape(n_seq, model // n_seq, model)
        down_ref[...] = lines[:, first : first + per].reshape(n_units, model)

    w_gate = w_ref[:, :n_units]
    w_up = w_ref[:, n_units : 2 * n_units]
    mid = mid_ref[...]
    gate = dot(mid, w_gate)
    up = dot(mid, w_up)
    d_act = dot(d_top_ref[...], down_ref[...], 1, 1)
    sig = jax.nn.sigmoid(gate)
    silu = gate * sig
    act_ref[...] = (silu * up).astype(BF)
    d_gate = (d_act * up * sig * (1.0 + gate * (1.0 - sig))).astype(BF)
    d_up = (d_act * silu).astype(BF)
    d_gu_ref[0] = d_gate
    d_gu_ref[1] = d_up
    d_mid_ref[...] = (dot(d_gate, w_gate, 1, 1) + dot(d_up, w_up, 1, 1)).astype(BF)


def feed(mid, d_top, weights, n_units, n_seq, first, size=256):
    tokens, model = mid.shape
    rows = lambda n: pl.BlockSpec((size, n), lambda i: (i, 0))
    return pl.pallas_call(
        partial(feed_kernel, n_seq, first),
        grid=(tokens // size,),
        in_specs=[rows(model), rows(model), whole(weights.shape)],
        out_specs=[
            rows(n_units), pl.BlockSpec((2, size, n_units), lambda i: (0, i, 0)),
            rows(model), whole((n_units, model)),
        ],
        out_shape=[
            jax.ShapeDtypeStruct((tokens, n_units), BF),
            jax.ShapeDtypeStruct((2, tokens, n_units), BF),
            jax.ShapeDtypeStruct((tokens, model), BF),
            jax.ShapeDtypeStruct((n_units, model), BF),
        ],
        compiler_params=params("arbitrary"),
        cost_estimate=cost(1, 14.0),
        name="feed",
    )(mid, d_top, weights)


def times_kernel(left_ref, right_ref, out_ref):
    out_ref[...] = dot(left_ref[...], right_ref[...]).astype(BF)


def times(left, right, earlier=(), size=256):
    tokens, inner = left.shape
    rows = lambda n: pl.BlockSpec((size, n), lambda i: (i, 0))
    return launch(
        times_kernel,
        [rows(inner), whole(right.shape)],
        earlier,
        grid=(tokens // size,),
        out_specs=rows(right.shape[1]),
        out_shape=jax.ShapeDtypeStruct((tokens, right.shape[1]), BF),
        compiler_params=params("arbitrary"),
        cost_estimate=cost(1, 3.0),
        name="times",
    )(left, right)


def feed_grads(mid, d_gu, rows, earlier=()):
    tokens, model = mid.shape
    n_units = d_gu.shape[2]
    size = max(rows, 128)
    per = size // rows

    def body(mid_ref, d_gu_ref, out_ref):
        mid = mid_ref[...]
        for half in range(2):
            value = dot(mid, d_gu_ref[half], 0, 0).astype(BF)
            for part in range(per):
                out_ref[part, half] = value[part * rows : (part + 1) * rows]

    return launch(
        body,
        [pl.BlockSpec((tokens, size), lambda i: (0, i)), whole(d_gu.shape)],
        earlier,
        grid=(model // size,),
        out_specs=pl.BlockSpec((per, 2, rows, n_units), lambda i: (i, 0, 0, 0)),
        out_shape=jax.ShapeDtypeStruct((model // rows, 2, rows, n_units), BF),
        compiler_params=params("arbitrary"),
        cost_estimate=cost(1, 6.0),
        name="feed_grads",
    )(mid, d_gu)


def pick(stacked, at, axis=0):
    return lax.dynamic_index_in_dim(stacked, at, axis, False, allow_negative_indices=False)


def tie(value, *earlier):
    for other in earlier:
        first = lax.slice(other, (0,) * other.ndim, (1,) * other.ndim).reshape(())
        value = value + (first * 0).astype(value.dtype)
    return value


def exchange(value, axis, bit):
    count = lax.axis_size(axis)
    return lax.ppermute(value, axis, [(i, i ^ bit) for i in range(count)])


def bits(axis):
    count = lax.axis_size(axis)
    return [1 << b for b in range(count.bit_length() - 1)]


def row_gather(value):
    parts = {0: value}
    for bit in reversed(bits("row")):
        parts.update({j ^ bit: exchange(part, "row", bit) for j, part in parts.items()})
    return [parts[j] for j in range(len(parts))]


def row_scatter(parts):
    parts = dict(enumerate(parts))
    for bit in bits("row"):
        got = {j ^ bit: exchange(parts[j].astype(BF), "row", bit) for j in parts if j & bit}
        parts = {j: parts[j].astype(F32) + part.astype(F32) for j, part in got.items()}
    return parts[0]


def row_gather_chain(value, gate):
    parts = {0: value}
    for bit in reversed(bits("row")):
        got = {j ^ bit: exchange(fence(part, gate), "row", bit) for j, part in parts.items()}
        parts.update(got)
        gate = yield list(got.values())
    return [parts[j] for j in range(len(parts))], gate


def row_scatter_chain(parts, gate):
    parts = dict(enumerate(parts))
    for bit in bits("row"):
        got = {j: exchange(fence(parts[j].astype(BF), gate), "row", bit) for j in parts if j & bit}
        gate = yield list(got.values())
        parts = {j ^ bit: parts[j ^ bit].astype(F32) + part.astype(F32) for j, part in got.items()}
    return parts[0], gate


def row_sum_chain(value, gate):
    for bit in bits("row"):
        got = exchange(fence(value, gate), "row", bit)
        gate = yield [got]
        value = value + got
    return value, gate


def wait(rounds):
    for _ in range(rounds):
        gate = yield []
    return gate


def ring():
    count, mine = lax.axis_size("seq"), lax.axis_index("seq")
    order = list(range(0, count, 2)) + list(range(1, count, 2))[::-1]
    half = mine >> 1
    place = jnp.where((mine & 1) == 0, half, count - 1 - half)

    def owner(k):
        at = (place + (k % count)) & (count - 1)
        return jnp.where(at < count // 2, 2 * at, 2 * count - 1 - 2 * at)

    ahead = [(order[i], order[(i + 1) % count]) for i in range(count)]
    behind = [(b, a) for a, b in ahead]
    return count, owner, ahead, behind


def ring_gather(value, earlier):
    count, owner, ahead, behind = ring()
    blocks = jnp.zeros(value.shape[:1] + (count,) + value.shape[1:], value.dtype)
    put = lambda blocks, block, k: lax.dynamic_update_index_in_dim(
        blocks, block, owner(k), 1, allow_negative_indices=False
    )
    blocks = put(blocks, value, 0)
    there, back = value, value
    for k in range(1, count // 2):
        there = lax.ppermute(there, "seq", ahead)
        back = lax.ppermute(back, "seq", behind)
        if k == count // 4:
            there = tie(there, earlier)
        blocks = put(put(blocks, there, -k), back, k)
    cut = value.shape[1] // 2
    there = lax.ppermute(there[:, :cut], "seq", ahead)
    back = lax.ppermute(back[:, cut:], "seq", behind)
    return put(blocks, jnp.concatenate([there, back], axis=1), count // 2)


def ring_scatter(parts, chains):
    count, owner, ahead, behind = ring()
    steps = jnp.arange(2, count + 1, dtype=jnp.int32)
    table = owner(jnp.stack([-steps, steps], axis=1).reshape(-1))
    there, back = pick(parts[0], owner(-1)), pick(parts[1], owner(1))
    gate, live, done = None, dict(chains), {}
    for k in range(count - 1):
        there = lax.ppermute(there, "seq", ahead)
        back = lax.ppermute(back, "seq", behind)
        kind = BF if k < count - 2 else F32
        there, back = ring_add(table, k, there, back, parts, kind, advance(live, gate, done))
        gate = there
    while live:
        advance(live, gate, done)
    return jnp.concatenate([there, back], axis=0), done


def advance(live, gate, done):
    needed = []
    for name in list(live):
        try:
            needed.extend(live[name].send(gate))
        except StopIteration as end:
            done[name] = end.value[0]
            del live[name]
    return needed


def rms_scale(values):
    return lax.rsqrt(jnp.mean(values * values, axis=-1, keepdims=True) + EPS_NORM)


def rms_back(grad_norm, values, inv_scale):
    return inv_scale * grad_norm - values * inv_scale**3 * jnp.mean(
        grad_norm * values, axis=-1, keepdims=True
    )


def matmul(spec, left, right, kind=F32):
    return jnp.einsum(spec, left, right, preferred_element_type=F32).astype(kind)


def local(
    tokens,
    cotangent,
    row_lengths,
    norm1_gain,
    w_in,
    w_router,
    conv_weight,
    a_log,
    dt_bias,
    head_gain,
    w_out,
    norm2_gain,
    w_gu,
    w_down,
):
    n_seq, n_row = lax.axis_size("seq"), lax.axis_size("row")
    seq, row = lax.axis_index("seq"), lax.axis_index("row")
    n_micro, _, n_tok, model = tokens.shape
    micros = list(range(n_micro))
    n_heads = a_log.shape[0]
    head_dim = head_gain.shape[0]
    n_taps, conv_width = conv_weight.shape
    slots = w_in.shape[1] // (n_heads * head_dim)
    width = conv_width // n_heads
    full = slots * head_dim
    length = n_tok * n_seq
    copies = n_seq // n_heads
    head = seq // copies
    gate_at = slots - 1

    def to_heads(value):
        return lax.all_to_all(jnp.repeat(value, copies, axis=0), "seq", 0, 0, tiled=True)

    def seq_parts(value):
        return lax.all_to_all(value, "seq", 0, 0, tiled=True)

    def from_heads(value):
        got = lax.all_to_all(value, "seq", 0, 0, tiled=True)
        return got if copies == 1 else got[::copies]

    def in_order(parts, axis):
        stacked = jnp.stack(parts)
        return jnp.concatenate([pick(stacked, row ^ j) for j in range(n_row)], axis=axis)

    cut = w_in.shape[0] // n_row
    w_piece = pick(w_in.reshape(n_row, cut, slots, n_heads, head_dim), row)
    w_got = to_heads(w_piece.transpose(2, 0, 1, 3).reshape(n_heads, cut, full))
    w_head = in_order(row_gather(w_got[:, None]), 1).reshape(model, full)
    w_rt = pick(w_router.reshape(model, -1, n_heads), head, 2)
    n_rt = w_rt.shape[1]
    w_rt = jnp.pad(w_rt, ((0, 0), (0, LANES - n_rt)))
    w_ext = jnp.concatenate([w_head, w_rt], axis=1)
    taps = pick(conv_weight.reshape(n_taps, gate_at, n_heads, head_dim), head, 2)
    taps = jnp.pad(taps.reshape(n_taps, width), ((0, 8 - n_taps), (0, 0)))
    par = jnp.concatenate(
        [
            head_gain[None],
            jnp.broadcast_to(lax.dynamic_index_in_dim(a_log, head, 0), (1, LANES)),
            jnp.broadcast_to(lax.dynamic_index_in_dim(dt_bias, head, 0), (1, LANES)),
            jnp.zeros((5, LANES), F32),
        ]
    )
    position = seq * n_tok + jnp.arange(n_tok, dtype=jnp.int32)
    live = (position[None, :] < row_lengths[:, :1]).astype(F32)[:, :, None]
    d_top = (cotangent[:, 0].astype(F32) * live).reshape(-1, model)
    d_rows = jnp.concatenate(row_gather(d_top.astype(BF)), axis=0)
    x_own = tokens[:, 0].astype(F32).reshape(-1, model)

    x_all = ring_gather(tokens[:, 0], w_got).reshape(n_micro, length, model)

    out_cut = w_out.shape[0] // n_row
    shard = w_out.shape[0]
    hidden = w_gu.shape[1] // 2
    unit_cut = hidden // n_seq // n_row
    unit_pad = -(-unit_cut // 16) * 16
    n_units = unit_pad * n_seq
    gu_piece = pick(w_gu.reshape(shard, 2, n_seq, n_row, unit_cut), row, 3)
    gu_piece = jnp.pad(gu_piece, ((0, 0), (0, 0), (0, 0), (0, unit_pad - unit_cut)))
    down_piece = lax.dynamic_slice_in_dim(w_down, row * unit_cut, unit_cut, 0)
    down_piece = jnp.pad(down_piece, ((shard - unit_pad, unit_pad - unit_cut), (0, 0)))
    weights = jnp.concatenate([gu_piece.reshape(shard, -1), down_piece], axis=1)
    weights = fence(weights, x_all)
    weights_all = lax.all_gather(weights, "seq", axis=0, tiled=True)

    normed_in, projected, router = project(x_all, norm1_gain, w_head, w_rt, [d_rows, weights])
    out_piece = lax.dynamic_slice_in_dim(w_out, row * out_cut, out_cut, 0)
    out_piece = jnp.broadcast_to(out_piece[None], (n_seq,) + out_piece.shape)
    out_got = lax.all_to_all(fence(out_piece, projected), "seq", 0, 0, tiled=True)
    prep = prepare(projected, router, taps, par, width)
    full_out = in_order([part[:, None] for part in row_gather(fence(out_got, prep[0]))], 1)
    full_out = full_out.reshape(model, model)
    sent, *kept = scan_states(prep, router, projected, par, gate_at)
    gated = sent.reshape(n_micro, n_seq, n_tok, head_dim).transpose(1, 0, 2, 3)
    gated = from_heads(gated).transpose(1, 2, 0, 3).reshape(-1, model)

    residual = x_own + matmul("tc,cd->td", gated, full_out)
    scale_mid = rms_scale(residual)
    mid_rows = jnp.concatenate(
        row_gather((residual * scale_mid * norm2_gain).astype(BF)), axis=0
    )
    act, d_gu, d_mid, down = feed(
        mid_rows, d_rows, weights_all, n_units, n_seq, shard - unit_pad
    )
    d_mid = row_scatter(list(d_mid.reshape(n_row, -1, model)))

    def row_parts(value, axis):
        return [pick(value, row ^ j, axis) for j in range(n_row)]

    g_gu = feed_grads(mid_rows, d_gu, shard)
    g_gu_sum = lax.psum_scatter(g_gu, "seq", scatter_dimension=0, tiled=True)[0]
    g_down = matmul("tf,td->fd", act, d_rows, BF)
    g_down_sum = lax.psum_scatter(g_down, "seq", scatter_dimension=0, tiled=True)

    d_mid = tie(d_mid, g_gu, g_down)
    g_norm2 = jnp.sum(d_mid * residual * scale_mid, axis=0)
    d_residual = d_top + rms_back(d_mid * norm2_gain, residual, scale_mid)
    d_low = d_residual.astype(BF)
    d_sent = matmul("td,cd->tc", d_low, full_out, BF)
    d_gated = d_sent.reshape(n_micro, n_tok, n_heads, head_dim).transpose(2, 0, 1, 3)
    d_gated = to_heads(d_gated).transpose(1, 0, 2, 3).reshape(n_micro, length, head_dim)

    mlp = times(act, down, [d_sent])
    out = (residual + row_scatter(list(mlp.reshape(n_row, -1, model)))).astype(BF)
    out = out.reshape(n_micro, 1, n_tok, model)
    g_out = matmul("tc,td->cd", tie(gated, d_sent), d_low).reshape(n_seq, n_row, out_cut, model)
    g_out = row_scatter(row_parts(g_out, 1)).astype(BF)

    mixed, news, state = kept
    d_mixed, d_news, d_state, d_gate_pre, g_head = scan_back(
        prep, router, projected, par, gate_at, mixed, d_gated
    )
    d_ext, g_taps, g_par = mixer_grads(
        prep, router, projected, taps, par, width,
        news, state, d_mixed, d_news, d_state, d_gate_pre,
    )
    if copies > 1:
        mine = (seq % copies == 0).astype(F32)
        d_ext = d_ext * mine.astype(BF)
        g_taps, g_par, g_head = g_taps * mine, g_par * mine, g_head * mine
    d_in = matmul("mtc,dc->mtd", d_ext, w_ext, BF).reshape(n_micro, n_seq, n_tok, model)
    g_in, in_lines = input_grads(normed_in, d_ext, w_ext, norm1_gain, full, [d_in])
    where = row.astype(jnp.int32).reshape(1)

    def input_chain():
        gate = yield [g_in]
        parts = row_parts(g_in.reshape(n_seq, n_row, cut, full), 1)
        part, gate = yield from row_scatter_chain(parts, gate)
        got = from_heads(fence(part.astype(BF), gate))
        gate = yield from wait(1)
        gate = yield [got]
        return (yield from row_gather_chain(got, gate))

    def small_chain():
        gate = yield from wait(1)
        padded = lambda value: jnp.pad(value, ((0, 0), (0, model - value.shape[1])))
        scalars = jnp.concatenate([g_head[:1], g_par[1:2], g_par[2:3]], axis=1)
        packed = [in_lines[: n_rt + 1], g_norm2[None], padded(scalars), padded(g_taps[:n_taps])]
        packed, gate = yield from row_sum_chain(jnp.concatenate(packed), gate)
        gate = yield from wait(1)
        packed = jnp.broadcast_to(packed[None], (n_seq,) + packed.shape)
        got = lax.all_to_all(fence(packed, gate), "seq", 0, 0, tiled=True)
        gate = yield from wait(1)
        gate = yield [got]
        return got, gate

    def output_chain():
        gate = yield from wait(1)
        got = seq_parts(fence(g_out, gate))
        gate = yield from wait(1)
        gate = yield [got]
        got = jnp.sum(got.astype(F32), axis=0).astype(BF)
        return (yield from row_gather_chain(got, gate))

    def feed_chain(value, rounds):
        gate = yield from wait(rounds)
        return (yield from row_gather_chain(value, gate))

    d_in, done = ring_scatter(
        d_in,
        {
            "input": input_chain(),
            "small": small_chain(),
            "output": output_chain(),
            "down": feed_chain(g_down_sum, 1),
            "gu": feed_chain(g_gu_sum, 4),
        },
    )
    grad_tokens = d_residual + rms_back(d_in * norm1_gain, x_own, rms_scale(x_own))
    grad_tokens = grad_tokens.reshape(n_micro, 1, n_tok, model)
    grad_out = place_rows(where, done["output"], out_cut)
    grad_down = place_rows(where, done["down"], unit_cut)
    grad_gu = place_units(where, done["gu"], unit_cut, unit_pad, n_seq)
    grad_in = place_heads(where, done["input"], slots)
    small = done["small"]

    total = jnp.sum(small[:, n_rt : n_rt + 3], axis=0)
    heads = small[::copies]
    conv_sum = heads[:, n_rt + 3 :, :width].reshape(n_heads, n_taps, gate_at, head_dim)
    conv_sum = conv_sum.transpose(1, 2, 0, 3).reshape(n_taps, conv_width)
    router_sum = heads[:, :n_rt].transpose(2, 1, 0).reshape(model, n_rt * n_heads)
    return (
        out,
        grad_tokens,
        total[0],
        grad_in,
        router_sum,
        conv_sum,
        heads[:, n_rt + 2, LANES + 2],
        heads[:, n_rt + 2, 2 * LANES + 2],
        total[2, :head_dim],
        grad_out,
        total[1],
        grad_gu,
        grad_down,
    )


def solution(mesh):
    by_rows = P("seq", None)
    by_tokens = P(None, "row", "seq", None)
    return jax.shard_map(
        local,
        mesh=mesh,
        in_specs=(
            by_tokens, by_tokens, P(None, "row"), P(), by_rows, P(), P(), P(), P(), P(),
            by_rows, P(), by_rows, by_rows,
        ),
        out_specs=(
            by_tokens, by_tokens, P(), by_rows, P(), P(), P(), P(), P(),
            by_rows, P(), by_rows, by_rows,
        ),
        check_vma=False,
    )
```

```python
from functools import partial

import jax
import jax.numpy as jnp
from jax import lax
from jax.experimental import pallas as pl
from jax.experimental.pallas import tpu as pltpu
from jax.sharding import PartitionSpec as P

BF = jnp.bfloat16
F32 = jnp.float32
EPS_NORM = 1e-05
EPS_UNIT = 1e-06
CH = 64
ST = 128
HALO = 16
LANES = 128
VMEM_BYTES = 60 * 1024 * 1024
SMALL_BYTES = 50 * 1024 * 1024


def halves(value):
    high = value.astype(BF)
    return (high, (value - high.astype(F32)).astype(BF))


def dot(left, right, over_left=1, over_right=0):
    return lax.dot_general(
        left, right, (((over_left,), (over_right,)), ((), ())), preferred_element_type=F32
    )


def mm(left, right, over_left=1, over_right=0):
    left = left if isinstance(left, tuple) else (left,)
    right = right if isinstance(right, tuple) else (right,)
    total = dot(left[0], right[0], over_left, over_right)
    if len(right) > 1:
        total = total + dot(left[0], right[1], over_left, over_right)
    if len(left) > 1:
        total = total + dot(left[1], right[0], over_left, over_right)
    return total


def exact_sum(ones, value):
    high = value.astype(BF)
    rest = value - high.astype(F32)
    mid = rest.astype(BF)
    low = (rest - mid.astype(F32)).astype(BF)
    return dot(ones, high) + dot(ones, mid) + dot(ones, low)


def step_orders():
    row = lax.broadcasted_iota(jnp.int32, (ST, ST), 0)
    col = lax.broadcasted_iota(jnp.int32, (ST, ST), 1)
    order = lambda i: 2 * (i & (CH - 1)) + (i >> 6)
    return order(row), order(col)


def sees():
    row = lax.broadcasted_iota(jnp.int32, (CH, ST), 0)
    col = lax.broadcasted_iota(jnp.int32, (CH, ST), 1)
    return (col & (CH - 1)) <= row


def twice(value):
    return jnp.concatenate([value, value], axis=0)


def log_decays(router, par):
    lane = lax.broadcasted_iota(jnp.int32, (CH, LANES), 1)
    pre = router + par[2:3]
    soft = jnp.maximum(pre, 0.0) + jnp.log1p(jnp.exp(-jnp.abs(pre)))
    decay = -jnp.exp(par[1:2]) * soft
    row = lax.broadcasted_iota(jnp.int32, (CH, CH), 0)
    col = lax.broadcasted_iota(jnp.int32, (CH, CH), 1)
    below = jnp.where(col <= row, 1.0, 0.0).astype(BF)
    total = exact_sum(below, jnp.where(lane == 2, decay, 0.0))
    return decay, total


def gate_columns(router, par):
    strength = jax.nn.sigmoid(router)
    decay, total = log_decays(router, par)
    beta = jnp.concatenate([strength[:, 0:1], strength[:, 1:2]], axis=0)
    doubled = twice(total)
    g_col = doubled[:, 2:3]
    g_row = doubled.T[2:3, :]
    g_last = total[CH - 1 : CH, 2:3]
    return beta, g_col, g_row, g_last, decay


def seen_decay(g_col, g_row, visible):
    return jnp.where(visible, jnp.exp(jnp.where(visible, g_col[:CH] - g_row, 0.0)), 0.0)


def unit(value):
    scale = lax.rsqrt(jnp.sum(value * value, axis=-1, keepdims=True) + EPS_UNIT)
    return value * scale, scale


def taps_sum(window, weight, start):
    total = weight[0:1] * window[pl.ds(start + 5, CH), :]
    for tap in range(1, 4):
        total = total + weight[tap : tap + 1] * window[pl.ds(start + 5 + tap, CH), :]
    return total


def fill_window(window, proj_ref, halo_ref, is_first):
    width = window.shape[1]
    edge = halo_ref[0, :, :width].astype(F32)[HALO - 8 :]
    window[0:8, :] = jnp.where(is_first, 0.0, edge)
    window[8:, :] = proj_ref[0, :, :width].astype(F32)


def prep_kernel(
    count, proj_ref, halo_ref, router_ref, taps_ref, par_ref,
    solve_ref, wmat_ref, umat_ref, seen_ref, q_ref, k_ref, window,
):
    fill_window(window, proj_ref, halo_ref, pl.program_id(1) == 0)
    weight = taps_ref[...]
    par = par_ref[...]
    o_row, o_col = step_orders()
    strict = o_row > o_col
    eye = jnp.where(o_row == o_col, 1.0, 0.0)
    visible = sees()
    many = range(count)
    lower, rights = [], []
    for n in many:
        conv = taps_sum(window, weight, n * CH)
        act = conv * jax.nn.sigmoid(conv)
        q = unit(act[:, 0:128])[0].astype(BF)
        k = jnp.concatenate(
            [unit(act[:, 128:256])[0], unit(act[:, 256:384])[0]], axis=0
        ).astype(BF)
        v = jnp.concatenate([act[:, 384:512], act[:, 512:640]], axis=0).astype(BF)
        beta, g_col, g_row, _, _ = gate_columns(
            router_ref[0, n * CH : (n + 1) * CH, :], par
        )
        gaps = seen_decay(g_col, g_row, visible)
        lower.append(jnp.where(strict, beta * twice(gaps) * dot(k, k, 1, 1), 0.0))
        kf = k.astype(F32)
        rights.append(
            jnp.concatenate([beta * jnp.exp(g_col) * kf, beta * v.astype(F32)], axis=1)
        )
        seen_ref[0, n] = gaps * dot(q, k, 1, 1)
        q_ref[0, n] = q
        k_ref[0, n] = k
    inverse = [eye - jnp.where((o_row >> 1) == (o_col >> 1), part, 0.0) for part in lower]
    for level in range(1, 7):
        at = ((o_row >> level) ^ (o_col >> level)) == 1
        parts = [halves(jnp.where(at, part, 0.0)) for part in lower]
        known = [halves(value) for value in inverse]
        inner = [halves(mm(parts[n], known[n])) for n in many]
        inverse = [inverse[n] - mm(known[n], inner[n]) for n in many]
    for n in many:
        solve_ref[0, n] = inverse[n]
        both = mm(halves(inverse[n]), halves(rights[n]))
        wmat_ref[0, n] = both[:, :128]
        umat_ref[0, n] = both[:, 128:]


def head_norm(mixed):
    return lax.rsqrt(jnp.mean(mixed * mixed, axis=-1, keepdims=True) + EPS_NORM)


def scan_kernel(
    n_micro, count, wmat_ref, umat_ref, seen_ref, q_ref, k_ref, router_ref, gate_ref, par_ref,
    out_ref, mixed_ref, news_ref, state_ref, state,
):
    @pl.when(pl.program_id(0) == 0)
    def _():
        state[...] = jnp.zeros_like(state)

    par = par_ref[...]
    now = [state[m] for m in range(n_micro)]
    for n in range(count):
        rows = slice(n * CH, (n + 1) * CH)
        for m in range(n_micro):
            _, g_col, _, g_last, _ = gate_columns(router_ref[m, rows, :], par)
            held = halves(now[m])
            state_ref[m, n] = now[m]
            news = umat_ref[m, n] - mm(halves(wmat_ref[m, n]), held)
            news_ref[m, n] = news
            news_h = halves(news)
            ends = halves(jnp.exp(g_last - g_col) * k_ref[m, n].astype(F32))
            now[m] = jnp.exp(g_last) * now[m] + mm(ends, news_h, 0, 0)
            mixed = jnp.exp(g_col[:CH]) * mm(q_ref[m, n], held) + mm(halves(seen_ref[m, n]), news_h)
            mixed_ref[m, n] = mixed
            gate = gate_ref[m, rows, :].astype(F32)
            tok = out_ref.shape[2]
            at = slice(n * CH % tok, n * CH % tok + CH)
            out_ref[n * CH // tok, m, at, :] = (
                mixed * head_norm(mixed) * par[0:1] * (gate * jax.nn.sigmoid(gate))
            ).astype(BF)
    for m in range(n_micro):
        state[m] = now[m]


def scan_back_kernel(
    n_micro, count, wmat_ref, seen_ref, q_ref, k_ref, router_ref, gate_ref, par_ref, mixed_ref, d_out_ref,
    d_mixed_ref, d_news_ref, d_state_ref, d_gate_ref, gain_ref, state,
):
    @pl.when(pl.program_id(0) == 0)
    def _():
        state[...] = jnp.zeros_like(state)
        gain_ref[...] = jnp.zeros_like(gain_ref)

    par = par_ref[...]
    now = [state[m] for m in range(n_micro)]
    gain = jnp.zeros((1, LANES), F32)
    for n in reversed(range(count)):
        rows = slice(n * CH, (n + 1) * CH)
        for m in range(n_micro):
            _, g_col, _, g_last, _ = gate_columns(router_ref[m, rows, :], par)
            mixed = mixed_ref[m, n]
            gate = gate_ref[m, rows, :].astype(F32)
            tok = d_out_ref.shape[2]
            at = slice(n * CH % tok, n * CH % tok + CH)
            d_out = d_out_ref[n * CH // tok, m, at, :].astype(F32)
            scale = head_norm(mixed)
            normed = mixed * scale
            sig = jax.nn.sigmoid(gate)
            silu = gate * sig
            gain = gain + jnp.sum(d_out * normed * silu, axis=0, keepdims=True)
            d_gate = d_out * normed * par[0:1] * (sig * (1.0 + gate * (1.0 - sig)))
            d_gate_ref[m, rows, :] = d_gate.astype(BF)
            d_normed = d_out * par[0:1] * silu
            d_mixed = scale * d_normed - mixed * scale**3 * jnp.mean(
                d_normed * mixed, axis=-1, keepdims=True
            )
            d_mixed_ref[m, n] = d_mixed
            d_mixed_h = halves(d_mixed)
            d_state_ref[m, n] = now[m]
            ends = halves(jnp.exp(g_last - g_col) * k_ref[m, n].astype(F32))
            d_news = mm(halves(seen_ref[m, n]), d_mixed_h, 0, 0) + mm(ends, halves(now[m]))
            d_news_ref[m, n] = d_news
            q_eff = halves(jnp.exp(g_col[:CH]) * q_ref[m, n].astype(F32))
            now[m] = (
                jnp.exp(g_last) * now[m]
                + mm(q_eff, d_mixed_h, 0, 0)
                - mm(halves(wmat_ref[m, n]), halves(d_news), 0, 0)
            )
    gain_ref[0:1, :] += gain
    for m in range(n_micro):
        state[m] = now[m]


def in_step(chains):
    while chains:
        chains = [chain for chain in chains if next(chain, chain) is not chain]


def unit_back(grad, value, scale):
    return scale * grad - value * scale**3 * jnp.sum(grad * value, axis=-1, keepdims=True)


def grads_kernel(
    count, proj_ref, halo_ref, router_ref, taps_ref, par_ref, solve_ref, seen_ref, news_ref, state_ref,
    d_mixed_ref, d_news_ref, d_state_ref, d_gate_ref,
    d_ext_ref, g_taps_ref, g_par_ref, window, d_window,
):
    step = pl.program_id(1)
    size = count * CH
    fill_window(window, proj_ref, halo_ref, step == pl.num_programs(1) - 1)

    @pl.when((step == 0) & (pl.program_id(0) == 0))
    def _():
        g_taps_ref[...] = jnp.zeros_like(g_taps_ref)
        g_par_ref[...] = jnp.zeros_like(g_par_ref)

    @pl.when(step == 0)
    def _():
        d_window[size:, :] = jnp.zeros((8, d_window.shape[1]), F32)

    @pl.when(step > 0)
    def _():
        d_window[size:, :] = d_window[0:8, :]

    weight = taps_ref[...]
    par = par_ref[...]
    o_row, o_col = step_orders()
    strict = o_row > o_col
    visible = sees()
    row = lax.broadcasted_iota(jnp.int32, (CH, CH), 0)
    col = lax.broadcasted_iota(jnp.int32, (CH, CH), 1)
    above = jnp.where(col >= row, 1.0, 0.0).astype(BF)
    lane = lax.broadcasted_iota(jnp.int32, (CH, LANES), 1)
    last = lax.broadcasted_iota(jnp.int32, (CH, LANES), 0) == CH - 1
    sums = [jnp.zeros((1, LANES), F32), jnp.zeros((1, LANES), F32)]

    def one(n):
        rows = slice(n * CH, (n + 1) * CH)
        conv = taps_sum(window, weight, n * CH)
        sig = jax.nn.sigmoid(conv)
        act = conv * sig
        qn, q_scale = unit(act[:, 0:128])
        k0n, k0_scale = unit(act[:, 128:256])
        k1n, k1_scale = unit(act[:, 256:384])
        q = qn.astype(BF)
        k = jnp.concatenate([k0n, k1n], axis=0).astype(BF)
        kf, qf = k.astype(F32), q.astype(F32)
        router = router_ref[0, rows, :]
        yield
        d_right = mm(halves(solve_ref[0, n]), halves(d_news_ref[0, n]), 0, 0)
        beta, g_col, g_row, g_last, decay = gate_columns(router, par)
        gaps = seen_decay(g_col, g_row, visible)
        yield
        ratio = jnp.where(strict, twice(gaps), 0.0)
        grown = jnp.exp(g_col)
        left = jnp.exp(g_last - g_col)
        gram = dot(k, k, 1, 1)
        state = state_ref[0, n]
        state_h = halves(state)
        news = news_ref[0, n]
        news_h = halves(news)
        d_mixed_h = halves(d_mixed_ref[0, n])
        d_state = d_state_ref[0, n]
        d_seen = mm(d_mixed_h, news_h, 1, 1)
        yield
        d_q_grown = grown[:CH] * mm(d_mixed_h, state_h, 1, 1)
        d_right_h = halves(d_right)
        d_lower = jnp.where(strict, -mm(d_right_h, news_h, 1, 1), 0.0)
        yield
        d_ends = left * mm(news_h, halves(d_state), 1, 1)
        d_pre = (1.0 - beta) * jnp.sum(d_right * news, axis=-1, keepdims=True)
        d_v = beta * d_right
        yield
        d_grown_k = -beta * mm(d_right_h, state_h, 1, 1)
        d_scores = halves(d_seen * gaps)
        seen_both = d_seen * seen_ref[0, n]
        yield
        d_q = d_q_grown + mm(d_scores, k)
        d_k = grown * d_grown_k
        d_gram = beta * ratio * d_lower
        both = d_gram * gram
        d_g = jnp.sum(both, axis=-1, keepdims=True) + jnp.sum(d_k * kf, axis=-1, keepdims=True)
        d_g_row = -jnp.sum(both, axis=0, keepdims=True)
        yield
        d_k = d_k + mm(halves(d_gram + d_gram.T), k) + d_ends
        d_g_q = jnp.sum(seen_both + d_q_grown * qf, axis=-1, keepdims=True)
        yield
        d_k = d_k + mm(d_scores, q, 0, 0)
        d_g_row = d_g_row - jnp.sum(seen_both, axis=0, keepdims=True)
        ends_sum = jnp.sum(d_ends * kf, axis=-1, keepdims=True)
        d_g = d_g - ends_sum
        d_last = jnp.sum(ends_sum, axis=0, keepdims=True) + jnp.exp(g_last) * jnp.sum(
            jnp.sum(d_state * state, axis=-1, keepdims=True), axis=0, keepdims=True
        )
        d_g_rows = jnp.broadcast_to(d_g_row, (LANES, ST)).T
        d_g_tok = d_g_q + d_g[:CH] + d_g[CH:] + d_g_rows[:CH] + d_g_rows[CH:]
        d_g_tok = d_g_tok + jnp.where(last, d_last, 0.0)
        yield
        d_decay = exact_sum(above, d_g_tok)
        yield
        d_soft = -jnp.exp(par[1:2]) * jax.nn.sigmoid(router + par[2:3]) * d_decay
        d_router = jnp.where(
            lane == 0,
            d_pre[:CH],
            jnp.where(lane == 1, d_pre[CH:], jnp.where(lane == 2, d_soft, 0.0)),
        )
        width = window.shape[1]
        d_ext_ref[0, rows, width : width + LANES] = d_gate_ref[0, rows, :]
        d_ext_ref[0, rows, width + LANES :] = d_router.astype(BF)
        sums[0] += jnp.sum(jnp.where(lane == 2, d_decay * decay, 0.0), axis=0, keepdims=True)
        sums[1] += jnp.sum(jnp.where(lane == 2, d_soft, 0.0), axis=0, keepdims=True)
        d_act = jnp.concatenate(
            [
                unit_back(d_q, act[:, 0:128], q_scale),
                unit_back(d_k[:CH], act[:, 128:256], k0_scale),
                unit_back(d_k[CH:], act[:, 256:384], k1_scale),
                d_v[:CH],
                d_v[CH:],
            ],
            axis=1,
        )
        d_window[rows, :] = d_act * (sig * (1.0 + conv * (1.0 - sig)))

    in_step([one(n) for n in range(count)])
    g_alog, g_dt = sums
    g_par_ref[1:2, :] += g_alog
    g_par_ref[2:3, :] += g_dt
    for n in range(count):
        start = n * CH
        here = d_window[pl.ds(start, CH), :]
        total = weight[3:4] * here
        for tap in range(3):
            total = total + weight[tap : tap + 1] * d_window[pl.ds(start + 3 - tap, CH), :]
        d_ext_ref[0, pl.ds(start, CH), : total.shape[1]] = total.astype(BF)
        for tap in range(4):
            g_taps_ref[tap : tap + 1, :] += jnp.sum(
                here * window[pl.ds(start + 5 + tap, CH), :], axis=0, keepdims=True
            )


def params(*semantics):
    return pltpu.CompilerParams(dimension_semantics=semantics, vmem_limit_bytes=VMEM_BYTES)


def small_params(*semantics):
    return pltpu.CompilerParams(dimension_semantics=semantics, vmem_limit_bytes=SMALL_BYTES)


def cost(chunks, per_chunk):
    return pl.CostEstimate(
        flops=int(chunks * per_chunk * 1.1e9), transcendentals=0, bytes_accessed=1 << 20
    )


def launch(kernel, in_specs, earlier, **options):
    n_in = len(in_specs)

    def body(*refs):
        kernel(*refs[:n_in], *refs[n_in + len(earlier) :])

    specs = list(in_specs) + [pl.BlockSpec(memory_space=pl.ANY)] * len(earlier)
    called = pl.pallas_call(body, in_specs=specs, **options)
    return lambda *operands: called(*operands, *earlier)


def fence(value, *earlier):
    earlier = [other for other in earlier if other is not None]
    if not earlier:
        return value
    anywhere = pl.BlockSpec(memory_space=pl.ANY)
    return pl.pallas_call(
        lambda *refs: None,
        in_specs=[anywhere] * (1 + len(earlier)),
        out_specs=anywhere,
        out_shape=jax.ShapeDtypeStruct(value.shape, value.dtype),
        input_output_aliases={0: 0},
        name="fence",
    )(value, *earlier)


def whole(shape):
    return pl.BlockSpec(shape, lambda *_: (0,) * len(shape))


def prepare(projected, router, taps, par, width, earlier=(), count=8):
    n_micro, length, full = projected.shape
    steps = length // (count * CH)
    chunks = length // CH
    size = count * CH
    per = lambda *tail: pl.BlockSpec((1, count) + tail, lambda m, i: (m, i, 0, 0))
    made = lambda kind, *tail: jax.ShapeDtypeStruct((n_micro, chunks) + tail, kind)
    return launch(
        partial(prep_kernel, count),
        [
            pl.BlockSpec((1, size, full), lambda m, i: (m, i, 0)),
            pl.BlockSpec((1, HALO, full), lambda m, i: (m, jnp.maximum(i * (size // HALO) - 1, 0), 0)),
            pl.BlockSpec((1, size, LANES), lambda m, i: (m, i, 0)),
            whole(taps.shape),
            whole(par.shape),
        ],
        earlier,
        grid=(n_micro, steps),
        out_specs=[per(ST, ST), per(ST, 128), per(ST, 128), per(CH, ST), per(CH, 128), per(ST, 128)],
        out_shape=[
            made(F32, ST, ST), made(F32, ST, 128), made(F32, ST, 128), made(F32, CH, ST),
            made(BF, CH, 128), made(BF, ST, 128),
        ],
        scratch_shapes=[pltpu.VMEM((size + 8, width), F32)],
        compiler_params=params("arbitrary", "arbitrary"),
        cost_estimate=cost(n_micro * chunks, 0.75),
        name="mixer_prepare",
    )(projected, projected, router, taps, par)


def scan_states(prep, router, projected, par, gate_at, n_tok, earlier=(), count=4):
    _, wmat, umat, seen, q, k = prep
    n_micro, chunks = wmat.shape[:2]
    length = chunks * CH
    size = count * CH
    per = lambda *tail: pl.BlockSpec((n_micro, count) + tail, lambda i: (0, i, 0, 0))
    made = lambda kind, *tail: jax.ShapeDtypeStruct((n_micro, chunks) + tail, kind)
    return launch(
        partial(scan_kernel, n_micro, count),
        [
            per(ST, 128), per(ST, 128), per(CH, ST), per(CH, 128), per(ST, 128),
            pl.BlockSpec((n_micro, size, LANES), lambda i: (0, i, 0)),
            pl.BlockSpec((n_micro, size, 128), lambda i: (0, i, gate_at)),
            whole(par.shape),
        ],
        earlier,
        grid=(chunks // count,),
        out_specs=[
            pl.BlockSpec((size // n_tok, n_micro, n_tok, 128), lambda i: (i, 0, 0, 0)),
            per(CH, 128), per(ST, 128), per(128, 128),
        ],
        out_shape=[
            jax.ShapeDtypeStruct((length // n_tok, n_micro, n_tok, 128), BF),
            made(F32, CH, 128), made(F32, ST, 128), made(F32, 128, 128),
        ],
        scratch_shapes=[pltpu.VMEM((n_micro, 128, 128), F32)],
        compiler_params=params("arbitrary"),
        cost_estimate=cost(n_micro * chunks, 0.5),
        name="mixer_scan",
    )(wmat, umat, seen, q, k, router, projected, par)


def scan_back(prep, router, projected, par, gate_at, mixed, d_out, earlier=(), count=4):
    _, wmat, _, seen, q, k = prep
    n_micro, chunks = wmat.shape[:2]
    length = chunks * CH
    size = count * CH
    blocks = chunks // count
    n_tok = d_out.shape[2]
    per = lambda *tail: pl.BlockSpec((n_micro, count) + tail, lambda i: (0, blocks - 1 - i, 0, 0))
    made = lambda kind, *tail: jax.ShapeDtypeStruct((n_micro, chunks) + tail, kind)
    return launch(
        partial(scan_back_kernel, n_micro, count),
        [
            per(ST, 128), per(CH, ST), per(CH, 128), per(ST, 128),
            pl.BlockSpec((n_micro, size, LANES), lambda i: (0, blocks - 1 - i, 0)),
            pl.BlockSpec((n_micro, size, 128), lambda i: (0, blocks - 1 - i, gate_at)),
            whole(par.shape),
            per(CH, 128),
            pl.BlockSpec(
                (size // n_tok, n_micro, n_tok, 128), lambda i: (blocks - 1 - i, 0, 0, 0)
            ),
        ],
        earlier,
        grid=(blocks,),
        out_specs=[
            per(CH, 128), per(ST, 128), per(128, 128),
            pl.BlockSpec((n_micro, size, 128), lambda i: (0, blocks - 1 - i, 0)),
            whole((8, LANES)),
        ],
        out_shape=[
            made(F32, CH, 128), made(F32, ST, 128), made(F32, 128, 128),
            jax.ShapeDtypeStruct((n_micro, length, 128), BF),
            jax.ShapeDtypeStruct((8, LANES), F32),
        ],
        scratch_shapes=[pltpu.VMEM((n_micro, 128, 128), F32)],
        compiler_params=params("arbitrary"),
        cost_estimate=cost(n_micro * chunks, 0.4),
        name="mixer_scan_back",
    )(wmat, seen, q, k, router, projected, par, mixed, d_out)


def mixer_grads(
    prep, router, projected, taps, par, width, news, state, d_mixed, d_news, d_state, d_gate,
    earlier=(), count=4,
):
    solve, _, _, seen, _, _ = prep
    n_micro, chunks = solve.shape[:2]
    length = chunks * CH
    size = count * CH
    blocks = chunks // count
    full = projected.shape[2]
    per = lambda *tail: pl.BlockSpec((1, count) + tail, lambda m, i: (m, blocks - 1 - i, 0, 0))
    rows = lambda n: pl.BlockSpec((1, size, n), lambda m, i: (m, blocks - 1 - i, 0))
    before = lambda m, i: (m, jnp.maximum((blocks - 1 - i) * (size // HALO) - 1, 0), 0)
    return launch(
        partial(grads_kernel, count),
        [
            rows(full), pl.BlockSpec((1, HALO, full), before), rows(LANES),
            whole(taps.shape), whole(par.shape),
            per(ST, ST), per(CH, ST), per(ST, 128), per(128, 128),
            per(CH, 128), per(ST, 128), per(128, 128), rows(LANES),
        ],
        earlier,
        grid=(n_micro, blocks),
        out_specs=[rows(width + 2 * LANES), whole((8, width)), whole((8, LANES))],
        out_shape=[
            jax.ShapeDtypeStruct((n_micro, length, width + 2 * LANES), BF),
            jax.ShapeDtypeStruct((8, width), F32),
            jax.ShapeDtypeStruct((8, LANES), F32),
        ],
        scratch_shapes=[pltpu.VMEM((size + 8, width), F32), pltpu.VMEM((size + 8, width), F32)],
        compiler_params=params("arbitrary", "arbitrary"),
        cost_estimate=cost(n_micro * chunks, 1.0),
        name="mixer_grads",
    )(projected, projected, router, taps, par, solve, seen, news, state, d_mixed, d_news, d_state, d_gate)


def project_kernel(x_ref, gain_ref, weight_ref, router_weight_ref, normed_ref, out_ref, router_ref):
    per, _, n_tok, model = x_ref.shape
    x = x_ref[:, 0].reshape(per * n_tok, model).astype(F32)
    scale = lax.rsqrt(jnp.mean(x * x, axis=-1, keepdims=True) + EPS_NORM)
    normed = (x * scale * gain_ref[...]).astype(BF)
    normed_ref[0] = normed
    out_ref[0] = dot(normed, weight_ref[...]).astype(BF)
    router_ref[0] = dot(normed, router_weight_ref[...])


def project(x, gain, weight, router_weight, earlier=(), size=256):
    n_seq, n_micro, n_tok, model = x.shape
    length = n_seq * n_tok
    full = weight.shape[1]
    blocks = pl.BlockSpec((size // n_tok, 1, n_tok, model), lambda m, i: (i, m, 0, 0))
    rows = lambda n: pl.BlockSpec((1, size, n), lambda m, i: (m, i, 0))
    return launch(
        project_kernel,
        [blocks, whole((1, model)), whole(weight.shape), whole(router_weight.shape)],
        earlier,
        grid=(n_micro, length // size),
        out_specs=[rows(model), rows(full), rows(LANES)],
        out_shape=[
            jax.ShapeDtypeStruct((n_micro, length, model), BF),
            jax.ShapeDtypeStruct((n_micro, length, full), BF),
            jax.ShapeDtypeStruct((n_micro, length, LANES), F32),
        ],
        compiler_params=params("arbitrary", "arbitrary"),
        cost_estimate=cost(n_micro * length // CH, 0.35),
        name="project",
    )(x, gain[None], weight, router_weight)


def ring_add_kernel(table, ahead_ref, behind_ref, up_ref, low_ref, up_out, low_out):
    up_out[...] = (ahead_ref[...].astype(F32) + up_ref[0, 0].astype(F32)).astype(up_out.dtype)
    low_out[...] = (behind_ref[...].astype(F32) + low_ref[0, 0].astype(F32)).astype(low_out.dtype)


def ring_add(table, step, ahead, behind, parts, kind, earlier=()):
    rows, model = ahead.shape
    one = pl.BlockSpec((rows, model), lambda i, table: (0, 0))
    part = lambda m: pl.BlockSpec((1, 1, rows, model), lambda i, table: (m, table[2 * step + m], 0, 0))
    made = jax.ShapeDtypeStruct((rows, model), kind)
    n_in = 5

    def body(*refs):
        ring_add_kernel(*refs[:n_in], *refs[n_in + len(earlier) :])

    return pl.pallas_call(
        body,
        grid_spec=pltpu.PrefetchScalarGridSpec(
            num_scalar_prefetch=1,
            grid=(1,),
            in_specs=[one, one, part(0), part(1)] + [pl.BlockSpec(memory_space=pl.ANY)] * len(earlier),
            out_specs=[one, one],
        ),
        out_shape=[made, made],
        compiler_params=small_params("arbitrary"),
        cost_estimate=cost(1, 1.0),
        name="ring_add",
    )(table, ahead, behind, parts, parts, *earlier)


def input_grads_kernel(normed_ref, d_ext_ref, w_ext_ref, gain_ref, out_ref, lines_ref):
    total = dot(normed_ref[0], d_ext_ref[0], 0, 0)
    for m in range(1, normed_ref.shape[0]):
        total = total + dot(normed_ref[m], d_ext_ref[m], 0, 0)
    full = out_ref.shape[1]
    out_ref[...] = total[:, :full].astype(BF)
    norm = jnp.sum(total * w_ext_ref[...].astype(F32), axis=1, keepdims=True)
    lane = lax.broadcasted_iota(jnp.int32, (total.shape[0], LANES), 1)
    tail = jnp.where(lane == 3, norm, total[:, full:])
    lines = tail.T[:8]
    row = lax.broadcasted_iota(jnp.int32, lines.shape, 0)
    lines_ref[...] = jnp.where(row == 3, lines / gain_ref[...], lines)


def input_grads(normed, d_ext, w_ext, gain, full, earlier=(), size=256):
    n_micro, length, model = normed.shape
    wide = d_ext.shape[2]
    return launch(
        input_grads_kernel,
        [
            pl.BlockSpec((n_micro, length, size), lambda i: (0, 0, i)),
            whole(d_ext.shape),
            pl.BlockSpec((size, wide), lambda i: (i, 0)),
            pl.BlockSpec((1, size), lambda i: (0, i)),
        ],
        earlier,
        grid=(model // size,),
        out_specs=[
            pl.BlockSpec((size, full), lambda i: (i, 0)),
            pl.BlockSpec((8, size), lambda i: (0, i)),
        ],
        out_shape=[
            jax.ShapeDtypeStruct((model, full), BF),
            jax.ShapeDtypeStruct((8, model), F32),
        ],
        compiler_params=params("arbitrary"),
        cost_estimate=cost(1, 7.0),
        name="input_grads",
    )(normed, d_ext, w_ext, gain[None])


def place_heads_kernel(n_heads, copies, slots, cut, lines, where, *refs):
    parts, out_ref, small_ref = refs[:-2], refs[-2], refs[-1]
    for j, part in enumerate(parts):
        at = where[0] ^ j
        for slot in range(slots):
            for h in range(n_heads):
                to = (slot * n_heads + h) * LANES
                value = part[h * copies, :cut, slot * LANES : (slot + 1) * LANES]
                out_ref[at, :, to : to + LANES] = value.astype(F32)
        for s in range(part.shape[0]):
            high = part[s, cut : cut + lines].astype(F32)
            low = part[s, cut + lines : cut + 2 * lines].astype(F32)
            for r in range(len(parts)):

                @pl.when(at == r)
                def _(s=s, r=r, value=high + low):
                    small_ref[s, r * lines : (r + 1) * lines] = value


def place_heads(where, parts, n_heads, slots, cut, lines):
    n_seq, rows, full = parts[0].shape
    n_parts = len(parts)
    shape = (n_parts, cut, full * n_heads)
    small = (n_seq, n_parts * lines, full)
    grad, values = pl.pallas_call(
        partial(place_heads_kernel, n_heads, n_seq // n_heads, slots, cut, lines),
        grid_spec=pltpu.PrefetchScalarGridSpec(
            num_scalar_prefetch=1,
            grid=(1,),
            in_specs=[pl.BlockSpec(part.shape, lambda i, where: (0, 0, 0)) for part in parts],
            out_specs=[
                pl.BlockSpec(shape, lambda i, where: (0, 0, 0)),
                pl.BlockSpec(small, lambda i, where: (0, 0, 0)),
            ],
        ),
        out_shape=[jax.ShapeDtypeStruct(shape, F32), jax.ShapeDtypeStruct(small, F32)],
        compiler_params=small_params("arbitrary"),
        cost_estimate=cost(1, 3.0),
        name="place_heads",
    )(where, *parts)
    return grad.reshape(-1, full * n_heads), values


def pack_kernel(lines, own_ref, got_ref, small_ref, out_ref):
    n_seq, cut, full = own_ref.shape
    rows = out_ref.shape[1]
    tail = list(halves(small_ref[...]))
    if rows > cut + 2 * lines:
        tail.append(jnp.zeros((rows - cut - 2 * lines, full), BF))
    tail = jnp.concatenate(tail, axis=0)
    for s in range(n_seq):
        out_ref[s, :cut] = (own_ref[s].astype(F32) + got_ref[s].astype(F32)).astype(BF)
        out_ref[s, cut:] = tail


def pack(own, got, small, rows, earlier=()):
    n_seq, cut, full = own.shape
    return launch(
        partial(pack_kernel, small.shape[0]),
        [whole(own.shape), whole(got.shape), whole(small.shape)],
        earlier,
        grid=(1,),
        out_specs=whole((n_seq, rows, full)),
        out_shape=jax.ShapeDtypeStruct((n_seq, rows, full), BF),
        compiler_params=small_params("arbitrary"),
        cost_estimate=cost(1, 1.5),
        name="pack",
    )(own, got, small)


def place_units_kernel(unit_cut, unit_pad, n_seq, where, *refs):
    parts, out_ref = refs[:-1], refs[-1]
    n_row = len(parts)
    group = unit_cut * n_row
    hidden = group * n_seq
    for block in range(hidden // LANES):
        low = (block * LANES // group) * unit_pad // LANES * LANES
        high = ((block * LANES + LANES - 1) // group + 1) * unit_pad
        high = min(n_seq * unit_pad, -(-high // LANES) * LANES)
        col = lax.broadcasted_iota(jnp.int32, (high - low, LANES), 1) + block * LANES
        row = lax.broadcasted_iota(jnp.int32, (high - low, LANES), 0) + low
        inner = lax.rem(col, group)
        owner = lax.div(inner, unit_cut)
        unit = lax.div(col, group) * unit_pad + lax.rem(inner, unit_cut)
        total = [0.0, 0.0]
        for j, part in enumerate(parts):
            chosen = jnp.where((unit == row) & (owner == (where[0] ^ j)), 1.0, 0.0).astype(BF)
            for half in range(2):
                at = half * n_seq * unit_pad
                total[half] = total[half] + dot(part[:, at + low : at + high], chosen)
        for half in range(2):
            to = half * hidden + block * LANES
            out_ref[:, to : to + LANES] = total[half]


def place_units(where, parts, unit_cut, unit_pad, n_seq):
    rows = parts[0].shape[0]
    shape = (rows, 2 * unit_cut * n_seq * len(parts))
    return pl.pallas_call(
        partial(place_units_kernel, unit_cut, unit_pad, n_seq),
        grid_spec=pltpu.PrefetchScalarGridSpec(
            num_scalar_prefetch=1,
            grid=(1,),
            in_specs=[pl.BlockSpec(part.shape, lambda i, where: (0, 0)) for part in parts],
            out_specs=pl.BlockSpec(shape, lambda i, where: (0, 0)),
        ),
        out_shape=jax.ShapeDtypeStruct(shape, F32),
        compiler_params=small_params("arbitrary"),
        cost_estimate=cost(1, 5.0),
        name="place_units",
    )(where, *parts)


def place_rows_kernel(where, *refs):
    parts, out_ref = refs[:-1], refs[-1]
    for j, part in enumerate(parts):
        out_ref[where[0] ^ j] = part[...].astype(F32)


def place_down_kernel(unit_pad, left, where, *refs):
    parts, out_ref = refs[:-1], refs[-1]
    _, keep, model = out_ref.shape
    n_units = parts[0].shape[1] - left
    rest = model - n_units
    step = unit_pad * rest // n_units
    for j, part in enumerate(parts):
        at = where[0] ^ j
        out_ref[at, :, :n_units] = part[:keep, left:].astype(F32)
        for b in range(n_units // rest):
            have = min(step, keep - b * step)
            if have > 0:
                value = part[unit_pad : unit_pad + have, left + b * rest : left + (b + 1) * rest]
                out_ref[at, b * step : b * step + have, n_units:] = value.astype(F32)


def place_rows(where, parts, shape, kernel=place_rows_kernel):
    return pl.pallas_call(
        kernel,
        grid_spec=pltpu.PrefetchScalarGridSpec(
            num_scalar_prefetch=1,
            grid=(1,),
            in_specs=[pl.BlockSpec(part.shape, lambda i, where: (0, 0)) for part in parts],
            out_specs=pl.BlockSpec((len(parts),) + shape, lambda i, where: (0, 0, 0)),
        ),
        out_shape=jax.ShapeDtypeStruct((len(parts),) + shape, F32),
        compiler_params=small_params("arbitrary"),
        cost_estimate=cost(1, 2.0),
        name="place_rows",
    )(where, *parts).reshape(-1, shape[1])


def place_down(where, parts, unit_pad, left, shape):
    return place_rows(where, parts, shape, partial(place_down_kernel, unit_pad, left))


def feed_kernel(n_seq, mid_ref, d_top_ref, w_ref, act_ref, d_gu_ref, down_ref, *d_mid_refs):
    n_units = act_ref.shape[1]
    model = mid_ref.shape[1]
    per = n_units // n_seq

    @pl.when(pl.program_id(0) == 0)
    def _():
        lines = w_ref[:, 2 * n_units :].reshape(n_seq, model // n_seq, n_units)
        rest = model - n_units
        step = per * rest // n_units
        for s in range(n_seq):
            down_ref[s * per : (s + 1) * per, :n_units] = lines[s, :per]
            for b in range(n_units // rest):
                at = s * per + b * step
                down_ref[at : at + step, n_units:] = lines[s, per:, b * rest : (b + 1) * rest]

    w_gate = w_ref[:, :n_units]
    w_up = w_ref[:, n_units : 2 * n_units]
    mid = mid_ref[...]
    gate = dot(mid, w_gate)
    up = dot(mid, w_up)
    d_act = dot(d_top_ref[...], down_ref[...], 1, 1)
    sig = jax.nn.sigmoid(gate)
    silu = gate * sig
    act_ref[...] = (silu * up).astype(BF)
    d_gate = (d_act * up * sig * (1.0 + gate * (1.0 - sig))).astype(BF)
    d_up = (d_act * silu).astype(BF)
    d_gu_ref[0] = d_gate
    d_gu_ref[1] = d_up
    d_mid = (dot(d_gate, w_gate, 1, 1) + dot(d_up, w_up, 1, 1)).astype(BF)
    for j, d_mid_ref in enumerate(d_mid_refs):

        @pl.when(pl.program_id(0) == j)
        def _(d_mid_ref=d_mid_ref):
            d_mid_ref[...] = d_mid


def feed(mid, d_top, weights, n_units, n_seq, n_parts):
    tokens, model = mid.shape
    size = tokens // n_parts
    rows = lambda n: pl.BlockSpec((size, n), lambda i: (i, 0))
    return pl.pallas_call(
        partial(feed_kernel, n_seq),
        grid=(n_parts,),
        in_specs=[rows(model), rows(model), whole(weights.shape)],
        out_specs=[
            rows(n_units), pl.BlockSpec((2, size, n_units), lambda i: (0, i, 0)),
            whole((n_units, model)),
        ] + [whole((size, model))] * n_parts,
        out_shape=[
            jax.ShapeDtypeStruct((tokens, n_units), BF),
            jax.ShapeDtypeStruct((2, tokens, n_units), BF),
            jax.ShapeDtypeStruct((n_units, model), BF),
        ] + [jax.ShapeDtypeStruct((size, model), BF)] * n_parts,
        compiler_params=params("arbitrary"),
        cost_estimate=cost(1, 14.0),
        name="feed",
    )(mid, d_top, weights)


def times_kernel(left_ref, right_ref, *out_refs):
    value = dot(left_ref[...], right_ref[...]).astype(BF)
    for j, out_ref in enumerate(out_refs):

        @pl.when(pl.program_id(0) == j)
        def _(out_ref=out_ref):
            out_ref[...] = value


def times(left, right, n_parts, earlier=()):
    tokens, inner = left.shape
    size = tokens // n_parts
    return launch(
        times_kernel,
        [pl.BlockSpec((size, inner), lambda i: (i, 0)), whole(right.shape)],
        earlier,
        grid=(n_parts,),
        out_specs=[whole((size, right.shape[1]))] * n_parts,
        out_shape=[jax.ShapeDtypeStruct((size, right.shape[1]), BF)] * n_parts,
        compiler_params=small_params("arbitrary"),
        cost_estimate=cost(1, 3.0),
        name="times",
    )(left, right)


def feed_grads(mid, d_gu, g_down, n_seq, earlier=(), size=256):
    tokens, model = mid.shape
    n_units = d_gu.shape[2]
    shard, unit_pad = model // n_seq, n_units // n_seq
    per = size // shard

    def body(mid_ref, d_gu_ref, g_down_ref, out_ref):
        mid = mid_ref[...]
        for half in range(2):
            value = dot(mid, d_gu_ref[half], 0, 0).astype(BF)
            out_ref[:, half * n_units : (half + 1) * n_units] = value
        rest = model - n_units
        step = unit_pad * rest // n_units
        for part in range(per):
            at, rows = part * shard, g_down_ref[part * unit_pad : (part + 1) * unit_pad]
            out_ref[at : at + unit_pad, 2 * n_units :] = rows[:, :n_units]
            for b in range(n_units // rest):
                to = 2 * n_units + b * rest
                out_ref[at + unit_pad : at + shard, to : to + rest] = rows[
                    b * step : (b + 1) * step, n_units:
                ]

    return launch(
        body,
        [
            pl.BlockSpec((tokens, size), lambda i: (0, i)), whole(d_gu.shape),
            pl.BlockSpec((per * unit_pad, model), lambda i: (i, 0)),
        ],
        earlier,
        grid=(model // size,),
        out_specs=pl.BlockSpec((size, 3 * n_units), lambda i: (i, 0)),
        out_shape=jax.ShapeDtypeStruct((model, 3 * n_units), BF),
        compiler_params=params("arbitrary"),
        cost_estimate=cost(1, 7.0),
        name="feed_grads",
    )(mid, d_gu, g_down)


def place_pieces_kernel(n_seq, where, *refs):
    parts, out_ref = refs[:-1], refs[-1]
    for j, part in enumerate(parts):
        for s in range(n_seq):
            out_ref[s, where[0] ^ j] = part[s]


def place_pieces(where, parts):
    n_seq, cut, width = parts[0].shape
    shape = (n_seq, len(parts), cut, width)
    return pl.pallas_call(
        partial(place_pieces_kernel, n_seq),
        grid_spec=pltpu.PrefetchScalarGridSpec(
            num_scalar_prefetch=1,
            grid=(1,),
            in_specs=[pl.BlockSpec(part.shape, lambda i, where: (0, 0, 0)) for part in parts],
            out_specs=pl.BlockSpec(shape, lambda i, where: (0, 0, 0, 0)),
        ),
        out_shape=jax.ShapeDtypeStruct(shape, BF),
        compiler_params=small_params("arbitrary"),
        cost_estimate=cost(1, 2.0),
        name="place_pieces",
    )(where, *parts).reshape(-1, width)


def middle_kernel(copies, gated_ref, x_ref, w_ref, gain_ref, residual_ref, normed_ref, gated_out_ref):
    n_heads = gated_ref.shape[0] // copies
    total = x_ref[0].astype(F32)
    for h in range(n_heads):
        part = gated_ref[h * copies, 0]
        gated_out_ref[0, :, h * LANES : (h + 1) * LANES] = part
        total = total + dot(part, w_ref[h * LANES : (h + 1) * LANES])
    scale = lax.rsqrt(jnp.mean(total * total, axis=-1, keepdims=True) + EPS_NORM)
    residual_ref[0] = total
    normed_ref[0] = (total * scale * gain_ref[...]).astype(BF)


def middle(gated, x, w_out, gain, copies):
    n_micro, n_tok, model = x.shape
    n_seq = gated.shape[0]
    rows = pl.BlockSpec((1, n_tok, model), lambda m: (m, 0, 0))
    made = lambda kind: jax.ShapeDtypeStruct((n_micro, n_tok, model), kind)
    return pl.pallas_call(
        partial(middle_kernel, copies),
        grid=(n_micro,),
        in_specs=[
            pl.BlockSpec((n_seq, 1, n_tok, LANES), lambda m: (0, m, 0, 0)),
            rows, whole(w_out.shape), whole((1, model)),
        ],
        out_specs=[rows] * 3,
        out_shape=[made(F32), made(BF), made(BF)],
        compiler_params=small_params("arbitrary"),
        cost_estimate=cost(1, 4.0),
        name="middle",
    )(gated, x, w_out, gain[None])


def input_back_kernel(d_ext_ref, w_ref, out_ref):
    value = dot(d_ext_ref[0], w_ref[...], 1, 1).astype(BF)
    per, _, n_tok, _ = out_ref.shape
    for part in range(per):
        out_ref[part, 0] = value[part * n_tok : (part + 1) * n_tok]


def input_back(d_ext, w_ext, n_tok, size=512):
    n_micro, length, wide = d_ext.shape
    model = w_ext.shape[0]
    per = size // n_tok
    return pl.pallas_call(
        input_back_kernel,
        grid=(n_micro, length // size),
        in_specs=[pl.BlockSpec((1, size, wide), lambda m, s: (m, s, 0)), whole(w_ext.shape)],
        out_specs=pl.BlockSpec((per, 1, n_tok, model), lambda m, s: (s, m, 0, 0)),
        out_shape=jax.ShapeDtypeStruct((length // n_tok, n_micro, n_tok, model), BF),
        compiler_params=params("arbitrary", "arbitrary"),
        cost_estimate=cost(1, 7.0),
        name="input_back",
    )(d_ext, w_ext)


def pick(stacked, at, axis=0):
    return lax.dynamic_index_in_dim(stacked, at, axis, False, allow_negative_indices=False)


def exchange(value, axis, bit):
    count = lax.axis_size(axis)
    return lax.ppermute(value, axis, [(i, i ^ bit) for i in range(count)])


def bits(axis):
    count = lax.axis_size(axis)
    return [1 << b for b in range(count.bit_length() - 1)]


def row_gather(value):
    parts = {0: value}
    for bit in reversed(bits("row")):
        parts.update({j ^ bit: exchange(part, "row", bit) for j, part in parts.items()})
    return [parts[j] for j in range(len(parts))]


def row_gather_steps(value):
    parts = {0: value}
    for bit in reversed(bits("row")):
        got = {j ^ bit: exchange(part, "row", bit) for j, part in parts.items()}
        parts.update(got)
        yield list(got.values())
    return [parts[j] for j in range(len(parts))]


def seq_scatter_steps(parts):
    mine = lax.axis_index("seq")
    for bit in reversed(bits("seq")):
        parts = parts.reshape((2, bit) + parts.shape[1:])
        side = (mine & bit) // bit
        got = exchange(pick(parts, 1 - side).astype(BF), "seq", bit)
        yield got
        parts = pick(parts, side).astype(F32) + got.astype(F32)
    return parts[0].astype(BF)


def finish(steps):
    try:
        while True:
            next(steps)
    except StopIteration as end:
        return end.value


def row_scatter(parts, earlier=()):
    parts = dict(enumerate(parts))
    for bit in bits("row"):
        got = {j ^ bit: exchange(parts[j].astype(BF), "row", bit) for j in parts if j & bit}
        if len(got) == 1:
            got = {j: fence(part, *earlier) for j, part in got.items()}
        parts = {j: parts[j].astype(F32) + part.astype(F32) for j, part in got.items()}
    return parts[0]


def ring():
    count, mine = lax.axis_size("seq"), lax.axis_index("seq")
    order = list(range(0, count, 2)) + list(range(1, count, 2))[::-1]
    half = mine >> 1
    place = jnp.where((mine & 1) == 0, half, count - 1 - half)

    def owner(k):
        at = (place + (k % count)) & (count - 1)
        return jnp.where(at < count // 2, 2 * at, 2 * count - 1 - 2 * at)

    ahead = [(order[i], order[(i + 1) % count]) for i in range(count)]
    behind = [(b, a) for a, b in ahead]
    return count, owner, ahead, behind


def ring_gather(value, earlier):
    count, owner, ahead, behind = ring()
    blocks = jnp.zeros((count,) + value.shape, value.dtype)
    put = lambda blocks, block, k: lax.dynamic_update_index_in_dim(
        blocks, block, owner(k), 0, allow_negative_indices=False
    )
    blocks = put(blocks, value, 0)
    there, back = value, value
    for k in range(1, count // 2):
        there = lax.ppermute(there, "seq", ahead)
        back = lax.ppermute(back, "seq", behind)
        if k in earlier:
            there = fence(there, *earlier[k])
        blocks = put(put(blocks, there, -k), back, k)
    cut = value.shape[1] // 2
    there = lax.ppermute(there[:, :cut], "seq", ahead)
    back = lax.ppermute(back[:, cut:], "seq", behind)
    return put(blocks, jnp.concatenate([there, back], axis=1), count // 2)


def rms_scale(values):
    return lax.rsqrt(jnp.mean(values * values, axis=-1, keepdims=True) + EPS_NORM)


def rms_back(grad_norm, values, inv_scale):
    return inv_scale * grad_norm - values * inv_scale**3 * jnp.mean(
        grad_norm * values, axis=-1, keepdims=True
    )


def matmul(spec, left, right, kind=F32):
    return jnp.einsum(spec, left, right, preferred_element_type=F32).astype(kind)


def local(
    tokens,
    cotangent,
    row_lengths,
    norm1_gain,
    w_in,
    w_router,
    conv_weight,
    a_log,
    dt_bias,
    head_gain,
    w_out,
    norm2_gain,
    w_gu,
    w_down,
):
    n_seq, n_row = lax.axis_size("seq"), lax.axis_size("row")
    seq, row = lax.axis_index("seq"), lax.axis_index("row")
    n_micro, _, n_tok, model = tokens.shape
    micros = list(range(n_micro))
    n_heads = a_log.shape[0]
    head_dim = head_gain.shape[0]
    n_taps, conv_width = conv_weight.shape
    slots = w_in.shape[1] // (n_heads * head_dim)
    width = conv_width // n_heads
    full = slots * head_dim
    length = n_tok * n_seq
    copies = n_seq // n_heads
    head = seq // copies
    gate_at = slots - 1

    def to_heads(value):
        return lax.all_to_all(jnp.repeat(value, copies, axis=0), "seq", 0, 0, tiled=True)

    def seq_parts(value):
        return lax.all_to_all(value, "seq", 0, 0, tiled=True)

    def from_heads(value):
        got = lax.all_to_all(value, "seq", 0, 0, tiled=True)
        return got if copies == 1 else got[::copies]

    def in_order(parts, axis):
        stacked = jnp.stack(parts)
        return jnp.concatenate([pick(stacked, row ^ j) for j in range(n_row)], axis=axis)

    where = jnp.stack([row, seq]).astype(jnp.int32)

    cut = w_in.shape[0] // n_row
    w_piece = pick(w_in.reshape(n_row, cut, slots, n_heads, head_dim), row)
    w_got = to_heads(w_piece.transpose(2, 0, 1, 3).reshape(n_heads, cut, full))
    w_head = place_pieces(where, row_gather(w_got))
    w_rt = pick(w_router.reshape(model, -1, n_heads), head, 2)
    n_rt = w_rt.shape[1]
    w_rt = jnp.pad(w_rt, ((0, 0), (0, LANES - n_rt)))
    w_ext = jnp.concatenate([w_head, w_rt], axis=1)
    taps = pick(conv_weight.reshape(n_taps, gate_at, n_heads, head_dim), head, 2)
    taps = jnp.pad(taps.reshape(n_taps, width), ((0, 8 - n_taps), (0, 0)))
    par = jnp.concatenate(
        [
            head_gain[None],
            jnp.broadcast_to(lax.dynamic_index_in_dim(a_log, head, 0), (1, LANES)),
            jnp.broadcast_to(lax.dynamic_index_in_dim(dt_bias, head, 0), (1, LANES)),
            jnp.zeros((5, LANES), F32),
        ]
    )
    position = seq * n_tok + jnp.arange(n_tok, dtype=jnp.int32)
    live = (position[None, :] < row_lengths[:, :1]).astype(F32)[:, :, None]
    d_top = (cotangent[:, 0].astype(F32) * live).reshape(-1, model)
    d_rows = jnp.concatenate(row_gather(d_top.astype(BF)), axis=0)
    x_own = tokens[:, 0].astype(F32).reshape(-1, model)

    x_all = ring_gather(
        tokens[:, 0], {n_seq // 4: [w_got], n_seq // 2 - 1: [w_ext, w_rt, taps, par, d_rows]}
    )

    out_cut = w_out.shape[0] // n_row
    out_piece = lax.dynamic_slice_in_dim(w_out, row * out_cut, out_cut, 0)
    shard = w_out.shape[0]
    hidden = w_gu.shape[1] // 2
    unit_cut = hidden // n_seq // n_row
    unit_pad = -(-unit_cut // 16) * 16
    n_units = unit_pad * n_seq
    gu_piece = pick(w_gu.reshape(shard, 2, n_seq, n_row, unit_cut), row, 3)
    gu_piece = jnp.pad(gu_piece, ((0, 0), (0, 0), (0, 0), (0, unit_pad - unit_cut)))
    down_piece = lax.dynamic_slice_in_dim(w_down, row * unit_cut, unit_cut, 0)
    down_piece = jnp.pad(down_piece, ((0, unit_pad - unit_cut), (0, 0)))
    beside = down_piece[:, n_units:]
    beside = beside.reshape(n_units // beside.shape[1], -1, beside.shape[1])
    beside = jnp.concatenate(list(beside), axis=1)
    down_piece = jnp.concatenate([down_piece[:, :n_units], beside])
    weights = jnp.concatenate([gu_piece.reshape(shard, -1), down_piece], axis=1)
    weights = fence(weights, x_all)
    weights_all = lax.all_gather(weights, "seq", axis=0, tiled=True)

    normed_in, projected, router = project(x_all, norm1_gain, w_head, w_rt, [d_rows, weights])
    out_piece = jnp.broadcast_to(out_piece[None], (n_seq,) + out_piece.shape)
    out_got = seq_parts(fence(out_piece, projected))
    prep = prepare(projected, router, taps, par, width)
    full_out = place_pieces(where, row_gather(fence(out_got, prep[0])))
    gated, *kept = scan_states(prep, router, projected, par, gate_at, n_tok)

    residual, normed_mid, gated = middle(
        seq_parts(gated), tokens[:, 0], full_out, norm2_gain, copies
    )
    residual, normed_mid, gated = (
        value.reshape(-1, model) for value in (residual, normed_mid, gated)
    )
    scale_mid = rms_scale(residual)
    mid_rows = jnp.concatenate(row_gather(normed_mid), axis=0)
    act, d_gu, down, *d_mid = feed(
        mid_rows, d_rows, weights_all, n_units, n_seq, n_row
    )
    g_down = matmul("tf,td->fd", act, d_rows, BF)
    g_feed = feed_grads(mid_rows, d_gu, g_down, n_seq)
    g_feed_sum = lax.psum_scatter(g_feed, "seq", scatter_dimension=0, tiled=True)
    d_mid = row_scatter(d_mid, [g_feed])

    def row_parts(value, axis):
        return [pick(value, row ^ j, axis) for j in range(n_row)]

    g_norm2 = jnp.sum(d_mid * residual * scale_mid, axis=0)
    d_residual = d_top + rms_back(d_mid * norm2_gain, residual, scale_mid)
    d_low = d_residual.astype(BF)
    d_sent = matmul("td,cd->tc", d_low, full_out, BF)
    d_gated = d_sent.reshape(n_micro, n_tok, n_heads, head_dim).transpose(2, 0, 1, 3)
    d_gated = to_heads(d_gated)

    mlp = times(act, down, n_row, [d_sent])
    out = residual + row_scatter(mlp)
    out = out.astype(BF).reshape(n_micro, 1, n_tok, model)
    g_out_full = matmul("tc,td->cd", fence(gated, d_sent), d_low)
    g_out = g_out_full
    g_out = row_scatter(row_parts(g_out.reshape(n_seq, n_row, out_cut, model), 1)).astype(BF)

    mixed, news, state = kept
    d_mixed, d_news, d_state, d_gate_pre, g_head = scan_back(
        prep, router, projected, par, gate_at, mixed, d_gated
    )
    d_ext, g_taps, g_par = mixer_grads(
        prep, router, projected, taps, par, width,
        news, state, d_mixed, d_news, d_state, d_gate_pre, [g_out, out],
    )
    if copies > 1:
        mine = (seq % copies == 0).astype(F32)
        d_ext = d_ext * mine.astype(BF)
        g_taps, g_par, g_head = g_taps * mine, g_par * mine, g_head * mine
    d_in_part = input_back(d_ext, w_ext, n_tok).reshape(-1, model)
    d_in = lax.psum_scatter(d_in_part, "seq", scatter_dimension=0, tiled=True)
    g_in, in_lines = input_grads(normed_in, d_ext, w_ext, norm1_gain, full, [d_in_part])
    fill = lambda value: jnp.pad(value, ((0, 0), (0, full - value.shape[1])))
    scalars = jnp.concatenate([g_head[:1], g_par[1:2], g_par[2:3]], axis=1)
    vectors = jnp.concatenate([in_lines[: n_rt + 1], g_norm2[None]]).reshape(-1, model // 2)
    small = jnp.concatenate([fill(vectors), fill(scalars), fill(g_taps[:n_taps])])
    n_vec = vectors.shape[0]
    lines = -(-small.shape[0] // n_row)
    small = jnp.pad(small, ((0, n_row * lines - small.shape[0]), (0, 0))).reshape(n_row, lines, full)

    parts = dict(enumerate(row_parts(g_in.reshape(n_seq, n_row, cut, full), 1)))
    smalls = dict(enumerate(row_parts(small, 0)))
    for bit in bits("row"):
        got = {j ^ bit: exchange(parts[j], "row", bit) for j in parts if j & bit}
        got_small = {j ^ bit: exchange(smalls[j], "row", bit) for j in smalls if j & bit}
        smalls = {j: smalls[j] + part for j, part in got_small.items()}
        if len(got) > 1:
            parts = {
                j: (parts[j].astype(F32) + part.astype(F32)).astype(BF) for j, part in got.items()
            }
    g_out_steps = seq_scatter_steps(fence(g_out, parts[0]))
    rows = cut + -(-2 * lines // 16) * 16
    g_in_got = seq_parts(pack(parts[0], got[0], smalls[0], rows, [next(g_out_steps)]))
    feed_steps = row_gather_steps(fence(g_feed_sum, got[0]))
    g_in_got = fence(g_in_got, *next(feed_steps), next(g_out_steps))
    in_steps = row_gather_steps(g_in_got)
    first_in = next(in_steps)
    g_out_sum = finish(g_out_steps)
    g_feed_all = finish(feed_steps)
    g_out_all = row_gather(g_out_sum)
    grad_out = place_rows(where, g_out_all, (out_cut, model))
    grad_down = place_down(where, g_feed_all, unit_pad, 2 * n_units, (unit_cut, model))
    grad_gu = place_units(where, g_feed_all, unit_cut, unit_pad, n_seq)
    g_in_all = finish(in_steps)
    grad_in, small = place_heads(where, g_in_all, n_heads, slots, cut, lines)
    d_in = fence(d_in, grad_in, grad_gu, grad_down, grad_out).astype(F32)
    grad_tokens = d_residual + rms_back(d_in * norm1_gain, x_own, rms_scale(x_own))
    grad_tokens = grad_tokens.reshape(n_micro, 1, n_tok, model)
    total = jnp.sum(small[:, 2 * n_rt : n_vec + 1], axis=0)
    norms = total[:4, : model // 2].reshape(2, model)
    heads = small[::copies]
    conv_sum = heads[:, n_vec + 1 : n_vec + 1 + n_taps, :width]
    conv_sum = conv_sum.reshape(n_heads, n_taps, gate_at, head_dim)
    conv_sum = conv_sum.transpose(1, 2, 0, 3).reshape(n_taps, conv_width)
    router_sum = heads[:, : 2 * n_rt, : model // 2].reshape(n_heads, n_rt, model)
    router_sum = router_sum.transpose(2, 1, 0).reshape(model, n_rt * n_heads)
    return (
        out,
        grad_tokens,
        norms[0],
        grad_in,
        router_sum,
        conv_sum,
        heads[:, n_vec, LANES + 2],
        heads[:, n_vec, 2 * LANES + 2],
        total[4, :head_dim],
        grad_out,
        norms[1],
        grad_gu,
        grad_down,
    )


def solution(mesh):
    by_rows = P("seq", None)
    by_tokens = P(None, "row", "seq", None)
    return jax.shard_map(
        local,
        mesh=mesh,
        in_specs=(
            by_tokens, by_tokens, P(None, "row"), P(), by_rows, P(), P(), P(), P(), P(),
            by_rows, P(), by_rows, by_rows,
        ),
        out_specs=(
            by_tokens, by_tokens, P(), by_rows, P(), P(), P(), P(), P(),
            by_rows, P(), by_rows, by_rows,
        ),
        check_vma=False,
    )
```

```python
from functools import partial

import jax
import jax.numpy as jnp
from jax import lax
from jax.experimental import pallas as pl
from jax.experimental.pallas import tpu as pltpu
from jax.sharding import PartitionSpec as P

BF = jnp.bfloat16
F32 = jnp.float32
EPS_NORM = 1e-05
EPS_UNIT = 1e-06
CH = 64
ST = 128
HALO = 16
LANES = 128
VMEM_BYTES = 60 * 1024 * 1024
SMALL_BYTES = 50 * 1024 * 1024


def halves(value):
    high = value.astype(BF)
    return (high, (value - high.astype(F32)).astype(BF))


def dot(left, right, over_left=1, over_right=0):
    return lax.dot_general(
        left, right, (((over_left,), (over_right,)), ((), ())), preferred_element_type=F32
    )


def mm(left, right, over_left=1, over_right=0):
    left = left if isinstance(left, tuple) else (left,)
    right = right if isinstance(right, tuple) else (right,)
    total = dot(left[0], right[0], over_left, over_right)
    if len(right) > 1:
        total = total + dot(left[0], right[1], over_left, over_right)
    if len(left) > 1:
        total = total + dot(left[1], right[0], over_left, over_right)
    return total


def exact_sum(ones, value):
    high = value.astype(BF)
    rest = value - high.astype(F32)
    mid = rest.astype(BF)
    low = (rest - mid.astype(F32)).astype(BF)
    return dot(ones, high) + dot(ones, mid) + dot(ones, low)


def step_orders():
    row = lax.broadcasted_iota(jnp.int32, (ST, ST), 0)
    col = lax.broadcasted_iota(jnp.int32, (ST, ST), 1)
    order = lambda i: 2 * (i & (CH - 1)) + (i >> 6)
    return order(row), order(col)


def sees():
    row = lax.broadcasted_iota(jnp.int32, (CH, ST), 0)
    col = lax.broadcasted_iota(jnp.int32, (CH, ST), 1)
    return (col & (CH - 1)) <= row


def twice(value):
    return jnp.concatenate([value, value], axis=0)


def log_decays(router, par):
    lane = lax.broadcasted_iota(jnp.int32, (CH, LANES), 1)
    pre = router + par[2:3]
    soft = jnp.maximum(pre, 0.0) + jnp.log1p(jnp.exp(-jnp.abs(pre)))
    decay = -jnp.exp(par[1:2]) * soft
    row = lax.broadcasted_iota(jnp.int32, (CH, CH), 0)
    col = lax.broadcasted_iota(jnp.int32, (CH, CH), 1)
    below = jnp.where(col <= row, 1.0, 0.0).astype(BF)
    total = exact_sum(below, jnp.where(lane == 2, decay, 0.0))
    return decay, total


def gate_columns(router, par):
    strength = jax.nn.sigmoid(router)
    decay, total = log_decays(router, par)
    beta = jnp.concatenate([strength[:, 0:1], strength[:, 1:2]], axis=0)
    doubled = twice(total)
    g_col = doubled[:, 2:3]
    g_row = doubled.T[2:3, :]
    g_last = total[CH - 1 : CH, 2:3]
    return beta, g_col, g_row, g_last, decay


def seen_decay(g_col, g_row, visible):
    return jnp.where(visible, jnp.exp(jnp.where(visible, g_col[:CH] - g_row, 0.0)), 0.0)


def unit(value):
    scale = lax.rsqrt(jnp.sum(value * value, axis=-1, keepdims=True) + EPS_UNIT)
    return value * scale, scale


def taps_sum(window, weight, start):
    total = weight[0:1] * window[pl.ds(start + 5, CH), :]
    for tap in range(1, 4):
        total = total + weight[tap : tap + 1] * window[pl.ds(start + 5 + tap, CH), :]
    return total


def fill_window(window, proj_ref, halo_ref, is_first):
    width = window.shape[1]
    edge = halo_ref[0, :, :width].astype(F32)[HALO - 8 :]
    window[0:8, :] = jnp.where(is_first, 0.0, edge)
    window[8:, :] = proj_ref[0, :, :width].astype(F32)


def prep_kernel(
    count, proj_ref, halo_ref, router_ref, taps_ref, par_ref,
    solve_ref, wmat_ref, umat_ref, seen_ref, q_ref, k_ref, window,
):
    fill_window(window, proj_ref, halo_ref, pl.program_id(1) == 0)
    weight = taps_ref[...]
    par = par_ref[...]
    o_row, o_col = step_orders()
    strict = o_row > o_col
    eye = jnp.where(o_row == o_col, 1.0, 0.0)
    visible = sees()
    many = range(count)
    lower, rights = [], []
    for n in many:
        conv = taps_sum(window, weight, n * CH)
        act = conv * jax.nn.sigmoid(conv)
        q = unit(act[:, 0:128])[0].astype(BF)
        k = jnp.concatenate(
            [unit(act[:, 128:256])[0], unit(act[:, 256:384])[0]], axis=0
        ).astype(BF)
        v = jnp.concatenate([act[:, 384:512], act[:, 512:640]], axis=0).astype(BF)
        beta, g_col, g_row, _, _ = gate_columns(
            router_ref[0, n * CH : (n + 1) * CH, :], par
        )
        gaps = seen_decay(g_col, g_row, visible)
        lower.append(jnp.where(strict, beta * twice(gaps) * dot(k, k, 1, 1), 0.0))
        kf = k.astype(F32)
        rights.append(
            jnp.concatenate([beta * jnp.exp(g_col) * kf, beta * v.astype(F32)], axis=1)
        )
        seen_ref[0, n] = gaps * dot(q, k, 1, 1)
        q_ref[0, n] = q
        k_ref[0, n] = k
    inverse = [eye - jnp.where((o_row >> 1) == (o_col >> 1), part, 0.0) for part in lower]
    for level in range(1, 7):
        at = ((o_row >> level) ^ (o_col >> level)) == 1
        parts = [halves(jnp.where(at, part, 0.0)) for part in lower]
        known = [halves(value) for value in inverse]
        inner = [halves(mm(parts[n], known[n])) for n in many]
        inverse = [inverse[n] - mm(known[n], inner[n]) for n in many]
    for n in many:
        solve_ref[0, n] = inverse[n]
        both = mm(halves(inverse[n]), halves(rights[n]))
        wmat_ref[0, n] = both[:, :128]
        umat_ref[0, n] = both[:, 128:]


def head_norm(mixed):
    return lax.rsqrt(jnp.mean(mixed * mixed, axis=-1, keepdims=True) + EPS_NORM)


def scan_kernel(
    n_micro, count, wmat_ref, umat_ref, seen_ref, q_ref, k_ref, router_ref, gate_ref, par_ref,
    out_ref, mixed_ref, news_ref, state_ref, state,
):
    @pl.when(pl.program_id(0) == 0)
    def _():
        state[...] = jnp.zeros_like(state)

    par = par_ref[...]
    now = [state[m] for m in range(n_micro)]
    for n in range(count):
        rows = slice(n * CH, (n + 1) * CH)
        for m in range(n_micro):
            _, g_col, _, g_last, _ = gate_columns(router_ref[m, rows, :], par)
            held = halves(now[m])
            state_ref[m, n] = now[m]
            news = umat_ref[m, n] - mm(halves(wmat_ref[m, n]), held)
            news_ref[m, n] = news
            news_h = halves(news)
            ends = halves(jnp.exp(g_last - g_col) * k_ref[m, n].astype(F32))
            now[m] = jnp.exp(g_last) * now[m] + mm(ends, news_h, 0, 0)
            mixed = jnp.exp(g_col[:CH]) * mm(q_ref[m, n], held) + mm(halves(seen_ref[m, n]), news_h)
            mixed_ref[m, n] = mixed
            gate = gate_ref[m, rows, :].astype(F32)
            tok = out_ref.shape[2]
            at = slice(n * CH % tok, n * CH % tok + CH)
            out_ref[n * CH // tok, m, at, :] = (
                mixed * head_norm(mixed) * par[0:1] * (gate * jax.nn.sigmoid(gate))
            ).astype(BF)
    for m in range(n_micro):
        state[m] = now[m]


def scan_back_kernel(
    n_micro, count, wmat_ref, seen_ref, q_ref, k_ref, router_ref, gate_ref, par_ref, mixed_ref, d_out_ref,
    d_mixed_ref, d_news_ref, d_state_ref, d_gate_ref, gain_ref, state,
):
    @pl.when(pl.program_id(0) == 0)
    def _():
        state[...] = jnp.zeros_like(state)
        gain_ref[...] = jnp.zeros_like(gain_ref)

    par = par_ref[...]
    now = [state[m] for m in range(n_micro)]
    gain = jnp.zeros((1, LANES), F32)
    for n in reversed(range(count)):
        rows = slice(n * CH, (n + 1) * CH)
        for m in range(n_micro):
            _, g_col, _, g_last, _ = gate_columns(router_ref[m, rows, :], par)
            mixed = mixed_ref[m, n]
            gate = gate_ref[m, rows, :].astype(F32)
            tok = d_out_ref.shape[2]
            at = slice(n * CH % tok, n * CH % tok + CH)
            d_out = d_out_ref[n * CH // tok, m, at, :].astype(F32)
            scale = head_norm(mixed)
            normed = mixed * scale
            sig = jax.nn.sigmoid(gate)
            silu = gate * sig
            gain = gain + jnp.sum(d_out * normed * silu, axis=0, keepdims=True)
            d_gate = d_out * normed * par[0:1] * (sig * (1.0 + gate * (1.0 - sig)))
            d_gate_ref[m, rows, :] = d_gate.astype(BF)
            d_normed = d_out * par[0:1] * silu
            d_mixed = scale * d_normed - mixed * scale**3 * jnp.mean(
                d_normed * mixed, axis=-1, keepdims=True
            )
            d_mixed_ref[m, n] = d_mixed
            d_mixed_h = halves(d_mixed)
            d_state_ref[m, n] = now[m]
            ends = halves(jnp.exp(g_last - g_col) * k_ref[m, n].astype(F32))
            d_news = mm(halves(seen_ref[m, n]), d_mixed_h, 0, 0) + mm(ends, halves(now[m]))
            d_news_ref[m, n] = d_news
            q_eff = halves(jnp.exp(g_col[:CH]) * q_ref[m, n].astype(F32))
            now[m] = (
                jnp.exp(g_last) * now[m]
                + mm(q_eff, d_mixed_h, 0, 0)
                - mm(halves(wmat_ref[m, n]), halves(d_news), 0, 0)
            )
    gain_ref[0:1, :] += gain
    for m in range(n_micro):
        state[m] = now[m]


def in_step(chains):
    while chains:
        chains = [chain for chain in chains if next(chain, chain) is not chain]


def unit_back(grad, value, scale):
    return scale * grad - value * scale**3 * jnp.sum(grad * value, axis=-1, keepdims=True)


def grads_kernel(
    count, proj_ref, halo_ref, router_ref, taps_ref, par_ref, solve_ref, seen_ref, news_ref, state_ref,
    d_mixed_ref, d_news_ref, d_state_ref, d_gate_ref,
    d_ext_ref, g_taps_ref, g_par_ref, window, d_window,
):
    step = pl.program_id(1)
    size = count * CH
    fill_window(window, proj_ref, halo_ref, step == pl.num_programs(1) - 1)

    @pl.when((step == 0) & (pl.program_id(0) == 0))
    def _():
        g_taps_ref[...] = jnp.zeros_like(g_taps_ref)
        g_par_ref[...] = jnp.zeros_like(g_par_ref)

    @pl.when(step == 0)
    def _():
        d_window[size:, :] = jnp.zeros((8, d_window.shape[1]), F32)

    @pl.when(step > 0)
    def _():
        d_window[size:, :] = d_window[0:8, :]

    weight = taps_ref[...]
    par = par_ref[...]
    o_row, o_col = step_orders()
    strict = o_row > o_col
    visible = sees()
    row = lax.broadcasted_iota(jnp.int32, (CH, CH), 0)
    col = lax.broadcasted_iota(jnp.int32, (CH, CH), 1)
    above = jnp.where(col >= row, 1.0, 0.0).astype(BF)
    lane = lax.broadcasted_iota(jnp.int32, (CH, LANES), 1)
    last = lax.broadcasted_iota(jnp.int32, (CH, LANES), 0) == CH - 1
    sums = [jnp.zeros((1, LANES), F32), jnp.zeros((1, LANES), F32)]

    def one(n):
        rows = slice(n * CH, (n + 1) * CH)
        conv = taps_sum(window, weight, n * CH)
        sig = jax.nn.sigmoid(conv)
        act = conv * sig
        qn, q_scale = unit(act[:, 0:128])
        k0n, k0_scale = unit(act[:, 128:256])
        k1n, k1_scale = unit(act[:, 256:384])
        q = qn.astype(BF)
        k = jnp.concatenate([k0n, k1n], axis=0).astype(BF)
        kf, qf = k.astype(F32), q.astype(F32)
        router = router_ref[0, rows, :]
        yield
        d_right = mm(halves(solve_ref[0, n]), halves(d_news_ref[0, n]), 0, 0)
        beta, g_col, g_row, g_last, decay = gate_columns(router, par)
        gaps = seen_decay(g_col, g_row, visible)
        yield
        ratio = jnp.where(strict, twice(gaps), 0.0)
        grown = jnp.exp(g_col)
        left = jnp.exp(g_last - g_col)
        gram = dot(k, k, 1, 1)
        state = state_ref[0, n]
        state_h = halves(state)
        news = news_ref[0, n]
        news_h = halves(news)
        d_mixed_h = halves(d_mixed_ref[0, n])
        d_state = d_state_ref[0, n]
        d_seen = mm(d_mixed_h, news_h, 1, 1)
        yield
        d_q_grown = grown[:CH] * mm(d_mixed_h, state_h, 1, 1)
        d_right_h = halves(d_right)
        d_lower = jnp.where(strict, -mm(d_right_h, news_h, 1, 1), 0.0)
        yield
        d_ends = left * mm(news_h, halves(d_state), 1, 1)
        d_pre = (1.0 - beta) * jnp.sum(d_right * news, axis=-1, keepdims=True)
        d_v = beta * d_right
        yield
        d_grown_k = -beta * mm(d_right_h, state_h, 1, 1)
        d_scores = halves(d_seen * gaps)
        seen_both = d_seen * seen_ref[0, n]
        yield
        d_q = d_q_grown + mm(d_scores, k)
        d_k = grown * d_grown_k
        d_gram = beta * ratio * d_lower
        both = d_gram * gram
        d_g = jnp.sum(both, axis=-1, keepdims=True) + jnp.sum(d_k * kf, axis=-1, keepdims=True)
        d_g_row = -jnp.sum(both, axis=0, keepdims=True)
        yield
        d_k = d_k + mm(halves(d_gram + d_gram.T), k) + d_ends
        d_g_q = jnp.sum(seen_both + d_q_grown * qf, axis=-1, keepdims=True)
        yield
        d_k = d_k + mm(d_scores, q, 0, 0)
        d_g_row = d_g_row - jnp.sum(seen_both, axis=0, keepdims=True)
        ends_sum = jnp.sum(d_ends * kf, axis=-1, keepdims=True)
        d_g = d_g - ends_sum
        d_last = jnp.sum(ends_sum, axis=0, keepdims=True) + jnp.exp(g_last) * jnp.sum(
            jnp.sum(d_state * state, axis=-1, keepdims=True), axis=0, keepdims=True
        )
        d_g_rows = jnp.broadcast_to(d_g_row, (LANES, ST)).T
        d_g_tok = d_g_q + d_g[:CH] + d_g[CH:] + d_g_rows[:CH] + d_g_rows[CH:]
        d_g_tok = d_g_tok + jnp.where(last, d_last, 0.0)
        yield
        d_decay = exact_sum(above, d_g_tok)
        yield
        d_soft = -jnp.exp(par[1:2]) * jax.nn.sigmoid(router + par[2:3]) * d_decay
        d_router = jnp.where(
            lane == 0,
            d_pre[:CH],
            jnp.where(lane == 1, d_pre[CH:], jnp.where(lane == 2, d_soft, 0.0)),
        )
        width = window.shape[1]
        d_ext_ref[0, rows, width : width + LANES] = d_gate_ref[0, rows, :]
        d_ext_ref[0, rows, width + LANES :] = d_router.astype(BF)
        sums[0] += jnp.sum(jnp.where(lane == 2, d_decay * decay, 0.0), axis=0, keepdims=True)
        sums[1] += jnp.sum(jnp.where(lane == 2, d_soft, 0.0), axis=0, keepdims=True)
        d_act = jnp.concatenate(
            [
                unit_back(d_q, act[:, 0:128], q_scale),
                unit_back(d_k[:CH], act[:, 128:256], k0_scale),
                unit_back(d_k[CH:], act[:, 256:384], k1_scale),
                d_v[:CH],
                d_v[CH:],
            ],
            axis=1,
        )
        d_window[rows, :] = d_act * (sig * (1.0 + conv * (1.0 - sig)))

    in_step([one(n) for n in range(count)])
    g_alog, g_dt = sums
    g_par_ref[1:2, :] += g_alog
    g_par_ref[2:3, :] += g_dt
    for n in range(count):
        start = n * CH
        here = d_window[pl.ds(start, CH), :]
        total = weight[3:4] * here
        for tap in range(3):
            total = total + weight[tap : tap + 1] * d_window[pl.ds(start + 3 - tap, CH), :]
        d_ext_ref[0, pl.ds(start, CH), : total.shape[1]] = total.astype(BF)
        for tap in range(4):
            g_taps_ref[tap : tap + 1, :] += jnp.sum(
                here * window[pl.ds(start + 5 + tap, CH), :], axis=0, keepdims=True
            )


def params(*semantics):
    return pltpu.CompilerParams(dimension_semantics=semantics, vmem_limit_bytes=VMEM_BYTES)


def small_params(*semantics):
    return pltpu.CompilerParams(dimension_semantics=semantics, vmem_limit_bytes=SMALL_BYTES)


def cost(chunks, per_chunk):
    return pl.CostEstimate(
        flops=int(chunks * per_chunk * 1.1e9), transcendentals=0, bytes_accessed=1 << 20
    )


def launch(kernel, in_specs, earlier, **options):
    n_in = len(in_specs)

    def body(*refs):
        kernel(*refs[:n_in], *refs[n_in + len(earlier) :])

    specs = list(in_specs) + [pl.BlockSpec(memory_space=pl.ANY)] * len(earlier)
    called = pl.pallas_call(body, in_specs=specs, **options)
    return lambda *operands: called(*operands, *earlier)


def fence(value, *earlier):
    earlier = [other for other in earlier if other is not None]
    if not earlier:
        return value
    anywhere = pl.BlockSpec(memory_space=pl.ANY)
    return pl.pallas_call(
        lambda *refs: None,
        in_specs=[anywhere] * (1 + len(earlier)),
        out_specs=anywhere,
        out_shape=jax.ShapeDtypeStruct(value.shape, value.dtype),
        input_output_aliases={0: 0},
        name="fence",
    )(value, *earlier)


def whole(shape):
    return pl.BlockSpec(shape, lambda *_: (0,) * len(shape))


def prepare(projected, router, taps, par, width, earlier=(), count=8):
    n_micro, length, full = projected.shape
    steps = length // (count * CH)
    chunks = length // CH
    size = count * CH
    per = lambda *tail: pl.BlockSpec((1, count) + tail, lambda m, i: (m, i, 0, 0))
    made = lambda kind, *tail: jax.ShapeDtypeStruct((n_micro, chunks) + tail, kind)
    return launch(
        partial(prep_kernel, count),
        [
            pl.BlockSpec((1, size, full), lambda m, i: (m, i, 0)),
            pl.BlockSpec((1, HALO, full), lambda m, i: (m, jnp.maximum(i * (size // HALO) - 1, 0), 0)),
            pl.BlockSpec((1, size, LANES), lambda m, i: (m, i, 0)),
            whole(taps.shape),
            whole(par.shape),
        ],
        earlier,
        grid=(n_micro, steps),
        out_specs=[per(ST, ST), per(ST, 128), per(ST, 128), per(CH, ST), per(CH, 128), per(ST, 128)],
        out_shape=[
            made(F32, ST, ST), made(F32, ST, 128), made(F32, ST, 128), made(F32, CH, ST),
            made(BF, CH, 128), made(BF, ST, 128),
        ],
        scratch_shapes=[pltpu.VMEM((size + 8, width), F32)],
        compiler_params=params("arbitrary", "arbitrary"),
        cost_estimate=cost(n_micro * chunks, 0.75),
        name="mixer_prepare",
    )(projected, projected, router, taps, par)


def scan_states(prep, router, projected, par, gate_at, n_tok, earlier=(), count=4):
    _, wmat, umat, seen, q, k = prep
    n_micro, chunks = wmat.shape[:2]
    length = chunks * CH
    size = count * CH
    per = lambda *tail: pl.BlockSpec((n_micro, count) + tail, lambda i: (0, i, 0, 0))
    made = lambda kind, *tail: jax.ShapeDtypeStruct((n_micro, chunks) + tail, kind)
    return launch(
        partial(scan_kernel, n_micro, count),
        [
            per(ST, 128), per(ST, 128), per(CH, ST), per(CH, 128), per(ST, 128),
            pl.BlockSpec((n_micro, size, LANES), lambda i: (0, i, 0)),
            pl.BlockSpec((n_micro, size, 128), lambda i: (0, i, gate_at)),
            whole(par.shape),
        ],
        earlier,
        grid=(chunks // count,),
        out_specs=[
            pl.BlockSpec((size // n_tok, n_micro, n_tok, 128), lambda i: (i, 0, 0, 0)),
            per(CH, 128), per(ST, 128), per(128, 128),
        ],
        out_shape=[
            jax.ShapeDtypeStruct((length // n_tok, n_micro, n_tok, 128), BF),
            made(F32, CH, 128), made(F32, ST, 128), made(F32, 128, 128),
        ],
        scratch_shapes=[pltpu.VMEM((n_micro, 128, 128), F32)],
        compiler_params=params("arbitrary"),
        cost_estimate=cost(n_micro * chunks, 0.5),
        name="mixer_scan",
    )(wmat, umat, seen, q, k, router, projected, par)


def scan_back(prep, router, projected, par, gate_at, mixed, d_out, earlier=(), count=4):
    _, wmat, _, seen, q, k = prep
    n_micro, chunks = wmat.shape[:2]
    length = chunks * CH
    size = count * CH
    blocks = chunks // count
    n_tok = d_out.shape[2]
    per = lambda *tail: pl.BlockSpec((n_micro, count) + tail, lambda i: (0, blocks - 1 - i, 0, 0))
    made = lambda kind, *tail: jax.ShapeDtypeStruct((n_micro, chunks) + tail, kind)
    return launch(
        partial(scan_back_kernel, n_micro, count),
        [
            per(ST, 128), per(CH, ST), per(CH, 128), per(ST, 128),
            pl.BlockSpec((n_micro, size, LANES), lambda i: (0, blocks - 1 - i, 0)),
            pl.BlockSpec((n_micro, size, 128), lambda i: (0, blocks - 1 - i, gate_at)),
            whole(par.shape),
            per(CH, 128),
            pl.BlockSpec(
                (size // n_tok, n_micro, n_tok, 128), lambda i: (blocks - 1 - i, 0, 0, 0)
            ),
        ],
        earlier,
        grid=(blocks,),
        out_specs=[
            per(CH, 128), per(ST, 128), per(128, 128),
            pl.BlockSpec((n_micro, size, 128), lambda i: (0, blocks - 1 - i, 0)),
            whole((8, LANES)),
        ],
        out_shape=[
            made(F32, CH, 128), made(F32, ST, 128), made(F32, 128, 128),
            jax.ShapeDtypeStruct((n_micro, length, 128), BF),
            jax.ShapeDtypeStruct((8, LANES), F32),
        ],
        scratch_shapes=[pltpu.VMEM((n_micro, 128, 128), F32)],
        compiler_params=params("arbitrary"),
        cost_estimate=cost(n_micro * chunks, 0.4),
        name="mixer_scan_back",
    )(wmat, seen, q, k, router, projected, par, mixed, d_out)


def mixer_grads(
    prep, router, projected, taps, par, width, news, state, d_mixed, d_news, d_state, d_gate,
    earlier=(), count=4,
):
    solve, _, _, seen, _, _ = prep
    n_micro, chunks = solve.shape[:2]
    length = chunks * CH
    size = count * CH
    blocks = chunks // count
    full = projected.shape[2]
    per = lambda *tail: pl.BlockSpec((1, count) + tail, lambda m, i: (m, blocks - 1 - i, 0, 0))
    rows = lambda n: pl.BlockSpec((1, size, n), lambda m, i: (m, blocks - 1 - i, 0))
    before = lambda m, i: (m, jnp.maximum((blocks - 1 - i) * (size // HALO) - 1, 0), 0)
    return launch(
        partial(grads_kernel, count),
        [
            rows(full), pl.BlockSpec((1, HALO, full), before), rows(LANES),
            whole(taps.shape), whole(par.shape),
            per(ST, ST), per(CH, ST), per(ST, 128), per(128, 128),
            per(CH, 128), per(ST, 128), per(128, 128), rows(LANES),
        ],
        earlier,
        grid=(n_micro, blocks),
        out_specs=[rows(width + 2 * LANES), whole((8, width)), whole((8, LANES))],
        out_shape=[
            jax.ShapeDtypeStruct((n_micro, length, width + 2 * LANES), BF),
            jax.ShapeDtypeStruct((8, width), F32),
            jax.ShapeDtypeStruct((8, LANES), F32),
        ],
        scratch_shapes=[pltpu.VMEM((size + 8, width), F32), pltpu.VMEM((size + 8, width), F32)],
        compiler_params=params("arbitrary", "arbitrary"),
        cost_estimate=cost(n_micro * chunks, 1.0),
        name="mixer_grads",
    )(projected, projected, router, taps, par, solve, seen, news, state, d_mixed, d_news, d_state, d_gate)


def project_kernel(x_ref, gain_ref, weight_ref, router_weight_ref, normed_ref, out_ref, router_ref):
    per, _, n_tok, model = x_ref.shape
    x = x_ref[:, 0].reshape(per * n_tok, model).astype(F32)
    scale = lax.rsqrt(jnp.mean(x * x, axis=-1, keepdims=True) + EPS_NORM)
    normed = (x * scale * gain_ref[...]).astype(BF)
    normed_ref[0] = normed
    out_ref[0] = dot(normed, weight_ref[...]).astype(BF)
    router_ref[0] = dot(normed, router_weight_ref[...])


def project(x, gain, weight, router_weight, earlier=(), size=512):
    n_seq, n_micro, n_tok, model = x.shape
    length = n_seq * n_tok
    full = weight.shape[1]
    blocks = pl.BlockSpec((size // n_tok, 1, n_tok, model), lambda m, i: (i, m, 0, 0))
    rows = lambda n: pl.BlockSpec((1, size, n), lambda m, i: (m, i, 0))
    return launch(
        project_kernel,
        [blocks, whole((1, model)), whole(weight.shape), whole(router_weight.shape)],
        earlier,
        grid=(n_micro, length // size),
        out_specs=[rows(model), rows(full), rows(LANES)],
        out_shape=[
            jax.ShapeDtypeStruct((n_micro, length, model), BF),
            jax.ShapeDtypeStruct((n_micro, length, full), BF),
            jax.ShapeDtypeStruct((n_micro, length, LANES), F32),
        ],
        compiler_params=params("arbitrary", "arbitrary"),
        cost_estimate=cost(n_micro * length // CH, 0.35),
        name="project",
    )(x, gain[None], weight, router_weight)


def ring_add_kernel(table, ahead_ref, behind_ref, up_ref, low_ref, up_out, low_out):
    up_out[...] = (ahead_ref[...].astype(F32) + up_ref[0, 0].astype(F32)).astype(up_out.dtype)
    low_out[...] = (behind_ref[...].astype(F32) + low_ref[0, 0].astype(F32)).astype(low_out.dtype)


def ring_add(table, step, ahead, behind, parts, kind, earlier=()):
    rows, model = ahead.shape
    one = pl.BlockSpec((rows, model), lambda i, table: (0, 0))
    part = lambda m: pl.BlockSpec((1, 1, rows, model), lambda i, table: (m, table[2 * step + m], 0, 0))
    made = jax.ShapeDtypeStruct((rows, model), kind)
    n_in = 5

    def body(*refs):
        ring_add_kernel(*refs[:n_in], *refs[n_in + len(earlier) :])

    return pl.pallas_call(
        body,
        grid_spec=pltpu.PrefetchScalarGridSpec(
            num_scalar_prefetch=1,
            grid=(1,),
            in_specs=[one, one, part(0), part(1)] + [pl.BlockSpec(memory_space=pl.ANY)] * len(earlier),
            out_specs=[one, one],
        ),
        out_shape=[made, made],
        compiler_params=small_params("arbitrary"),
        cost_estimate=cost(1, 1.0),
        name="ring_add",
    )(table, ahead, behind, parts, parts, *earlier)


def input_grads_kernel(normed_ref, d_ext_ref, w_ext_ref, gain_ref, out_ref, lines_ref):
    total = dot(normed_ref[0], d_ext_ref[0], 0, 0)
    for m in range(1, normed_ref.shape[0]):
        total = total + dot(normed_ref[m], d_ext_ref[m], 0, 0)
    full = out_ref.shape[1]
    out_ref[...] = total[:, :full].astype(BF)
    norm = jnp.sum(total * w_ext_ref[...].astype(F32), axis=1, keepdims=True)
    lane = lax.broadcasted_iota(jnp.int32, (total.shape[0], LANES), 1)
    tail = jnp.where(lane == 3, norm, total[:, full:])
    lines = tail.T[:8]
    row = lax.broadcasted_iota(jnp.int32, lines.shape, 0)
    lines_ref[...] = jnp.where(row == 3, lines / gain_ref[...], lines)


def input_grads(normed, d_ext, w_ext, gain, full, earlier=(), size=256):
    n_micro, length, model = normed.shape
    wide = d_ext.shape[2]
    return launch(
        input_grads_kernel,
        [
            pl.BlockSpec((n_micro, length, size), lambda i: (0, 0, i)),
            whole(d_ext.shape),
            pl.BlockSpec((size, wide), lambda i: (i, 0)),
            pl.BlockSpec((1, size), lambda i: (0, i)),
        ],
        earlier,
        grid=(model // size,),
        out_specs=[
            pl.BlockSpec((size, full), lambda i: (i, 0)),
            pl.BlockSpec((8, size), lambda i: (0, i)),
        ],
        out_shape=[
            jax.ShapeDtypeStruct((model, full), BF),
            jax.ShapeDtypeStruct((8, model), F32),
        ],
        compiler_params=params("arbitrary"),
        cost_estimate=cost(1, 7.0),
        name="input_grads",
    )(normed, d_ext, w_ext, gain[None])


def place_heads_kernel(n_heads, copies, slots, cut, lines, where, *refs):
    parts, out_ref, small_ref = refs[:-2], refs[-2], refs[-1]
    for j, part in enumerate(parts):
        at = where[0] ^ j
        for slot in range(slots):
            for h in range(n_heads):
                to = (slot * n_heads + h) * LANES
                value = part[h * copies, :cut, slot * LANES : (slot + 1) * LANES]
                out_ref[at, :, to : to + LANES] = value.astype(F32)
        for s in range(part.shape[0]):
            high = part[s, cut : cut + lines].astype(F32)
            low = part[s, cut + lines : cut + 2 * lines].astype(F32)
            for r in range(len(parts)):

                @pl.when(at == r)
                def _(s=s, r=r, value=high + low):
                    small_ref[s, r * lines : (r + 1) * lines] = value


def place_heads(where, parts, n_heads, slots, cut, lines):
    n_seq, rows, full = parts[0].shape
    n_parts = len(parts)
    shape = (n_parts, cut, full * n_heads)
    small = (n_seq, n_parts * lines, full)
    grad, values = pl.pallas_call(
        partial(place_heads_kernel, n_heads, n_seq // n_heads, slots, cut, lines),
        grid_spec=pltpu.PrefetchScalarGridSpec(
            num_scalar_prefetch=1,
            grid=(1,),
            in_specs=[pl.BlockSpec(part.shape, lambda i, where: (0, 0, 0)) for part in parts],
            out_specs=[
                pl.BlockSpec(shape, lambda i, where: (0, 0, 0)),
                pl.BlockSpec(small, lambda i, where: (0, 0, 0)),
            ],
        ),
        out_shape=[jax.ShapeDtypeStruct(shape, F32), jax.ShapeDtypeStruct(small, F32)],
        compiler_params=small_params("arbitrary"),
        cost_estimate=cost(1, 3.0),
        name="place_heads",
    )(where, *parts)
    return grad.reshape(-1, full * n_heads), values


def pack_kernel(lines, own_ref, got_ref, small_ref, out_ref):
    n_seq, cut, full = own_ref.shape
    rows = out_ref.shape[1]
    tail = list(halves(small_ref[...]))
    if rows > cut + 2 * lines:
        tail.append(jnp.zeros((rows - cut - 2 * lines, full), BF))
    tail = jnp.concatenate(tail, axis=0)
    for s in range(n_seq):
        out_ref[s, :cut] = (own_ref[s].astype(F32) + got_ref[s].astype(F32)).astype(BF)
        out_ref[s, cut:] = tail


def pack(own, got, small, rows, earlier=()):
    n_seq, cut, full = own.shape
    return launch(
        partial(pack_kernel, small.shape[0]),
        [whole(own.shape), whole(got.shape), whole(small.shape)],
        earlier,
        grid=(1,),
        out_specs=whole((n_seq, rows, full)),
        out_shape=jax.ShapeDtypeStruct((n_seq, rows, full), BF),
        compiler_params=small_params("arbitrary"),
        cost_estimate=cost(1, 1.5),
        name="pack",
    )(own, got, small)


def place_units_kernel(unit_cut, unit_pad, n_seq, where, *refs):
    parts, out_ref = refs[:-1], refs[-1]
    n_row = len(parts)
    group = unit_cut * n_row
    hidden = group * n_seq
    for block in range(hidden // LANES):
        low = (block * LANES // group) * unit_pad // LANES * LANES
        high = ((block * LANES + LANES - 1) // group + 1) * unit_pad
        high = min(n_seq * unit_pad, -(-high // LANES) * LANES)
        col = lax.broadcasted_iota(jnp.int32, (high - low, LANES), 1) + block * LANES
        row = lax.broadcasted_iota(jnp.int32, (high - low, LANES), 0) + low
        inner = lax.rem(col, group)
        owner = lax.div(inner, unit_cut)
        unit = lax.div(col, group) * unit_pad + lax.rem(inner, unit_cut)
        total = [0.0, 0.0]
        for j, part in enumerate(parts):
            chosen = jnp.where((unit == row) & (owner == (where[0] ^ j)), 1.0, 0.0).astype(BF)
            for half in range(2):
                at = half * n_seq * unit_pad
                total[half] = total[half] + dot(part[:, at + low : at + high], chosen)
        for half in range(2):
            to = half * hidden + block * LANES
            out_ref[:, to : to + LANES] = total[half]


def place_units(where, parts, unit_cut, unit_pad, n_seq):
    rows = parts[0].shape[0]
    shape = (rows, 2 * unit_cut * n_seq * len(parts))
    return pl.pallas_call(
        partial(place_units_kernel, unit_cut, unit_pad, n_seq),
        grid_spec=pltpu.PrefetchScalarGridSpec(
            num_scalar_prefetch=1,
            grid=(1,),
            in_specs=[pl.BlockSpec(part.shape, lambda i, where: (0, 0)) for part in parts],
            out_specs=pl.BlockSpec(shape, lambda i, where: (0, 0)),
        ),
        out_shape=jax.ShapeDtypeStruct(shape, F32),
        compiler_params=small_params("arbitrary"),
        cost_estimate=cost(1, 5.0),
        name="place_units",
    )(where, *parts)


def place_rows_kernel(where, *refs):
    parts, out_ref = refs[:-1], refs[-1]
    for j, part in enumerate(parts):
        out_ref[where[0] ^ j] = part[...].astype(F32)


def place_down_kernel(unit_pad, left, where, *refs):
    parts, out_ref = refs[:-1], refs[-1]
    _, keep, model = out_ref.shape
    n_units = parts[0].shape[1] - left
    rest = model - n_units
    step = unit_pad * rest // n_units
    for j, part in enumerate(parts):
        at = where[0] ^ j
        out_ref[at, :, :n_units] = part[:keep, left:].astype(F32)
        for b in range(n_units // rest):
            have = min(step, keep - b * step)
            if have > 0:
                value = part[unit_pad : unit_pad + have, left + b * rest : left + (b + 1) * rest]
                out_ref[at, b * step : b * step + have, n_units:] = value.astype(F32)


def place_rows(where, parts, shape, kernel=place_rows_kernel):
    return pl.pallas_call(
        kernel,
        grid_spec=pltpu.PrefetchScalarGridSpec(
            num_scalar_prefetch=1,
            grid=(1,),
            in_specs=[pl.BlockSpec(part.shape, lambda i, where: (0, 0)) for part in parts],
            out_specs=pl.BlockSpec((len(parts),) + shape, lambda i, where: (0, 0, 0)),
        ),
        out_shape=jax.ShapeDtypeStruct((len(parts),) + shape, F32),
        compiler_params=small_params("arbitrary"),
        cost_estimate=cost(1, 2.0),
        name="place_rows",
    )(where, *parts).reshape(-1, shape[1])


def place_down(where, parts, unit_pad, left, shape):
    return place_rows(where, parts, shape, partial(place_down_kernel, unit_pad, left))


def feed_kernel(n_seq, mid_ref, d_top_ref, w_ref, act_ref, d_gu_ref, down_ref, *d_mid_refs):
    n_units = act_ref.shape[1]
    model = mid_ref.shape[1]
    per = n_units // n_seq

    @pl.when(pl.program_id(0) == 0)
    def _():
        lines = w_ref[:, 2 * n_units :].reshape(n_seq, model // n_seq, n_units)
        rest = model - n_units
        step = per * rest // n_units
        for s in range(n_seq):
            down_ref[s * per : (s + 1) * per, :n_units] = lines[s, :per]
            for b in range(n_units // rest):
                at = s * per + b * step
                down_ref[at : at + step, n_units:] = lines[s, per:, b * rest : (b + 1) * rest]

    w_gate = w_ref[:, :n_units]
    w_up = w_ref[:, n_units : 2 * n_units]
    mid = mid_ref[...]
    gate = dot(mid, w_gate)
    up = dot(mid, w_up)
    d_act = dot(d_top_ref[...], down_ref[...], 1, 1)
    sig = jax.nn.sigmoid(gate)
    silu = gate * sig
    act_ref[...] = (silu * up).astype(BF)
    d_gate = (d_act * up * sig * (1.0 + gate * (1.0 - sig))).astype(BF)
    d_up = (d_act * silu).astype(BF)
    d_gu_ref[0] = d_gate
    d_gu_ref[1] = d_up
    d_mid = (dot(d_gate, w_gate, 1, 1) + dot(d_up, w_up, 1, 1)).astype(BF)
    for j, d_mid_ref in enumerate(d_mid_refs):

        @pl.when(pl.program_id(0) == j)
        def _(d_mid_ref=d_mid_ref):
            d_mid_ref[...] = d_mid


def feed(mid, d_top, weights, n_units, n_seq, n_parts):
    tokens, model = mid.shape
    size = tokens // n_parts
    rows = lambda n: pl.BlockSpec((size, n), lambda i: (i, 0))
    return pl.pallas_call(
        partial(feed_kernel, n_seq),
        grid=(n_parts,),
        in_specs=[rows(model), rows(model), whole(weights.shape)],
        out_specs=[
            rows(n_units), pl.BlockSpec((2, size, n_units), lambda i: (0, i, 0)),
            whole((n_units, model)),
        ] + [whole((size, model))] * n_parts,
        out_shape=[
            jax.ShapeDtypeStruct((tokens, n_units), BF),
            jax.ShapeDtypeStruct((2, tokens, n_units), BF),
            jax.ShapeDtypeStruct((n_units, model), BF),
        ] + [jax.ShapeDtypeStruct((size, model), BF)] * n_parts,
        compiler_params=params("arbitrary"),
        cost_estimate=cost(1, 14.0),
        name="feed",
    )(mid, d_top, weights)


def times_kernel(left_ref, right_ref, *out_refs):
    value = dot(left_ref[...], right_ref[...]).astype(BF)
    for j, out_ref in enumerate(out_refs):

        @pl.when(pl.program_id(0) == j)
        def _(out_ref=out_ref):
            out_ref[...] = value


def times(left, right, n_parts, earlier=()):
    tokens, inner = left.shape
    size = tokens // n_parts
    return launch(
        times_kernel,
        [pl.BlockSpec((size, inner), lambda i: (i, 0)), whole(right.shape)],
        earlier,
        grid=(n_parts,),
        out_specs=[whole((size, right.shape[1]))] * n_parts,
        out_shape=[jax.ShapeDtypeStruct((size, right.shape[1]), BF)] * n_parts,
        compiler_params=small_params("arbitrary"),
        cost_estimate=cost(1, 3.0),
        name="times",
    )(left, right)


def feed_grads(mid, d_gu, g_down, n_seq, earlier=(), size=256):
    tokens, model = mid.shape
    n_units = d_gu.shape[2]
    shard, unit_pad = model // n_seq, n_units // n_seq
    per = size // shard

    def body(mid_ref, d_gu_ref, g_down_ref, out_ref):
        mid = mid_ref[...]
        for half in range(2):
            value = dot(mid, d_gu_ref[half], 0, 0).astype(BF)
            out_ref[:, half * n_units : (half + 1) * n_units] = value
        rest = model - n_units
        step = unit_pad * rest // n_units
        for part in range(per):
            at, rows = part * shard, g_down_ref[part * unit_pad : (part + 1) * unit_pad]
            out_ref[at : at + unit_pad, 2 * n_units :] = rows[:, :n_units]
            for b in range(n_units // rest):
                to = 2 * n_units + b * rest
                out_ref[at + unit_pad : at + shard, to : to + rest] = rows[
                    b * step : (b + 1) * step, n_units:
                ]

    return launch(
        body,
        [
            pl.BlockSpec((tokens, size), lambda i: (0, i)), whole(d_gu.shape),
            pl.BlockSpec((per * unit_pad, model), lambda i: (i, 0)),
        ],
        earlier,
        grid=(model // size,),
        out_specs=pl.BlockSpec((size, 3 * n_units), lambda i: (i, 0)),
        out_shape=jax.ShapeDtypeStruct((model, 3 * n_units), BF),
        compiler_params=params("arbitrary"),
        cost_estimate=cost(1, 7.0),
        name="feed_grads",
    )(mid, d_gu, g_down)


def place_pieces_kernel(order, where, *refs):
    parts, out_ref = refs[:-1], refs[-1]
    for j, part in enumerate(parts):
        for n in range(part.shape[0]):
            at = n if order is None else where[1] ^ order[n]
            out_ref[at, where[0] ^ j] = part[n]


def place_pieces(where, parts, order=None):
    n_seq, cut, width = parts[0].shape
    shape = (n_seq, len(parts), cut, width)
    return pl.pallas_call(
        partial(place_pieces_kernel, order),
        grid_spec=pltpu.PrefetchScalarGridSpec(
            num_scalar_prefetch=1,
            grid=(1,),
            in_specs=[pl.BlockSpec(part.shape, lambda i, where: (0, 0, 0)) for part in parts],
            out_specs=pl.BlockSpec(shape, lambda i, where: (0, 0, 0, 0)),
        ),
        out_shape=jax.ShapeDtypeStruct(shape, BF),
        compiler_params=small_params("arbitrary"),
        cost_estimate=cost(1, 2.0),
        name="place_pieces",
    )(where, *parts).reshape(-1, width)


def middle_kernel(copies, gated_ref, x_ref, w_ref, gain_ref, residual_ref, normed_ref, gated_out_ref):
    n_heads = gated_ref.shape[0] // copies
    total = x_ref[0].astype(F32)
    for h in range(n_heads):
        part = gated_ref[h * copies, 0]
        gated_out_ref[0, :, h * LANES : (h + 1) * LANES] = part
        total = total + dot(part, w_ref[h * LANES : (h + 1) * LANES])
    scale = lax.rsqrt(jnp.mean(total * total, axis=-1, keepdims=True) + EPS_NORM)
    residual_ref[0] = total
    normed_ref[0] = (total * scale * gain_ref[...]).astype(BF)


def middle(gated, x, w_out, gain, copies):
    n_micro, n_tok, model = x.shape
    n_seq = gated.shape[0]
    rows = pl.BlockSpec((1, n_tok, model), lambda m: (m, 0, 0))
    made = lambda kind: jax.ShapeDtypeStruct((n_micro, n_tok, model), kind)
    return pl.pallas_call(
        partial(middle_kernel, copies),
        grid=(n_micro,),
        in_specs=[
            pl.BlockSpec((n_seq, 1, n_tok, LANES), lambda m: (0, m, 0, 0)),
            rows, whole(w_out.shape), whole((1, model)),
        ],
        out_specs=[rows] * 3,
        out_shape=[made(F32), made(BF), made(BF)],
        compiler_params=small_params("arbitrary"),
        cost_estimate=cost(1, 4.0),
        name="middle",
    )(gated, x, w_out, gain[None])


def input_back_kernel(d_ext_ref, w_ref, out_ref):
    value = dot(d_ext_ref[0], w_ref[...], 1, 1).astype(BF)
    per, _, n_tok, _ = out_ref.shape
    for part in range(per):
        out_ref[part, 0] = value[part * n_tok : (part + 1) * n_tok]


def input_back(d_ext, w_ext, n_tok, size=512):
    n_micro, length, wide = d_ext.shape
    model = w_ext.shape[0]
    per = size // n_tok
    return pl.pallas_call(
        input_back_kernel,
        grid=(n_micro, length // size),
        in_specs=[pl.BlockSpec((1, size, wide), lambda m, s: (m, s, 0)), whole(w_ext.shape)],
        out_specs=pl.BlockSpec((per, 1, n_tok, model), lambda m, s: (s, m, 0, 0)),
        out_shape=jax.ShapeDtypeStruct((length // n_tok, n_micro, n_tok, model), BF),
        compiler_params=params("arbitrary", "arbitrary"),
        cost_estimate=cost(1, 7.0),
        name="input_back",
    )(d_ext, w_ext)


def bottom_kernel(d_in_ref, d_residual_ref, x_ref, gain_ref, out_ref):
    x = x_ref[0].astype(F32)
    scale = lax.rsqrt(jnp.mean(x * x, axis=-1, keepdims=True) + EPS_NORM)
    d_normed = d_in_ref[...].astype(F32) * gain_ref[...]
    out_ref[0] = (
        d_residual_ref[...]
        + scale * d_normed
        - x * scale**3 * jnp.mean(d_normed * x, axis=-1, keepdims=True)
    )


def bottom(d_in, d_residual, x, gain, earlier=()):
    n_micro, n_tok, model = x.shape
    rows = pl.BlockSpec((n_tok, model), lambda m: (m, 0))
    block = pl.BlockSpec((1, n_tok, model), lambda m: (m, 0, 0))
    return launch(
        bottom_kernel,
        [rows, rows, block, whole((1, model))],
        earlier,
        grid=(n_micro,),
        out_specs=block,
        out_shape=jax.ShapeDtypeStruct((n_micro, n_tok, model), F32),
        compiler_params=small_params("arbitrary"),
        cost_estimate=cost(1, 2.0),
        name="bottom",
    )(d_in, d_residual, x, gain[None])


def turn_kernel(
    own_ref, got_ref, d_top_ref, residual_ref, w_ref, gain_ref, d_residual_ref, d_low_ref, d_sent_ref, norm_ref
):
    @pl.when(pl.program_id(0) == 0)
    def _():
        norm_ref[...] = jnp.zeros_like(norm_ref)

    residual = residual_ref[...]
    scale = lax.rsqrt(jnp.mean(residual * residual, axis=-1, keepdims=True) + EPS_NORM)
    d_mid = own_ref[...].astype(F32) + got_ref[...].astype(F32)
    norm_ref[0:1, :] += jnp.sum(d_mid * residual * scale, axis=0, keepdims=True)
    d_normed = d_mid * gain_ref[...]
    d_residual = (
        d_top_ref[...]
        + scale * d_normed
        - residual * scale**3 * jnp.mean(d_normed * residual, axis=-1, keepdims=True)
    )
    d_residual_ref[...] = d_residual
    d_low = d_residual.astype(BF)
    d_low_ref[...] = d_low
    d_gated = dot(d_low, w_ref[...], 1, 1).astype(BF)
    for h in range(d_sent_ref.shape[0]):
        d_sent_ref[h, 0] = d_gated[:, h * LANES : (h + 1) * LANES]


def turn(own, got, d_top, residual, w_out, gain, n_micro):
    tokens, model = own.shape
    n_tok = tokens // n_micro
    n_heads = model // LANES
    rows = pl.BlockSpec((n_tok, model), lambda m: (m, 0))
    return pl.pallas_call(
        turn_kernel,
        grid=(n_micro,),
        in_specs=[rows, rows, rows, rows, whole(w_out.shape), whole((1, model))],
        out_specs=[
            rows, rows,
            pl.BlockSpec((n_heads, 1, n_tok, LANES), lambda m: (0, m, 0, 0)),
            whole((8, model)),
        ],
        out_shape=[
            jax.ShapeDtypeStruct((tokens, model), F32),
            jax.ShapeDtypeStruct((tokens, model), BF),
            jax.ShapeDtypeStruct((n_heads, n_micro, n_tok, LANES), BF),
            jax.ShapeDtypeStruct((8, model), F32),
        ],
        compiler_params=small_params("arbitrary"),
        cost_estimate=cost(1, 5.0),
        name="turn",
    )(own, got, d_top, residual, w_out, gain[None])


def pick(stacked, at, axis=0):
    return lax.dynamic_index_in_dim(stacked, at, axis, False, allow_negative_indices=False)


def exchange(value, axis, bit):
    count = lax.axis_size(axis)
    return lax.ppermute(value, axis, [(i, i ^ bit) for i in range(count)])


def bits(axis):
    count = lax.axis_size(axis)
    return [1 << b for b in range(count.bit_length() - 1)]


def row_gather(value):
    parts = {0: value}
    for bit in reversed(bits("row")):
        parts.update({j ^ bit: exchange(part, "row", bit) for j, part in parts.items()})
    return [parts[j] for j in range(len(parts))]


def row_gather_steps(value):
    parts = {0: value}
    for bit in reversed(bits("row")):
        got = {j ^ bit: exchange(part, "row", bit) for j, part in parts.items()}
        parts.update(got)
        yield list(got.values())
    return [parts[j] for j in range(len(parts))]


def seq_scatter_steps(parts):
    mine = lax.axis_index("seq")
    for bit in reversed(bits("seq")):
        parts = parts.reshape((2, bit) + parts.shape[1:])
        side = (mine & bit) // bit
        got = exchange(pick(parts, 1 - side).astype(BF), "seq", bit)
        yield got
        parts = pick(parts, side).astype(F32) + got.astype(F32)
    return parts[0].astype(BF)


def seq_gather_steps(value):
    parts, order = value[None], [0]
    for n, bit in enumerate(reversed(bits("seq"))):
        parts = jnp.concatenate([parts, exchange(parts, "seq", bit)], axis=0)
        order = order + [place ^ bit for place in order]
        if n + 1 < len(bits("seq")):
            sent = yield parts
            parts = parts if sent is None else sent
    return parts, order


def finish(steps, value=None):
    try:
        steps.send(value)
        while True:
            next(steps)
    except StopIteration as end:
        return end.value


def row_scatter_halves(parts):
    parts = dict(enumerate(parts))
    for bit in bits("row"):
        got = {j ^ bit: exchange(parts[j].astype(BF), "row", bit) for j in parts if j & bit}
        if len(got) == 1:
            return parts[0], got[0]
        parts = {j: parts[j].astype(F32) + part.astype(F32) for j, part in got.items()}


def ring():
    count, mine = lax.axis_size("seq"), lax.axis_index("seq")
    order = list(range(0, count, 2)) + list(range(1, count, 2))[::-1]
    half = mine >> 1
    place = jnp.where((mine & 1) == 0, half, count - 1 - half)

    def owner(k):
        at = (place + (k % count)) & (count - 1)
        return jnp.where(at < count // 2, 2 * at, 2 * count - 1 - 2 * at)

    ahead = [(order[i], order[(i + 1) % count]) for i in range(count)]
    behind = [(b, a) for a, b in ahead]
    return count, owner, ahead, behind


def ring_gather(value, earlier):
    count, owner, ahead, behind = ring()
    blocks = jnp.zeros((count,) + value.shape, value.dtype)
    put = lambda blocks, block, k: lax.dynamic_update_index_in_dim(
        blocks, block, owner(k), 0, allow_negative_indices=False
    )
    blocks = put(blocks, value, 0)
    there, back = value, value
    for k in range(1, count // 2):
        there = lax.ppermute(there, "seq", ahead)
        back = lax.ppermute(back, "seq", behind)
        if k in earlier:
            there = fence(there, *earlier[k])
        blocks = put(put(blocks, there, -k), back, k)
    cut = value.shape[1] // 2
    there = lax.ppermute(there[:, :cut], "seq", ahead)
    back = lax.ppermute(back[:, cut:], "seq", behind)
    return put(blocks, jnp.concatenate([there, back], axis=1), count // 2)


def matmul(spec, left, right, kind=F32):
    return jnp.einsum(spec, left, right, preferred_element_type=F32).astype(kind)


def local(
    tokens,
    cotangent,
    row_lengths,
    norm1_gain,
    w_in,
    w_router,
    conv_weight,
    a_log,
    dt_bias,
    head_gain,
    w_out,
    norm2_gain,
    w_gu,
    w_down,
):
    n_seq, n_row = lax.axis_size("seq"), lax.axis_size("row")
    seq, row = lax.axis_index("seq"), lax.axis_index("row")
    n_micro, _, n_tok, model = tokens.shape
    micros = list(range(n_micro))
    n_heads = a_log.shape[0]
    head_dim = head_gain.shape[0]
    n_taps, conv_width = conv_weight.shape
    slots = w_in.shape[1] // (n_heads * head_dim)
    width = conv_width // n_heads
    full = slots * head_dim
    length = n_tok * n_seq
    copies = n_seq // n_heads
    head = seq // copies
    gate_at = slots - 1

    def to_heads(value):
        return lax.all_to_all(jnp.repeat(value, copies, axis=0), "seq", 0, 0, tiled=True)

    def seq_parts(value):
        return lax.all_to_all(value, "seq", 0, 0, tiled=True)

    def from_heads(value):
        got = lax.all_to_all(value, "seq", 0, 0, tiled=True)
        return got if copies == 1 else got[::copies]

    def in_order(parts, axis):
        stacked = jnp.stack(parts)
        return jnp.concatenate([pick(stacked, row ^ j) for j in range(n_row)], axis=axis)

    where = jnp.stack([row, seq]).astype(jnp.int32)

    cut = w_in.shape[0] // n_row
    w_piece = pick(w_in.reshape(n_row, cut, slots, n_heads, head_dim), row)
    w_got = to_heads(w_piece.transpose(2, 0, 1, 3).reshape(n_heads, cut, full))
    w_head = place_pieces(where, row_gather(w_got))
    w_rt = pick(w_router.reshape(model, -1, n_heads), head, 2)
    n_rt = w_rt.shape[1]
    w_rt = jnp.pad(w_rt, ((0, 0), (0, LANES - n_rt)))
    w_ext = jnp.concatenate([w_head, w_rt], axis=1)
    taps = pick(conv_weight.reshape(n_taps, gate_at, n_heads, head_dim), head, 2)
    taps = jnp.pad(taps.reshape(n_taps, width), ((0, 8 - n_taps), (0, 0)))
    par = jnp.concatenate(
        [
            head_gain[None],
            jnp.broadcast_to(lax.dynamic_index_in_dim(a_log, head, 0), (1, LANES)),
            jnp.broadcast_to(lax.dynamic_index_in_dim(dt_bias, head, 0), (1, LANES)),
            jnp.zeros((5, LANES), F32),
        ]
    )
    position = seq * n_tok + jnp.arange(n_tok, dtype=jnp.int32)
    live = (position[None, :] < row_lengths[:, :1]).astype(F32)[:, :, None]
    d_top = (cotangent[:, 0].astype(F32) * live).reshape(-1, model)
    d_rows = jnp.concatenate(row_gather(d_top.astype(BF)), axis=0)

    out_cut = w_out.shape[0] // n_row
    out_piece = lax.dynamic_slice_in_dim(w_out, row * out_cut, out_cut, 0)
    out_steps = seq_gather_steps(out_piece)
    out_got = next(out_steps)

    x_all = ring_gather(
        tokens[:, 0], {n_seq // 4: [w_got], n_seq // 2 - 1: [w_ext, w_rt, taps, par, d_rows, out_got]}
    )

    shard = w_out.shape[0]
    hidden = w_gu.shape[1] // 2
    unit_cut = hidden // n_seq // n_row
    unit_pad = -(-unit_cut // 16) * 16
    n_units = unit_pad * n_seq
    gu_piece = pick(w_gu.reshape(shard, 2, n_seq, n_row, unit_cut), row, 3)
    gu_piece = jnp.pad(gu_piece, ((0, 0), (0, 0), (0, 0), (0, unit_pad - unit_cut)))
    down_piece = lax.dynamic_slice_in_dim(w_down, row * unit_cut, unit_cut, 0)
    down_piece = jnp.pad(down_piece, ((0, unit_pad - unit_cut), (0, 0)))
    beside = down_piece[:, n_units:]
    beside = beside.reshape(n_units // beside.shape[1], -1, beside.shape[1])
    beside = jnp.concatenate(list(beside), axis=1)
    down_piece = jnp.concatenate([down_piece[:, :n_units], beside])
    weights = jnp.concatenate([gu_piece.reshape(shard, -1), down_piece], axis=1)
    weights = fence(weights, x_all)
    weights_all = lax.all_gather(weights, "seq", axis=0, tiled=True)

    normed_in, projected, router = project(x_all, norm1_gain, w_head, w_rt, [d_rows, weights])
    out_got = out_steps.send(fence(out_got, projected))
    prep = prepare(projected, router, taps, par, width)
    out_got, order = finish(out_steps, fence(out_got, prep[0]))
    gated, *kept = scan_states(prep, router, projected, par, gate_at, n_tok)
    full_out = place_pieces(where, row_gather(fence(out_got, gated)), order)

    residual, normed_mid, gated = middle(
        seq_parts(gated), tokens[:, 0], full_out, norm2_gain, copies
    )
    residual, normed_mid, gated = (
        value.reshape(-1, model) for value in (residual, normed_mid, gated)
    )
    mid_rows = jnp.concatenate(row_gather(normed_mid), axis=0)
    act, d_gu, down, *d_mid = feed(
        mid_rows, d_rows, weights_all, n_units, n_seq, n_row
    )
    g_down = matmul("tf,td->fd", act, d_rows, BF)
    g_feed = feed_grads(mid_rows, d_gu, g_down, n_seq)
    g_feed_sum = lax.psum_scatter(g_feed, "seq", scatter_dimension=0, tiled=True)
    d_mid_own, d_mid_got = row_scatter_halves(d_mid)

    def row_parts(value, axis):
        return [pick(value, row ^ j, axis) for j in range(n_row)]

    d_residual, d_low, d_sent, g_norm2 = turn(
        d_mid_own, fence(d_mid_got, g_feed), d_top, residual, full_out, norm2_gain, n_micro
    )
    d_gated = to_heads(d_sent)

    mlp = times(act, down, n_row, [d_sent])
    out_halves = row_scatter_halves(mlp)
    g_out_full = matmul("tc,td->cd", fence(gated, d_sent), d_low)
    g_out = g_out_full
    g_out = row_scatter_halves(row_parts(g_out.reshape(n_seq, n_row, out_cut, model), 1))

    mixed, news, state = kept
    d_mixed, d_news, d_state, d_gate_pre, g_head = scan_back(
        prep, router, projected, par, gate_at, mixed, d_gated
    )
    d_ext, g_taps, g_par = mixer_grads(
        prep, router, projected, taps, par, width,
        news, state, d_mixed, d_news, d_state, d_gate_pre, [g_out[1], out_halves[1]],
    )
    if copies > 1:
        mine = (seq % copies == 0).astype(F32)
        d_ext = d_ext * mine.astype(BF)
        g_taps, g_par, g_head = g_taps * mine, g_par * mine, g_head * mine
    d_in_part = input_back(d_ext, w_ext, n_tok).reshape(-1, model)
    d_in = lax.psum_scatter(d_in_part, "seq", scatter_dimension=0, tiled=True)
    g_in, in_lines = input_grads(normed_in, d_ext, w_ext, norm1_gain, full, [d_in_part])
    fill = lambda value: jnp.pad(value, ((0, 0), (0, full - value.shape[1])))
    scalars = jnp.concatenate([g_head[:1], g_par[1:2], g_par[2:3]], axis=1)
    vectors = jnp.concatenate([in_lines[: n_rt + 1], g_norm2[:1]]).reshape(-1, model // 2)
    small = jnp.concatenate([fill(vectors), fill(scalars), fill(g_taps[:n_taps])])
    n_vec = vectors.shape[0]
    lines = -(-small.shape[0] // n_row)
    small = jnp.pad(small, ((0, n_row * lines - small.shape[0]), (0, 0))).reshape(n_row, lines, full)

    parts = dict(enumerate(row_parts(g_in.reshape(n_seq, n_row, cut, full), 1)))
    smalls = dict(enumerate(row_parts(small, 0)))
    for bit in bits("row"):
        got = {j ^ bit: exchange(parts[j], "row", bit) for j in parts if j & bit}
        got_small = {j ^ bit: exchange(smalls[j], "row", bit) for j in smalls if j & bit}
        smalls = {j: smalls[j] + part for j, part in got_small.items()}
        if len(got) > 1:
            parts = {
                j: (parts[j].astype(F32) + part.astype(F32)).astype(BF) for j, part in got.items()
            }
    g_out = g_out[0].astype(F32) + fence(g_out[1], parts[0]).astype(F32)
    g_out_steps = seq_scatter_steps(g_out)
    rows = cut + -(-2 * lines // 16) * 16
    g_in_got = seq_parts(pack(parts[0], got[0], smalls[0], rows))
    feed_steps = row_gather_steps(fence(g_feed_sum, got[0]))
    g_in_got = fence(g_in_got, *next(feed_steps), next(g_out_steps))
    in_steps = row_gather_steps(g_in_got)
    first_in = next(in_steps)
    g_out_sum = finish(g_out_steps)
    g_feed_all = finish(feed_steps)
    g_out_all = row_gather(g_out_sum)
    grad_out = place_rows(where, g_out_all, (out_cut, model))
    grad_down = place_down(where, g_feed_all, unit_pad, 2 * n_units, (unit_cut, model))
    grad_gu = place_units(where, g_feed_all, unit_cut, unit_pad, n_seq)
    g_in_all = finish(in_steps)
    grad_in, small = place_heads(where, g_in_all, n_heads, slots, cut, lines)
    before = [grad_in, grad_gu, grad_down, grad_out]
    grad_tokens = bottom(d_in, d_residual, tokens[:, 0], norm1_gain, before)[:, None]
    out = residual + out_halves[0].astype(F32) + out_halves[1].astype(F32)
    out = out.astype(BF).reshape(n_micro, 1, n_tok, model)
    total = jnp.sum(small[:, 2 * n_rt : n_vec + 1], axis=0)
    norms = total[:4, : model // 2].reshape(2, model)
    heads = small[::copies]
    conv_sum = heads[:, n_vec + 1 : n_vec + 1 + n_taps, :width]
    conv_sum = conv_sum.reshape(n_heads, n_taps, gate_at, head_dim)
    conv_sum = conv_sum.transpose(1, 2, 0, 3).reshape(n_taps, conv_width)
    router_sum = heads[:, : 2 * n_rt, : model // 2].reshape(n_heads, n_rt, model)
    router_sum = router_sum.transpose(2, 1, 0).reshape(model, n_rt * n_heads)
    return (
        out,
        grad_tokens,
        norms[0],
        grad_in,
        router_sum,
        conv_sum,
        heads[:, n_vec, LANES + 2],
        heads[:, n_vec, 2 * LANES + 2],
        total[4, :head_dim],
        grad_out,
        norms[1],
        grad_gu,
        grad_down,
    )


def solution(mesh):
    by_rows = P("seq", None)
    by_tokens = P(None, "row", "seq", None)
    return jax.shard_map(
        local,
        mesh=mesh,
        in_specs=(
            by_tokens, by_tokens, P(None, "row"), P(), by_rows, P(), P(), P(), P(), P(),
            by_rows, P(), by_rows, by_rows,
        ),
        out_specs=(
            by_tokens, by_tokens, P(), by_rows, P(), P(), P(), P(), P(),
            by_rows, P(), by_rows, by_rows,
        ),
        check_vma=False,
    )
```

```python
from functools import partial

import jax
import jax.numpy as jnp
from jax import lax
from jax.experimental import pallas as pl
from jax.experimental.pallas import tpu as pltpu
from jax.sharding import PartitionSpec as P

BF = jnp.bfloat16
F32 = jnp.float32
EPS_NORM = 1e-05
EPS_UNIT = 1e-06
CH = 64
ST = 128
HALO = 16
LANES = 128
VMEM_BYTES = 60 * 1024 * 1024
SMALL_BYTES = 50 * 1024 * 1024


def halves(value):
    high = value.astype(BF)
    return (high, (value - high.astype(F32)).astype(BF))


def dot(left, right, over_left=1, over_right=0):
    return lax.dot_general(
        left, right, (((over_left,), (over_right,)), ((), ())), preferred_element_type=F32
    )


def mm(left, right, over_left=1, over_right=0):
    left = left if isinstance(left, tuple) else (left,)
    right = right if isinstance(right, tuple) else (right,)
    total = dot(left[0], right[0], over_left, over_right)
    if len(right) > 1:
        total = total + dot(left[0], right[1], over_left, over_right)
    if len(left) > 1:
        total = total + dot(left[1], right[0], over_left, over_right)
    return total


def exact_sum(ones, value):
    high = value.astype(BF)
    rest = value - high.astype(F32)
    mid = rest.astype(BF)
    low = (rest - mid.astype(F32)).astype(BF)
    return dot(ones, high) + dot(ones, mid) + dot(ones, low)


def step_orders():
    row = lax.broadcasted_iota(jnp.int32, (ST, ST), 0)
    col = lax.broadcasted_iota(jnp.int32, (ST, ST), 1)
    order = lambda i: 2 * (i & (CH - 1)) + (i >> 6)
    return order(row), order(col)


def sees():
    row = lax.broadcasted_iota(jnp.int32, (CH, ST), 0)
    col = lax.broadcasted_iota(jnp.int32, (CH, ST), 1)
    return (col & (CH - 1)) <= row


def twice(value):
    return jnp.concatenate([value, value], axis=0)


def log_decays(router, par):
    lane = lax.broadcasted_iota(jnp.int32, (CH, LANES), 1)
    pre = router + par[2:3]
    soft = jnp.maximum(pre, 0.0) + jnp.log1p(jnp.exp(-jnp.abs(pre)))
    decay = -jnp.exp(par[1:2]) * soft
    row = lax.broadcasted_iota(jnp.int32, (CH, CH), 0)
    col = lax.broadcasted_iota(jnp.int32, (CH, CH), 1)
    below = jnp.where(col <= row, 1.0, 0.0).astype(BF)
    total = exact_sum(below, jnp.where(lane == 2, decay, 0.0))
    return decay, total


def gate_columns(router, par):
    strength = jax.nn.sigmoid(router)
    decay, total = log_decays(router, par)
    beta = jnp.concatenate([strength[:, 0:1], strength[:, 1:2]], axis=0)
    doubled = twice(total)
    g_col = doubled[:, 2:3]
    g_row = doubled.T[2:3, :]
    g_last = total[CH - 1 : CH, 2:3]
    return beta, g_col, g_row, g_last, decay


def seen_decay(g_col, g_row, visible):
    return jnp.where(visible, jnp.exp(jnp.where(visible, g_col[:CH] - g_row, 0.0)), 0.0)


def unit(value):
    scale = lax.rsqrt(jnp.sum(value * value, axis=-1, keepdims=True) + EPS_UNIT)
    return value * scale, scale


def taps_sum(window, weight, start):
    total = weight[0:1] * window[pl.ds(start + 5, CH), :]
    for tap in range(1, 4):
        total = total + weight[tap : tap + 1] * window[pl.ds(start + 5 + tap, CH), :]
    return total


def fill_window(window, proj_ref, halo_ref, is_first):
    width = window.shape[1]
    edge = halo_ref[0, :, :width].astype(F32)[HALO - 8 :]
    window[0:8, :] = jnp.where(is_first, 0.0, edge)
    window[8:, :] = proj_ref[0, :, :width].astype(F32)


def prep_kernel(
    count, proj_ref, halo_ref, router_ref, taps_ref, par_ref,
    solve_ref, wmat_ref, umat_ref, seen_ref, q_ref, k_ref, window,
):
    fill_window(window, proj_ref, halo_ref, pl.program_id(0) == 0)
    weight = taps_ref[...]
    par = par_ref[...]
    o_row, o_col = step_orders()
    strict = o_row > o_col
    eye = jnp.where(o_row == o_col, 1.0, 0.0)
    visible = sees()
    many = range(count)
    lower, rights = [], []
    for n in many:
        conv = taps_sum(window, weight, n * CH)
        act = conv * jax.nn.sigmoid(conv)
        q = unit(act[:, 0:128])[0].astype(BF)
        k = jnp.concatenate(
            [unit(act[:, 128:256])[0], unit(act[:, 256:384])[0]], axis=0
        ).astype(BF)
        v = jnp.concatenate([act[:, 384:512], act[:, 512:640]], axis=0).astype(BF)
        beta, g_col, g_row, _, _ = gate_columns(
            router_ref[0, n * CH : (n + 1) * CH, :], par
        )
        gaps = seen_decay(g_col, g_row, visible)
        lower.append(jnp.where(strict, beta * twice(gaps) * dot(k, k, 1, 1), 0.0))
        kf = k.astype(F32)
        rights.append(
            jnp.concatenate([beta * jnp.exp(g_col) * kf, beta * v.astype(F32)], axis=1)
        )
        seen_ref[0, n] = gaps * dot(q, k, 1, 1)
        q_ref[0, n] = q
        k_ref[0, n] = k
    inverse = [eye - jnp.where((o_row >> 1) == (o_col >> 1), part, 0.0) for part in lower]
    for level in range(1, 7):
        at = ((o_row >> level) ^ (o_col >> level)) == 1
        parts = [halves(jnp.where(at, part, 0.0)) for part in lower]
        known = [halves(value) for value in inverse]
        inner = [halves(mm(parts[n], known[n])) for n in many]
        inverse = [inverse[n] - mm(known[n], inner[n]) for n in many]
    for n in many:
        solve_ref[0, n] = inverse[n]
        both = mm(halves(inverse[n]), halves(rights[n]))
        wmat_ref[0, n] = both[:, :128]
        umat_ref[0, n] = both[:, 128:]


def head_norm(mixed):
    return lax.rsqrt(jnp.mean(mixed * mixed, axis=-1, keepdims=True) + EPS_NORM)


def scan_kernel(
    n_micro, count, wmat_ref, umat_ref, seen_ref, q_ref, k_ref, router_ref, gate_ref, par_ref,
    out_ref, mixed_ref, news_ref, state_ref, state,
):
    @pl.when(pl.program_id(0) == 0)
    def _():
        state[...] = jnp.zeros_like(state)

    par = par_ref[...]
    now = [state[m] for m in range(n_micro)]
    for n in range(count):
        rows = slice(n * CH, (n + 1) * CH)
        for m in range(n_micro):
            _, g_col, _, g_last, _ = gate_columns(router_ref[m, rows, :], par)
            held = halves(now[m])
            state_ref[m, n] = now[m]
            news = umat_ref[m, n] - mm(halves(wmat_ref[m, n]), held)
            news_ref[m, n] = news
            news_h = halves(news)
            ends = halves(jnp.exp(g_last - g_col) * k_ref[m, n].astype(F32))
            now[m] = jnp.exp(g_last) * now[m] + mm(ends, news_h, 0, 0)
            mixed = jnp.exp(g_col[:CH]) * mm(q_ref[m, n], held) + mm(halves(seen_ref[m, n]), news_h)
            mixed_ref[m, n] = mixed
            gate = gate_ref[m, rows, :].astype(F32)
            tok = out_ref.shape[2]
            at = slice(n * CH % tok, n * CH % tok + CH)
            out_ref[n * CH // tok, m, at, :] = (
                mixed * head_norm(mixed) * par[0:1] * (gate * jax.nn.sigmoid(gate))
            ).astype(BF)
    for m in range(n_micro):
        state[m] = now[m]


def scan_back_kernel(
    n_micro, count, wmat_ref, seen_ref, q_ref, k_ref, router_ref, gate_ref, par_ref, mixed_ref, d_out_ref,
    d_mixed_ref, d_news_ref, d_state_ref, d_gate_ref, gain_ref, state,
):
    @pl.when(pl.program_id(0) == 0)
    def _():
        state[...] = jnp.zeros_like(state)
        gain_ref[...] = jnp.zeros_like(gain_ref)

    par = par_ref[...]
    now = [state[m] for m in range(n_micro)]
    gain = jnp.zeros((1, LANES), F32)
    for n in reversed(range(count)):
        rows = slice(n * CH, (n + 1) * CH)
        for m in range(n_micro):
            _, g_col, _, g_last, _ = gate_columns(router_ref[m, rows, :], par)
            mixed = mixed_ref[m, n]
            gate = gate_ref[m, rows, :].astype(F32)
            tok = d_out_ref.shape[2]
            at = slice(n * CH % tok, n * CH % tok + CH)
            d_out = d_out_ref[n * CH // tok, m, at, :].astype(F32)
            scale = head_norm(mixed)
            normed = mixed * scale
            sig = jax.nn.sigmoid(gate)
            silu = gate * sig
            gain = gain + jnp.sum(d_out * normed * silu, axis=0, keepdims=True)
            d_gate = d_out * normed * par[0:1] * (sig * (1.0 + gate * (1.0 - sig)))
            d_gate_ref[m, rows, :] = d_gate.astype(BF)
            d_normed = d_out * par[0:1] * silu
            d_mixed = scale * d_normed - mixed * scale**3 * jnp.mean(
                d_normed * mixed, axis=-1, keepdims=True
            )
            d_mixed_ref[m, n] = d_mixed
            d_mixed_h = halves(d_mixed)
            d_state_ref[m, n] = now[m]
            ends = halves(jnp.exp(g_last - g_col) * k_ref[m, n].astype(F32))
            d_news = mm(halves(seen_ref[m, n]), d_mixed_h, 0, 0) + mm(ends, halves(now[m]))
            d_news_ref[m, n] = d_news
            q_eff = halves(jnp.exp(g_col[:CH]) * q_ref[m, n].astype(F32))
            now[m] = (
                jnp.exp(g_last) * now[m]
                + mm(q_eff, d_mixed_h, 0, 0)
                - mm(halves(wmat_ref[m, n]), halves(d_news), 0, 0)
            )
    gain_ref[0:1, :] += gain
    for m in range(n_micro):
        state[m] = now[m]


def in_step(chains):
    while chains:
        chains = [chain for chain in chains if next(chain, chain) is not chain]


def unit_back(grad, value, scale):
    return scale * grad - value * scale**3 * jnp.sum(grad * value, axis=-1, keepdims=True)


def grads_kernel(
    count, proj_ref, halo_ref, router_ref, taps_ref, par_ref, solve_ref, seen_ref, news_ref, state_ref,
    d_mixed_ref, d_news_ref, d_state_ref, d_gate_ref,
    d_ext_ref, g_taps_ref, g_par_ref, window, d_window,
):
    step = pl.program_id(1)
    size = count * CH
    fill_window(window, proj_ref, halo_ref, step == pl.num_programs(1) - 1)

    @pl.when((step == 0) & (pl.program_id(0) == 0))
    def _():
        g_taps_ref[...] = jnp.zeros_like(g_taps_ref)
        g_par_ref[...] = jnp.zeros_like(g_par_ref)

    @pl.when(step == 0)
    def _():
        d_window[size:, :] = jnp.zeros((8, d_window.shape[1]), F32)

    @pl.when(step > 0)
    def _():
        d_window[size:, :] = d_window[0:8, :]

    weight = taps_ref[...]
    par = par_ref[...]
    o_row, o_col = step_orders()
    strict = o_row > o_col
    visible = sees()
    row = lax.broadcasted_iota(jnp.int32, (CH, CH), 0)
    col = lax.broadcasted_iota(jnp.int32, (CH, CH), 1)
    above = jnp.where(col >= row, 1.0, 0.0).astype(BF)
    lane = lax.broadcasted_iota(jnp.int32, (CH, LANES), 1)
    last = lax.broadcasted_iota(jnp.int32, (CH, LANES), 0) == CH - 1
    sums = [jnp.zeros((1, LANES), F32), jnp.zeros((1, LANES), F32)]

    def one(n):
        rows = slice(n * CH, (n + 1) * CH)
        conv = taps_sum(window, weight, n * CH)
        sig = jax.nn.sigmoid(conv)
        act = conv * sig
        qn, q_scale = unit(act[:, 0:128])
        k0n, k0_scale = unit(act[:, 128:256])
        k1n, k1_scale = unit(act[:, 256:384])
        q = qn.astype(BF)
        k = jnp.concatenate([k0n, k1n], axis=0).astype(BF)
        kf, qf = k.astype(F32), q.astype(F32)
        router = router_ref[0, rows, :]
        yield
        d_right = mm(halves(solve_ref[0, n]), halves(d_news_ref[0, n]), 0, 0)
        beta, g_col, g_row, g_last, decay = gate_columns(router, par)
        gaps = seen_decay(g_col, g_row, visible)
        yield
        ratio = jnp.where(strict, twice(gaps), 0.0)
        grown = jnp.exp(g_col)
        left = jnp.exp(g_last - g_col)
        gram = dot(k, k, 1, 1)
        state = state_ref[0, n]
        state_h = halves(state)
        news = news_ref[0, n]
        news_h = halves(news)
        d_mixed_h = halves(d_mixed_ref[0, n])
        d_state = d_state_ref[0, n]
        d_seen = mm(d_mixed_h, news_h, 1, 1)
        yield
        d_q_grown = grown[:CH] * mm(d_mixed_h, state_h, 1, 1)
        d_right_h = halves(d_right)
        d_lower = jnp.where(strict, -mm(d_right_h, news_h, 1, 1), 0.0)
        yield
        d_ends = left * mm(news_h, halves(d_state), 1, 1)
        d_pre = (1.0 - beta) * jnp.sum(d_right * news, axis=-1, keepdims=True)
        d_v = beta * d_right
        yield
        d_grown_k = -beta * mm(d_right_h, state_h, 1, 1)
        d_scores = halves(d_seen * gaps)
        seen_both = d_seen * seen_ref[0, n]
        yield
        d_q = d_q_grown + mm(d_scores, k)
        d_k = grown * d_grown_k
        d_gram = beta * ratio * d_lower
        both = d_gram * gram
        d_g = jnp.sum(both, axis=-1, keepdims=True) + jnp.sum(d_k * kf, axis=-1, keepdims=True)
        d_g_row = -jnp.sum(both, axis=0, keepdims=True)
        yield
        d_k = d_k + mm(halves(d_gram + d_gram.T), k) + d_ends
        d_g_q = jnp.sum(seen_both + d_q_grown * qf, axis=-1, keepdims=True)
        yield
        d_k = d_k + mm(d_scores, q, 0, 0)
        d_g_row = d_g_row - jnp.sum(seen_both, axis=0, keepdims=True)
        ends_sum = jnp.sum(d_ends * kf, axis=-1, keepdims=True)
        d_g = d_g - ends_sum
        d_last = jnp.sum(ends_sum, axis=0, keepdims=True) + jnp.exp(g_last) * jnp.sum(
            jnp.sum(d_state * state, axis=-1, keepdims=True), axis=0, keepdims=True
        )
        d_g_rows = jnp.broadcast_to(d_g_row, (LANES, ST)).T
        d_g_tok = d_g_q + d_g[:CH] + d_g[CH:] + d_g_rows[:CH] + d_g_rows[CH:]
        d_g_tok = d_g_tok + jnp.where(last, d_last, 0.0)
        yield
        d_decay = exact_sum(above, d_g_tok)
        yield
        d_soft = -jnp.exp(par[1:2]) * jax.nn.sigmoid(router + par[2:3]) * d_decay
        d_router = jnp.where(
            lane == 0,
            d_pre[:CH],
            jnp.where(lane == 1, d_pre[CH:], jnp.where(lane == 2, d_soft, 0.0)),
        )
        width = window.shape[1]
        d_ext_ref[0, rows, width : width + LANES] = d_gate_ref[0, rows, :]
        d_ext_ref[0, rows, width + LANES :] = d_router.astype(BF)
        sums[0] += jnp.sum(jnp.where(lane == 2, d_decay * decay, 0.0), axis=0, keepdims=True)
        sums[1] += jnp.sum(jnp.where(lane == 2, d_soft, 0.0), axis=0, keepdims=True)
        d_act = jnp.concatenate(
            [
                unit_back(d_q, act[:, 0:128], q_scale),
                unit_back(d_k[:CH], act[:, 128:256], k0_scale),
                unit_back(d_k[CH:], act[:, 256:384], k1_scale),
                d_v[:CH],
                d_v[CH:],
            ],
            axis=1,
        )
        d_window[rows, :] = d_act * (sig * (1.0 + conv * (1.0 - sig)))

    in_step([one(n) for n in range(count)])
    g_alog, g_dt = sums
    g_par_ref[1:2, :] += g_alog
    g_par_ref[2:3, :] += g_dt
    for n in range(count):
        start = n * CH
        here = d_window[pl.ds(start, CH), :]
        total = weight[3:4] * here
        for tap in range(3):
            total = total + weight[tap : tap + 1] * d_window[pl.ds(start + 3 - tap, CH), :]
        d_ext_ref[0, pl.ds(start, CH), : total.shape[1]] = total.astype(BF)
        for tap in range(4):
            g_taps_ref[tap : tap + 1, :] += jnp.sum(
                here * window[pl.ds(start + 5 + tap, CH), :], axis=0, keepdims=True
            )


def params(*semantics):
    return pltpu.CompilerParams(dimension_semantics=semantics, vmem_limit_bytes=VMEM_BYTES)


def small_params(*semantics):
    return pltpu.CompilerParams(dimension_semantics=semantics, vmem_limit_bytes=SMALL_BYTES)


def cost(chunks, per_chunk):
    return pl.CostEstimate(
        flops=int(chunks * per_chunk * 1.1e9), transcendentals=0, bytes_accessed=1 << 20
    )


def launch(kernel, in_specs, earlier, onto=(), first_out=0, **options):
    n_in = len(in_specs)
    others = list(earlier) + list(onto)

    def body(*refs):
        kernel(*refs[:n_in], *refs[n_in + len(others) :])

    specs = list(in_specs) + [pl.BlockSpec(memory_space=pl.ANY)] * len(others)
    at = n_in + len(earlier)
    aliases = {at + n: first_out + n for n in range(len(onto))}
    called = pl.pallas_call(body, in_specs=specs, input_output_aliases=aliases, **options)
    return lambda *operands: called(*operands, *others)


def fence(value, *earlier):
    earlier = [other for other in earlier if other is not None]
    if not earlier:
        return value
    anywhere = pl.BlockSpec(memory_space=pl.ANY)
    return pl.pallas_call(
        lambda *refs: None,
        in_specs=[anywhere] * (1 + len(earlier)),
        out_specs=anywhere,
        out_shape=jax.ShapeDtypeStruct(value.shape, value.dtype),
        input_output_aliases={0: 0},
        name="fence",
    )(value, *earlier)


def whole(shape):
    return pl.BlockSpec(shape, lambda *_: (0,) * len(shape))


def prepare(at, projected, router, taps, par, width, onto=(), earlier=(), count=8):
    n_micro, length, full = projected.shape
    chunks = length // CH
    size = count * CH
    per = lambda *tail: pl.BlockSpec((1, count) + tail, lambda i: (at, i, 0, 0))
    made = lambda kind, *tail: jax.ShapeDtypeStruct((n_micro, chunks) + tail, kind)
    return launch(
        partial(prep_kernel, count),
        [
            pl.BlockSpec((1, size, full), lambda i: (at, i, 0)),
            pl.BlockSpec((1, HALO, full), lambda i: (at, jnp.maximum(i * (size // HALO) - 1, 0), 0)),
            pl.BlockSpec((1, size, LANES), lambda i: (at, i, 0)),
            whole(taps.shape),
            whole(par.shape),
        ],
        earlier,
        onto,
        grid=(length // size,),
        out_specs=[per(ST, ST), per(ST, 128), per(ST, 128), per(CH, ST), per(CH, 128), per(ST, 128)],
        out_shape=[
            made(F32, ST, ST), made(F32, ST, 128), made(F32, ST, 128), made(F32, CH, ST),
            made(BF, CH, 128), made(BF, ST, 128),
        ],
        scratch_shapes=[pltpu.VMEM((size + 8, width), F32)],
        compiler_params=params("arbitrary"),
        cost_estimate=cost(chunks, 0.75),
        name="mixer_prepare",
    )(projected, projected, router, taps, par)


def scan_states(at, prep, router, projected, par, gate_at, n_tok, onto=(), earlier=(), count=4):
    _, wmat, umat, seen, q, k = prep
    n_micro, chunks = wmat.shape[:2]
    length = chunks * CH
    size = count * CH
    per = lambda *tail: pl.BlockSpec((1, count) + tail, lambda i: (at, i, 0, 0))
    made = lambda kind, *tail: jax.ShapeDtypeStruct((n_micro, chunks) + tail, kind)
    return launch(
        partial(scan_kernel, 1, count),
        [
            per(ST, 128), per(ST, 128), per(CH, ST), per(CH, 128), per(ST, 128),
            pl.BlockSpec((1, size, LANES), lambda i: (at, i, 0)),
            pl.BlockSpec((1, size, 128), lambda i: (at, i, gate_at)),
            whole(par.shape),
        ],
        earlier,
        onto,
        1,
        grid=(chunks // count,),
        out_specs=[
            pl.BlockSpec((size // n_tok, 1, n_tok, 128), lambda i: (i, 0, 0, 0)),
            per(CH, 128), per(ST, 128), per(128, 128),
        ],
        out_shape=[
            jax.ShapeDtypeStruct((length // n_tok, 1, n_tok, 128), BF),
            made(F32, CH, 128), made(F32, ST, 128), made(F32, 128, 128),
        ],
        scratch_shapes=[pltpu.VMEM((1, 128, 128), F32)],
        compiler_params=params("arbitrary"),
        cost_estimate=cost(chunks, 0.5),
        name="mixer_scan",
    )(wmat, umat, seen, q, k, router, projected, par)


def scan_back(prep, router, projected, par, gate_at, mixed, d_out, earlier=(), count=4):
    _, wmat, _, seen, q, k = prep
    n_micro, chunks = wmat.shape[:2]
    length = chunks * CH
    size = count * CH
    blocks = chunks // count
    n_tok = d_out.shape[2]
    per = lambda *tail: pl.BlockSpec((n_micro, count) + tail, lambda i: (0, blocks - 1 - i, 0, 0))
    made = lambda kind, *tail: jax.ShapeDtypeStruct((n_micro, chunks) + tail, kind)
    return launch(
        partial(scan_back_kernel, n_micro, count),
        [
            per(ST, 128), per(CH, ST), per(CH, 128), per(ST, 128),
            pl.BlockSpec((n_micro, size, LANES), lambda i: (0, blocks - 1 - i, 0)),
            pl.BlockSpec((n_micro, size, 128), lambda i: (0, blocks - 1 - i, gate_at)),
            whole(par.shape),
            per(CH, 128),
            pl.BlockSpec(
                (size // n_tok, n_micro, n_tok, 128), lambda i: (blocks - 1 - i, 0, 0, 0)
            ),
        ],
        earlier,
        grid=(blocks,),
        out_specs=[
            per(CH, 128), per(ST, 128), per(128, 128),
            pl.BlockSpec((n_micro, size, 128), lambda i: (0, blocks - 1 - i, 0)),
            whole((8, LANES)),
        ],
        out_shape=[
            made(F32, CH, 128), made(F32, ST, 128), made(F32, 128, 128),
            jax.ShapeDtypeStruct((n_micro, length, 128), BF),
            jax.ShapeDtypeStruct((8, LANES), F32),
        ],
        scratch_shapes=[pltpu.VMEM((n_micro, 128, 128), F32)],
        compiler_params=params("arbitrary"),
        cost_estimate=cost(n_micro * chunks, 0.4),
        name="mixer_scan_back",
    )(wmat, seen, q, k, router, projected, par, mixed, d_out)


def mixer_grads(
    prep, router, projected, taps, par, width, news, state, d_mixed, d_news, d_state, d_gate,
    earlier=(), count=4,
):
    solve, _, _, seen, _, _ = prep
    n_micro, chunks = solve.shape[:2]
    length = chunks * CH
    size = count * CH
    blocks = chunks // count
    full = projected.shape[2]
    per = lambda *tail: pl.BlockSpec((1, count) + tail, lambda m, i: (m, blocks - 1 - i, 0, 0))
    rows = lambda n: pl.BlockSpec((1, size, n), lambda m, i: (m, blocks - 1 - i, 0))
    before = lambda m, i: (m, jnp.maximum((blocks - 1 - i) * (size // HALO) - 1, 0), 0)
    return launch(
        partial(grads_kernel, count),
        [
            rows(full), pl.BlockSpec((1, HALO, full), before), rows(LANES),
            whole(taps.shape), whole(par.shape),
            per(ST, ST), per(CH, ST), per(ST, 128), per(128, 128),
            per(CH, 128), per(ST, 128), per(128, 128), rows(LANES),
        ],
        earlier,
        grid=(n_micro, blocks),
        out_specs=[rows(width + 2 * LANES), whole((8, width)), whole((8, LANES))],
        out_shape=[
            jax.ShapeDtypeStruct((n_micro, length, width + 2 * LANES), BF),
            jax.ShapeDtypeStruct((8, width), F32),
            jax.ShapeDtypeStruct((8, LANES), F32),
        ],
        scratch_shapes=[pltpu.VMEM((size + 8, width), F32), pltpu.VMEM((size + 8, width), F32)],
        compiler_params=params("arbitrary", "arbitrary"),
        cost_estimate=cost(n_micro * chunks, 1.0),
        name="mixer_grads",
    )(projected, projected, router, taps, par, solve, seen, news, state, d_mixed, d_news, d_state, d_gate)


def project_kernel(x_ref, gain_ref, weight_ref, router_weight_ref, normed_ref, out_ref, router_ref):
    per, _, n_tok, model = x_ref.shape
    x = x_ref[:, 0].reshape(per * n_tok, model).astype(F32)
    scale = lax.rsqrt(jnp.mean(x * x, axis=-1, keepdims=True) + EPS_NORM)
    normed = (x * scale * gain_ref[...]).astype(BF)
    normed_ref[0] = normed
    out_ref[0] = dot(normed, weight_ref[...]).astype(BF)
    router_ref[0] = dot(normed, router_weight_ref[...])


def project(x, gain, weight, router_weight, earlier=(), size=512):
    n_seq, n_micro, n_tok, model = x.shape
    length = n_seq * n_tok
    full = weight.shape[1]
    blocks = pl.BlockSpec((size // n_tok, 1, n_tok, model), lambda m, i: (i, m, 0, 0))
    rows = lambda n: pl.BlockSpec((1, size, n), lambda m, i: (m, i, 0))
    return launch(
        project_kernel,
        [blocks, whole((1, model)), whole(weight.shape), whole(router_weight.shape)],
        earlier,
        grid=(n_micro, length // size),
        out_specs=[rows(model), rows(full), rows(LANES)],
        out_shape=[
            jax.ShapeDtypeStruct((n_micro, length, model), BF),
            jax.ShapeDtypeStruct((n_micro, length, full), BF),
            jax.ShapeDtypeStruct((n_micro, length, LANES), F32),
        ],
        compiler_params=params("arbitrary", "arbitrary"),
        cost_estimate=cost(n_micro * length // CH, 0.35),
        name="project",
    )(x, gain[None], weight, router_weight)


def ring_add_kernel(table, ahead_ref, behind_ref, up_ref, low_ref, up_out, low_out):
    up_out[...] = (ahead_ref[...].astype(F32) + up_ref[0, 0].astype(F32)).astype(up_out.dtype)
    low_out[...] = (behind_ref[...].astype(F32) + low_ref[0, 0].astype(F32)).astype(low_out.dtype)


def ring_add(table, step, ahead, behind, parts, kind, earlier=()):
    rows, model = ahead.shape
    one = pl.BlockSpec((rows, model), lambda i, table: (0, 0))
    part = lambda m: pl.BlockSpec((1, 1, rows, model), lambda i, table: (m, table[2 * step + m], 0, 0))
    made = jax.ShapeDtypeStruct((rows, model), kind)
    n_in = 5

    def body(*refs):
        ring_add_kernel(*refs[:n_in], *refs[n_in + len(earlier) :])

    return pl.pallas_call(
        body,
        grid_spec=pltpu.PrefetchScalarGridSpec(
            num_scalar_prefetch=1,
            grid=(1,),
            in_specs=[one, one, part(0), part(1)] + [pl.BlockSpec(memory_space=pl.ANY)] * len(earlier),
            out_specs=[one, one],
        ),
        out_shape=[made, made],
        compiler_params=small_params("arbitrary"),
        cost_estimate=cost(1, 1.0),
        name="ring_add",
    )(table, ahead, behind, parts, parts, *earlier)


def input_grads_kernel(normed_ref, d_ext_ref, w_ext_ref, gain_ref, out_ref, lines_ref):
    total = dot(normed_ref[0], d_ext_ref[0], 0, 0)
    for m in range(1, normed_ref.shape[0]):
        total = total + dot(normed_ref[m], d_ext_ref[m], 0, 0)
    full = out_ref.shape[1]
    out_ref[...] = total[:, :full].astype(BF)
    norm = jnp.sum(total * w_ext_ref[...].astype(F32), axis=1, keepdims=True)
    lane = lax.broadcasted_iota(jnp.int32, (total.shape[0], LANES), 1)
    tail = jnp.where(lane == 3, norm, total[:, full:])
    lines = tail.T[:8]
    row = lax.broadcasted_iota(jnp.int32, lines.shape, 0)
    lines_ref[...] = jnp.where(row == 3, lines / gain_ref[...], lines)


def input_grads(normed, d_ext, w_ext, gain, full, earlier=(), size=256):
    n_micro, length, model = normed.shape
    wide = d_ext.shape[2]
    return launch(
        input_grads_kernel,
        [
            pl.BlockSpec((n_micro, length, size), lambda i: (0, 0, i)),
            whole(d_ext.shape),
            pl.BlockSpec((size, wide), lambda i: (i, 0)),
            pl.BlockSpec((1, size), lambda i: (0, i)),
        ],
        earlier,
        grid=(model // size,),
        out_specs=[
            pl.BlockSpec((size, full), lambda i: (i, 0)),
            pl.BlockSpec((8, size), lambda i: (0, i)),
        ],
        out_shape=[
            jax.ShapeDtypeStruct((model, full), BF),
            jax.ShapeDtypeStruct((8, model), F32),
        ],
        compiler_params=params("arbitrary"),
        cost_estimate=cost(1, 7.0),
        name="input_grads",
    )(normed, d_ext, w_ext, gain[None])


def place_heads_kernel(n_heads, copies, slots, cut, lines, where, *refs):
    parts, out_ref, small_ref = refs[:-2], refs[-2], refs[-1]
    for j, part in enumerate(parts):
        at = where[0] ^ j
        for slot in range(slots):
            for h in range(n_heads):
                to = (slot * n_heads + h) * LANES
                value = part[h * copies, :cut, slot * LANES : (slot + 1) * LANES]
                out_ref[at, :, to : to + LANES] = value.astype(F32)
        for s in range(part.shape[0]):
            high = part[s, cut : cut + lines].astype(F32)
            low = part[s, cut + lines : cut + 2 * lines].astype(F32)
            for r in range(len(parts)):

                @pl.when(at == r)
                def _(s=s, r=r, value=high + low):
                    small_ref[s, r * lines : (r + 1) * lines] = value


def place_heads(where, parts, n_heads, slots, cut, lines):
    n_seq, rows, full = parts[0].shape
    n_parts = len(parts)
    shape = (n_parts, cut, full * n_heads)
    small = (n_seq, n_parts * lines, full)
    grad, values = pl.pallas_call(
        partial(place_heads_kernel, n_heads, n_seq // n_heads, slots, cut, lines),
        grid_spec=pltpu.PrefetchScalarGridSpec(
            num_scalar_prefetch=1,
            grid=(1,),
            in_specs=[pl.BlockSpec(part.shape, lambda i, where: (0, 0, 0)) for part in parts],
            out_specs=[
                pl.BlockSpec(shape, lambda i, where: (0, 0, 0)),
                pl.BlockSpec(small, lambda i, where: (0, 0, 0)),
            ],
        ),
        out_shape=[jax.ShapeDtypeStruct(shape, F32), jax.ShapeDtypeStruct(small, F32)],
        compiler_params=small_params("arbitrary"),
        cost_estimate=cost(1, 3.0),
        name="place_heads",
    )(where, *parts)
    return grad.reshape(-1, full * n_heads), values


def pack_kernel(lines, own_ref, got_ref, small_ref, out_ref):
    n_seq, cut, full = own_ref.shape
    rows = out_ref.shape[1]
    tail = list(halves(small_ref[...]))
    if rows > cut + 2 * lines:
        tail.append(jnp.zeros((rows - cut - 2 * lines, full), BF))
    tail = jnp.concatenate(tail, axis=0)
    for s in range(n_seq):
        out_ref[s, :cut] = (own_ref[s].astype(F32) + got_ref[s].astype(F32)).astype(BF)
        out_ref[s, cut:] = tail


def pack(own, got, small, rows, earlier=()):
    n_seq, cut, full = own.shape
    return launch(
        partial(pack_kernel, small.shape[0]),
        [whole(own.shape), whole(got.shape), whole(small.shape)],
        earlier,
        grid=(1,),
        out_specs=whole((n_seq, rows, full)),
        out_shape=jax.ShapeDtypeStruct((n_seq, rows, full), BF),
        compiler_params=small_params("arbitrary"),
        cost_estimate=cost(1, 1.5),
        name="pack",
    )(own, got, small)


def place_units_kernel(unit_cut, unit_pad, n_seq, where, *refs):
    parts, out_ref = refs[:-1], refs[-1]
    n_row = len(parts)
    group = unit_cut * n_row
    hidden = group * n_seq
    for block in range(hidden // LANES):
        low = (block * LANES // group) * unit_pad // LANES * LANES
        high = ((block * LANES + LANES - 1) // group + 1) * unit_pad
        high = min(n_seq * unit_pad, -(-high // LANES) * LANES)
        col = lax.broadcasted_iota(jnp.int32, (high - low, LANES), 1) + block * LANES
        row = lax.broadcasted_iota(jnp.int32, (high - low, LANES), 0) + low
        inner = lax.rem(col, group)
        owner = lax.div(inner, unit_cut)
        unit = lax.div(col, group) * unit_pad + lax.rem(inner, unit_cut)
        total = [0.0, 0.0]
        for j, part in enumerate(parts):
            chosen = jnp.where((unit == row) & (owner == (where[0] ^ j)), 1.0, 0.0).astype(BF)
            for half in range(2):
                at = half * n_seq * unit_pad
                total[half] = total[half] + dot(part[:, at + low : at + high], chosen)
        for half in range(2):
            to = half * hidden + block * LANES
            out_ref[:, to : to + LANES] = total[half]


def place_units(where, parts, unit_cut, unit_pad, n_seq):
    rows = parts[0].shape[0]
    shape = (rows, 2 * unit_cut * n_seq * len(parts))
    return pl.pallas_call(
        partial(place_units_kernel, unit_cut, unit_pad, n_seq),
        grid_spec=pltpu.PrefetchScalarGridSpec(
            num_scalar_prefetch=1,
            grid=(1,),
            in_specs=[pl.BlockSpec(part.shape, lambda i, where: (0, 0)) for part in parts],
            out_specs=pl.BlockSpec(shape, lambda i, where: (0, 0)),
        ),
        out_shape=jax.ShapeDtypeStruct(shape, F32),
        compiler_params=small_params("arbitrary"),
        cost_estimate=cost(1, 5.0),
        name="place_units",
    )(where, *parts)


def place_rows_kernel(where, *refs):
    parts, out_ref = refs[:-1], refs[-1]
    for j, part in enumerate(parts):
        out_ref[where[0] ^ j] = part[...].astype(F32)


def place_down_kernel(unit_pad, left, where, *refs):
    parts, out_ref = refs[:-1], refs[-1]
    _, keep, model = out_ref.shape
    n_units = parts[0].shape[1] - left
    rest = model - n_units
    step = unit_pad * rest // n_units
    for j, part in enumerate(parts):
        at = where[0] ^ j
        out_ref[at, :, :n_units] = part[:keep, left:].astype(F32)
        for b in range(n_units // rest):
            have = min(step, keep - b * step)
            if have > 0:
                value = part[unit_pad : unit_pad + have, left + b * rest : left + (b + 1) * rest]
                out_ref[at, b * step : b * step + have, n_units:] = value.astype(F32)


def place_rows(where, parts, shape, kernel=place_rows_kernel):
    return pl.pallas_call(
        kernel,
        grid_spec=pltpu.PrefetchScalarGridSpec(
            num_scalar_prefetch=1,
            grid=(1,),
            in_specs=[pl.BlockSpec(part.shape, lambda i, where: (0, 0)) for part in parts],
            out_specs=pl.BlockSpec((len(parts),) + shape, lambda i, where: (0, 0, 0)),
        ),
        out_shape=jax.ShapeDtypeStruct((len(parts),) + shape, F32),
        compiler_params=small_params("arbitrary"),
        cost_estimate=cost(1, 2.0),
        name="place_rows",
    )(where, *parts).reshape(-1, shape[1])


def place_down(where, parts, unit_pad, left, shape):
    return place_rows(where, parts, shape, partial(place_down_kernel, unit_pad, left))


def feed_kernel(n_seq, n_parts, d_top_ref, w_ref, *refs):
    part_refs, (mid_ref, act_ref, d_gu_ref, down_ref), d_mid_refs = (
        refs[:-4 - n_parts], refs[-4 - n_parts : -n_parts], refs[-n_parts:]
    )
    per_step = len(part_refs) // n_parts
    n_tok = part_refs[0].shape[0]
    for j in range(n_parts):

        @pl.when(pl.program_id(0) == j)
        def _(j=j):
            for m in range(per_step):
                mid_ref[m * n_tok : (m + 1) * n_tok] = part_refs[j * per_step + m][...]

    n_units = act_ref.shape[1]
    model = mid_ref.shape[1]
    per = n_units // n_seq

    @pl.when(pl.program_id(0) == 0)
    def _():
        lines = w_ref[:, 2 * n_units :].reshape(n_seq, model // n_seq, n_units)
        rest = model - n_units
        step = per * rest // n_units
        for s in range(n_seq):
            down_ref[s * per : (s + 1) * per, :n_units] = lines[s, :per]
            for b in range(n_units // rest):
                at = s * per + b * step
                down_ref[at : at + step, n_units:] = lines[s, per:, b * rest : (b + 1) * rest]

    w_gate = w_ref[:, :n_units]
    w_up = w_ref[:, n_units : 2 * n_units]
    mid = mid_ref[...]
    gate = dot(mid, w_gate)
    up = dot(mid, w_up)
    d_act = dot(d_top_ref[...], down_ref[...], 1, 1)
    sig = jax.nn.sigmoid(gate)
    silu = gate * sig
    act_ref[...] = (silu * up).astype(BF)
    d_gate = (d_act * up * sig * (1.0 + gate * (1.0 - sig))).astype(BF)
    d_up = (d_act * silu).astype(BF)
    d_gu_ref[0] = d_gate
    d_gu_ref[1] = d_up
    d_mid = (dot(d_gate, w_gate, 1, 1) + dot(d_up, w_up, 1, 1)).astype(BF)
    for j, d_mid_ref in enumerate(d_mid_refs):

        @pl.when(pl.program_id(0) == j)
        def _(d_mid_ref=d_mid_ref):
            d_mid_ref[...] = d_mid


def feed(mid, d_top, weights, n_units, n_seq, n_parts):
    tokens, model = d_top.shape
    size = tokens // n_parts
    rows = lambda n: pl.BlockSpec((size, n), lambda i: (i, 0))
    return pl.pallas_call(
        partial(feed_kernel, n_seq, n_parts),
        grid=(n_parts,),
        in_specs=[rows(model), whole(weights.shape)] + [whole(part.shape) for part in mid],
        out_specs=[
            rows(model), rows(n_units), pl.BlockSpec((2, size, n_units), lambda i: (0, i, 0)),
            whole((n_units, model)),
        ] + [whole((size, model))] * n_parts,
        out_shape=[
            jax.ShapeDtypeStruct((tokens, model), BF),
            jax.ShapeDtypeStruct((tokens, n_units), BF),
            jax.ShapeDtypeStruct((2, tokens, n_units), BF),
            jax.ShapeDtypeStruct((n_units, model), BF),
        ] + [jax.ShapeDtypeStruct((size, model), BF)] * n_parts,
        compiler_params=params("arbitrary"),
        cost_estimate=cost(1, 14.0),
        name="feed",
    )(d_top, weights, *mid)


def times_kernel(left_ref, right_ref, *out_refs):
    value = dot(left_ref[...], right_ref[...]).astype(BF)
    for j, out_ref in enumerate(out_refs):

        @pl.when(pl.program_id(0) == j)
        def _(out_ref=out_ref):
            out_ref[...] = value


def times(left, right, n_parts, earlier=()):
    tokens, inner = left.shape
    size = tokens // n_parts
    return launch(
        times_kernel,
        [pl.BlockSpec((size, inner), lambda i: (i, 0)), whole(right.shape)],
        earlier,
        grid=(n_parts,),
        out_specs=[whole((size, right.shape[1]))] * n_parts,
        out_shape=[jax.ShapeDtypeStruct((size, right.shape[1]), BF)] * n_parts,
        compiler_params=small_params("arbitrary"),
        cost_estimate=cost(1, 3.0),
        name="times",
    )(left, right)


def feed_grads(mid, d_gu, g_down, n_seq, earlier=(), size=256):
    tokens, model = mid.shape
    n_units = d_gu.shape[2]
    shard, unit_pad = model // n_seq, n_units // n_seq
    per = size // shard

    def body(mid_ref, d_gu_ref, g_down_ref, out_ref):
        mid = mid_ref[...]
        for half in range(2):
            value = dot(mid, d_gu_ref[half], 0, 0).astype(BF)
            out_ref[:, half * n_units : (half + 1) * n_units] = value
        rest = model - n_units
        step = unit_pad * rest // n_units
        for part in range(per):
            at, rows = part * shard, g_down_ref[part * unit_pad : (part + 1) * unit_pad]
            out_ref[at : at + unit_pad, 2 * n_units :] = rows[:, :n_units]
            for b in range(n_units // rest):
                to = 2 * n_units + b * rest
                out_ref[at + unit_pad : at + shard, to : to + rest] = rows[
                    b * step : (b + 1) * step, n_units:
                ]

    return launch(
        body,
        [
            pl.BlockSpec((tokens, size), lambda i: (0, i)), whole(d_gu.shape),
            pl.BlockSpec((per * unit_pad, model), lambda i: (i, 0)),
        ],
        earlier,
        grid=(model // size,),
        out_specs=pl.BlockSpec((size, 3 * n_units), lambda i: (i, 0)),
        out_shape=jax.ShapeDtypeStruct((model, 3 * n_units), BF),
        compiler_params=params("arbitrary"),
        cost_estimate=cost(1, 7.0),
        name="feed_grads",
    )(mid, d_gu, g_down)


def place_pieces_kernel(order, where, *refs):
    parts, out_ref = refs[:-1], refs[-1]
    for j, part in enumerate(parts):
        for n in range(part.shape[0]):
            at = n if order is None else where[1] ^ order[n]
            out_ref[at, where[0] ^ j] = part[n]


def place_pieces(where, parts, order=None):
    n_seq, cut, width = parts[0].shape
    shape = (n_seq, len(parts), cut, width)
    return pl.pallas_call(
        partial(place_pieces_kernel, order),
        grid_spec=pltpu.PrefetchScalarGridSpec(
            num_scalar_prefetch=1,
            grid=(1,),
            in_specs=[pl.BlockSpec(part.shape, lambda i, where: (0, 0, 0)) for part in parts],
            out_specs=pl.BlockSpec(shape, lambda i, where: (0, 0, 0, 0)),
        ),
        out_shape=jax.ShapeDtypeStruct(shape, BF),
        compiler_params=small_params("arbitrary"),
        cost_estimate=cost(1, 2.0),
        name="place_pieces",
    )(where, *parts).reshape(-1, width)


def middle_kernel(copies, gated_ref, x_ref, w_ref, gain_ref, residual_ref, normed_ref, gated_out_ref):
    n_heads = gated_ref.shape[0] // copies
    total = x_ref[0].astype(F32)
    for h in range(n_heads):
        part = gated_ref[h * copies, 0]
        gated_out_ref[0, :, h * LANES : (h + 1) * LANES] = part
        total = total + dot(part, w_ref[h * LANES : (h + 1) * LANES])
    scale = lax.rsqrt(jnp.mean(total * total, axis=-1, keepdims=True) + EPS_NORM)
    residual_ref[0] = total
    normed_ref[0] = (total * scale * gain_ref[...]).astype(BF)


def middle(at, gated, x, w_out, gain, copies):
    _, n_tok, model = x.shape
    n_seq = gated.shape[0]
    rows = pl.BlockSpec((1, n_tok, model), lambda i: (0, 0, 0))
    made = lambda kind: jax.ShapeDtypeStruct((1, n_tok, model), kind)
    return pl.pallas_call(
        partial(middle_kernel, copies),
        grid=(1,),
        in_specs=[
            pl.BlockSpec((n_seq, 1, n_tok, LANES), lambda i: (0, 0, 0, 0)),
            pl.BlockSpec((1, n_tok, model), lambda i: (at, 0, 0)),
            whole(w_out.shape), whole((1, model)),
        ],
        out_specs=[rows] * 3,
        out_shape=[made(F32), made(BF), made(BF)],
        compiler_params=small_params("arbitrary"),
        cost_estimate=cost(1, 2.0),
        name="middle",
    )(gated, x, w_out, gain[None])


def input_back_kernel(d_ext_ref, w_ref, out_ref):
    value = dot(d_ext_ref[0], w_ref[...], 1, 1).astype(BF)
    per, _, n_tok, _ = out_ref.shape
    for part in range(per):
        out_ref[part, 0] = value[part * n_tok : (part + 1) * n_tok]


def input_back(d_ext, w_ext, n_tok, size=512):
    n_micro, length, wide = d_ext.shape
    model = w_ext.shape[0]
    per = size // n_tok
    return pl.pallas_call(
        input_back_kernel,
        grid=(n_micro, length // size),
        in_specs=[pl.BlockSpec((1, size, wide), lambda m, s: (m, s, 0)), whole(w_ext.shape)],
        out_specs=pl.BlockSpec((per, 1, n_tok, model), lambda m, s: (s, m, 0, 0)),
        out_shape=jax.ShapeDtypeStruct((length // n_tok, n_micro, n_tok, model), BF),
        compiler_params=params("arbitrary", "arbitrary"),
        cost_estimate=cost(1, 7.0),
        name="input_back",
    )(d_ext, w_ext)


def bottom_kernel(d_in_ref, d_residual_ref, x_ref, gain_ref, out_ref):
    x = x_ref[0].astype(F32)
    scale = lax.rsqrt(jnp.mean(x * x, axis=-1, keepdims=True) + EPS_NORM)
    d_normed = d_in_ref[...].astype(F32) * gain_ref[...]
    out_ref[0] = (
        d_residual_ref[...]
        + scale * d_normed
        - x * scale**3 * jnp.mean(d_normed * x, axis=-1, keepdims=True)
    )


def bottom(d_in, d_residual, x, gain, earlier=()):
    n_micro, n_tok, model = x.shape
    rows = pl.BlockSpec((n_tok, model), lambda m: (m, 0))
    block = pl.BlockSpec((1, n_tok, model), lambda m: (m, 0, 0))
    return launch(
        bottom_kernel,
        [rows, rows, block, whole((1, model))],
        earlier,
        grid=(n_micro,),
        out_specs=block,
        out_shape=jax.ShapeDtypeStruct((n_micro, n_tok, model), F32),
        compiler_params=small_params("arbitrary"),
        cost_estimate=cost(1, 2.0),
        name="bottom",
    )(d_in, d_residual, x, gain[None])


def turn_kernel(
    own_ref, got_ref, d_top_ref, residual_ref, w_ref, gain_ref, d_residual_ref, d_low_ref, d_sent_ref, norm_ref
):
    @pl.when(pl.program_id(0) == 0)
    def _():
        norm_ref[...] = jnp.zeros_like(norm_ref)

    residual = residual_ref[...]
    scale = lax.rsqrt(jnp.mean(residual * residual, axis=-1, keepdims=True) + EPS_NORM)
    d_mid = own_ref[...].astype(F32) + got_ref[...].astype(F32)
    norm_ref[0:1, :] += jnp.sum(d_mid * residual * scale, axis=0, keepdims=True)
    d_normed = d_mid * gain_ref[...]
    d_residual = (
        d_top_ref[...]
        + scale * d_normed
        - residual * scale**3 * jnp.mean(d_normed * residual, axis=-1, keepdims=True)
    )
    d_residual_ref[...] = d_residual
    d_low = d_residual.astype(BF)
    d_low_ref[...] = d_low
    d_gated = dot(d_low, w_ref[...], 1, 1).astype(BF)
    for h in range(d_sent_ref.shape[0]):
        d_sent_ref[h, 0] = d_gated[:, h * LANES : (h + 1) * LANES]


def turn(own, got, d_top, residual, w_out, gain, n_micro):
    tokens, model = own.shape
    n_tok = tokens // n_micro
    n_heads = model // LANES
    rows = pl.BlockSpec((n_tok, model), lambda m: (m, 0))
    return pl.pallas_call(
        turn_kernel,
        grid=(n_micro,),
        in_specs=[rows, rows, rows, rows, whole(w_out.shape), whole((1, model))],
        out_specs=[
            rows, rows,
            pl.BlockSpec((n_heads, 1, n_tok, LANES), lambda m: (0, m, 0, 0)),
            whole((8, model)),
        ],
        out_shape=[
            jax.ShapeDtypeStruct((tokens, model), F32),
            jax.ShapeDtypeStruct((tokens, model), BF),
            jax.ShapeDtypeStruct((n_heads, n_micro, n_tok, LANES), BF),
            jax.ShapeDtypeStruct((8, model), F32),
        ],
        compiler_params=small_params("arbitrary"),
        cost_estimate=cost(1, 5.0),
        name="turn",
    )(own, got, d_top, residual, w_out, gain[None])


def pick(stacked, at, axis=0):
    return lax.dynamic_index_in_dim(stacked, at, axis, False, allow_negative_indices=False)


def exchange(value, axis, bit):
    count = lax.axis_size(axis)
    return lax.ppermute(value, axis, [(i, i ^ bit) for i in range(count)])


def bits(axis):
    count = lax.axis_size(axis)
    return [1 << b for b in range(count.bit_length() - 1)]


def row_gather(value):
    parts = {0: value}
    for bit in reversed(bits("row")):
        parts.update({j ^ bit: exchange(part, "row", bit) for j, part in parts.items()})
    return [parts[j] for j in range(len(parts))]


def row_gather_steps(value):
    parts = {0: value}
    for bit in reversed(bits("row")):
        got = {j ^ bit: exchange(part, "row", bit) for j, part in parts.items()}
        parts.update(got)
        earlier = yield list(got.values())
        if earlier:
            parts = {j: fence(part, *earlier) for j, part in parts.items()}
    return [parts[j] for j in range(len(parts))]


def seq_scatter_steps(parts):
    mine = lax.axis_index("seq")
    for bit in reversed(bits("seq")):
        parts = parts.reshape((2, bit) + parts.shape[1:])
        side = (mine & bit) // bit
        got = exchange(pick(parts, 1 - side).astype(BF), "seq", bit)
        yield got
        parts = pick(parts, side).astype(F32) + got.astype(F32)
    return parts[0].astype(BF)


def seq_gather_steps(value):
    parts, order = value[None], [0]
    for n, bit in enumerate(reversed(bits("seq"))):
        parts = jnp.concatenate([parts, exchange(parts, "seq", bit)], axis=0)
        order = order + [place ^ bit for place in order]
        if n + 1 < len(bits("seq")):
            sent = yield parts
            parts = parts if sent is None else sent
    return parts, order


def finish(steps, value=None):
    try:
        steps.send(value)
        while True:
            next(steps)
    except StopIteration as end:
        return end.value


def row_scatter_halves(parts):
    parts = dict(enumerate(parts))
    for bit in bits("row"):
        got = {j ^ bit: exchange(parts[j].astype(BF), "row", bit) for j in parts if j & bit}
        if len(got) == 1:
            return parts[0], got[0]
        parts = {j: parts[j].astype(F32) + part.astype(F32) for j, part in got.items()}


def ring():
    count, mine = lax.axis_size("seq"), lax.axis_index("seq")
    order = list(range(0, count, 2)) + list(range(1, count, 2))[::-1]
    half = mine >> 1
    place = jnp.where((mine & 1) == 0, half, count - 1 - half)

    def owner(k):
        at = (place + (k % count)) & (count - 1)
        return jnp.where(at < count // 2, 2 * at, 2 * count - 1 - 2 * at)

    ahead = [(order[i], order[(i + 1) % count]) for i in range(count)]
    behind = [(b, a) for a, b in ahead]
    return count, owner, ahead, behind


def ring_gather(value, earlier):
    count, owner, ahead, behind = ring()
    blocks = jnp.zeros((count,) + value.shape, value.dtype)
    put = lambda blocks, block, k: lax.dynamic_update_index_in_dim(
        blocks, block, owner(k), 0, allow_negative_indices=False
    )
    blocks = put(blocks, value, 0)
    there, back = value, value
    for k in range(1, count // 2):
        there = lax.ppermute(there, "seq", ahead)
        back = lax.ppermute(back, "seq", behind)
        if k in earlier:
            there = fence(there, *earlier[k])
        blocks = put(put(blocks, there, -k), back, k)
    cut = value.shape[1] // 2
    there = lax.ppermute(there[:, :cut], "seq", ahead)
    back = lax.ppermute(back[:, cut:], "seq", behind)
    return put(blocks, jnp.concatenate([there, back], axis=1), count // 2)


def matmul(spec, left, right, kind=F32):
    return jnp.einsum(spec, left, right, preferred_element_type=F32).astype(kind)


def local(
    tokens,
    cotangent,
    row_lengths,
    norm1_gain,
    w_in,
    w_router,
    conv_weight,
    a_log,
    dt_bias,
    head_gain,
    w_out,
    norm2_gain,
    w_gu,
    w_down,
):
    n_seq, n_row = lax.axis_size("seq"), lax.axis_size("row")
    seq, row = lax.axis_index("seq"), lax.axis_index("row")
    n_micro, _, n_tok, model = tokens.shape
    micros = list(range(n_micro))
    n_heads = a_log.shape[0]
    head_dim = head_gain.shape[0]
    n_taps, conv_width = conv_weight.shape
    slots = w_in.shape[1] // (n_heads * head_dim)
    width = conv_width // n_heads
    full = slots * head_dim
    length = n_tok * n_seq
    copies = n_seq // n_heads
    head = seq // copies
    gate_at = slots - 1

    def to_heads(value):
        return lax.all_to_all(jnp.repeat(value, copies, axis=0), "seq", 0, 0, tiled=True)

    def seq_parts(value):
        return lax.all_to_all(value, "seq", 0, 0, tiled=True)

    def from_heads(value):
        got = lax.all_to_all(value, "seq", 0, 0, tiled=True)
        return got if copies == 1 else got[::copies]

    def in_order(parts, axis):
        stacked = jnp.stack(parts)
        return jnp.concatenate([pick(stacked, row ^ j) for j in range(n_row)], axis=axis)

    where = jnp.stack([row, seq]).astype(jnp.int32)

    cut = w_in.shape[0] // n_row
    w_piece = pick(w_in.reshape(n_row, cut, slots, n_heads, head_dim), row)
    w_got = to_heads(w_piece.transpose(2, 0, 1, 3).reshape(n_heads, cut, full))
    w_head = place_pieces(where, row_gather(w_got))
    w_rt = pick(w_router.reshape(model, -1, n_heads), head, 2)
    n_rt = w_rt.shape[1]
    w_rt = jnp.pad(w_rt, ((0, 0), (0, LANES - n_rt)))
    w_ext = jnp.concatenate([w_head, w_rt], axis=1)
    taps = pick(conv_weight.reshape(n_taps, gate_at, n_heads, head_dim), head, 2)
    taps = jnp.pad(taps.reshape(n_taps, width), ((0, 8 - n_taps), (0, 0)))
    par = jnp.concatenate(
        [
            head_gain[None],
            jnp.broadcast_to(lax.dynamic_index_in_dim(a_log, head, 0), (1, LANES)),
            jnp.broadcast_to(lax.dynamic_index_in_dim(dt_bias, head, 0), (1, LANES)),
            jnp.zeros((5, LANES), F32),
        ]
    )
    position = seq * n_tok + jnp.arange(n_tok, dtype=jnp.int32)
    live = (position[None, :] < row_lengths[:, :1]).astype(F32)[:, :, None]
    d_top = (cotangent[:, 0].astype(F32) * live).reshape(-1, model)
    d_rows = jnp.concatenate(row_gather(d_top.astype(BF)), axis=0)

    out_cut = w_out.shape[0] // n_row
    out_piece = lax.dynamic_slice_in_dim(w_out, row * out_cut, out_cut, 0)
    out_steps = seq_gather_steps(out_piece)
    out_got = next(out_steps)

    x_all = ring_gather(
        tokens[:, 0], {n_seq // 4: [w_got], n_seq // 2 - 1: [w_ext, w_rt, taps, par, d_rows, out_got]}
    )

    shard = w_out.shape[0]
    hidden = w_gu.shape[1] // 2
    unit_cut = hidden // n_seq // n_row
    unit_pad = -(-unit_cut // 16) * 16
    n_units = unit_pad * n_seq
    gu_piece = pick(w_gu.reshape(shard, 2, n_seq, n_row, unit_cut), row, 3)
    gu_piece = jnp.pad(gu_piece, ((0, 0), (0, 0), (0, 0), (0, unit_pad - unit_cut)))
    down_piece = lax.dynamic_slice_in_dim(w_down, row * unit_cut, unit_cut, 0)
    down_piece = jnp.pad(down_piece, ((0, unit_pad - unit_cut), (0, 0)))
    beside = down_piece[:, n_units:]
    beside = beside.reshape(n_units // beside.shape[1], -1, beside.shape[1])
    beside = jnp.concatenate(list(beside), axis=1)
    down_piece = jnp.concatenate([down_piece[:, :n_units], beside])
    weights = jnp.concatenate([gu_piece.reshape(shard, -1), down_piece], axis=1)
    weights = fence(weights, x_all)
    weights_all = lax.all_gather(weights, "seq", axis=0, tiled=True)

    normed_in, projected, router = project(x_all, norm1_gain, w_head, w_rt, [d_rows, weights])
    out_got = out_steps.send(fence(out_got, projected))
    prep, kept, sent = (), (), []
    for m in micros:
        prep = prepare(m, projected, router, taps, par, width, prep)
        if m == 0:
            out_got, order = finish(out_steps, fence(out_got, prep[0]))
        gated, *kept = scan_states(
            m, prep, router, projected, par, gate_at, n_tok, kept, sent[-1:]
        )
        sent.append(seq_parts(gated))
        if m == 0:
            full_out = place_pieces(where, row_gather(fence(out_got, gated)), order)

    middles = [middle(m, sent[m], tokens[:, 0], full_out, norm2_gain, copies) for m in micros]
    mid_rows = zip(*[row_gather(normed_mid[0]) for _, normed_mid, _ in middles])
    mid_rows = [part for parts in mid_rows for part in parts]
    residual = jnp.concatenate([value[0][0] for value in middles], axis=0)
    gated = jnp.concatenate([value[2][0] for value in middles], axis=0)
    mid_rows, act, d_gu, down, *d_mid = feed(
        mid_rows, d_rows, weights_all, n_units, n_seq, n_row
    )
    g_down = matmul("tf,td->fd", act, d_rows, BF)
    g_feed = feed_grads(mid_rows, d_gu, g_down, n_seq)
    g_feed_sum = lax.psum_scatter(g_feed, "seq", scatter_dimension=0, tiled=True)
    d_mid_own, d_mid_got = row_scatter_halves(d_mid)

    def row_parts(value, axis):
        return [pick(value, row ^ j, axis) for j in range(n_row)]

    d_residual, d_low, d_sent, g_norm2 = turn(
        d_mid_own, fence(d_mid_got, g_feed), d_top, residual, full_out, norm2_gain, n_micro
    )
    d_gated = to_heads(d_sent)

    mlp = times(act, down, n_row, [d_sent])
    out_halves = row_scatter_halves(mlp)
    g_out_full = matmul("tc,td->cd", fence(gated, d_sent), d_low)
    g_out = g_out_full
    g_out = row_scatter_halves(row_parts(g_out.reshape(n_seq, n_row, out_cut, model), 1))

    mixed, news, state = kept
    d_mixed, d_news, d_state, d_gate_pre, g_head = scan_back(
        prep, router, projected, par, gate_at, mixed, d_gated
    )
    d_ext, g_taps, g_par = mixer_grads(
        prep, router, projected, taps, par, width,
        news, state, d_mixed, d_news, d_state, d_gate_pre, [g_out[1], out_halves[1]],
    )
    if copies > 1:
        mine = (seq % copies == 0).astype(F32)
        d_ext = d_ext * mine.astype(BF)
        g_taps, g_par, g_head = g_taps * mine, g_par * mine, g_head * mine
    d_in_part = input_back(d_ext, w_ext, n_tok).reshape(-1, model)
    d_in = lax.psum_scatter(d_in_part, "seq", scatter_dimension=0, tiled=True)
    g_in, in_lines = input_grads(normed_in, d_ext, w_ext, norm1_gain, full, [d_in_part])
    fill = lambda value: jnp.pad(value, ((0, 0), (0, full - value.shape[1])))
    scalars = jnp.concatenate([g_head[:1], g_par[1:2], g_par[2:3]], axis=1)
    vectors = jnp.concatenate([in_lines[: n_rt + 1], g_norm2[:1]]).reshape(-1, model // 2)
    small = jnp.concatenate([fill(vectors), fill(scalars), fill(g_taps[:n_taps])])
    n_vec = vectors.shape[0]
    lines = -(-small.shape[0] // n_row)
    small = jnp.pad(small, ((0, n_row * lines - small.shape[0]), (0, 0))).reshape(n_row, lines, full)

    g_out = g_out[0].astype(F32) + fence(g_out[1], d_in_part).astype(F32)
    g_out_steps = seq_scatter_steps(g_out)
    moment = next(g_out_steps)
    parts = row_parts(g_in.reshape(n_seq, n_row, cut, full), 1)
    parts = {j: fence(part, moment) if j & 1 else part for j, part in enumerate(parts)}
    smalls = dict(enumerate(row_parts(small, 0)))
    for bit in bits("row"):
        got = {j ^ bit: exchange(parts[j], "row", bit) for j in parts if j & bit}
        got_small = {j ^ bit: exchange(smalls[j], "row", bit) for j in smalls if j & bit}
        smalls = {j: smalls[j] + part for j, part in got_small.items()}
        if len(got) > 1:
            parts = {
                j: (parts[j].astype(F32) + part.astype(F32)).astype(BF) for j, part in got.items()
            }
    rows = cut + -(-2 * lines // 16) * 16
    g_in_got = seq_parts(pack(parts[0], got[0], smalls[0], rows, [next(g_out_steps)]))
    feed_steps = row_gather_steps(fence(g_feed_sum, got[0]))
    g_in_got = fence(g_in_got, *next(feed_steps), next(g_out_steps))
    in_steps = row_gather_steps(g_in_got)
    first_in = next(in_steps)
    g_out_sum = finish(g_out_steps)
    g_feed_all = finish(feed_steps)
    g_out_all = row_gather(g_out_sum)
    grad_out = place_rows(where, g_out_all, (out_cut, model))
    grad_down = place_down(where, g_feed_all, unit_pad, 2 * n_units, (unit_cut, model))
    grad_gu = place_units(where, g_feed_all, unit_cut, unit_pad, n_seq)
    g_in_all = finish(in_steps, [grad_gu, grad_down])
    grad_in, small = place_heads(where, g_in_all, n_heads, slots, cut, lines)
    before = [grad_in, grad_gu, grad_down, grad_out]
    grad_tokens = bottom(d_in, d_residual, tokens[:, 0], norm1_gain, before)[:, None]
    out = residual + out_halves[0].astype(F32) + out_halves[1].astype(F32)
    out = out.astype(BF).reshape(n_micro, 1, n_tok, model)
    total = jnp.sum(small[:, 2 * n_rt : n_vec + 1], axis=0)
    norms = total[:4, : model // 2].reshape(2, model)
    heads = small[::copies]
    conv_sum = heads[:, n_vec + 1 : n_vec + 1 + n_taps, :width]
    conv_sum = conv_sum.reshape(n_heads, n_taps, gate_at, head_dim)
    conv_sum = conv_sum.transpose(1, 2, 0, 3).reshape(n_taps, conv_width)
    router_sum = heads[:, : 2 * n_rt, : model // 2].reshape(n_heads, n_rt, model)
    router_sum = router_sum.transpose(2, 1, 0).reshape(model, n_rt * n_heads)
    return (
        out,
        grad_tokens,
        norms[0],
        grad_in,
        router_sum,
        conv_sum,
        heads[:, n_vec, LANES + 2],
        heads[:, n_vec, 2 * LANES + 2],
        total[4, :head_dim],
        grad_out,
        norms[1],
        grad_gu,
        grad_down,
    )


def solution(mesh):
    by_rows = P("seq", None)
    by_tokens = P(None, "row", "seq", None)
    return jax.shard_map(
        local,
        mesh=mesh,
        in_specs=(
            by_tokens, by_tokens, P(None, "row"), P(), by_rows, P(), P(), P(), P(), P(),
            by_rows, P(), by_rows, by_rows,
        ),
        out_specs=(
            by_tokens, by_tokens, P(), by_rows, P(), P(), P(), P(), P(),
            by_rows, P(), by_rows, by_rows,
        ),
        check_vma=False,
    )
```

```python
from functools import partial

import jax
import jax.numpy as jnp
from jax import lax
from jax.experimental import pallas as pl
from jax.experimental.pallas import tpu as pltpu
from jax.sharding import PartitionSpec as P

BF = jnp.bfloat16
F32 = jnp.float32
EPS_NORM = 1e-05
EPS_UNIT = 1e-06
CH = 64
ST = 128
HALO = 16
LANES = 128
VMEM_BYTES = 60 * 1024 * 1024
SMALL_BYTES = 50 * 1024 * 1024


def halves(value):
    high = value.astype(BF)
    return (high, (value - high.astype(F32)).astype(BF))


def dot(left, right, over_left=1, over_right=0):
    return lax.dot_general(
        left, right, (((over_left,), (over_right,)), ((), ())), preferred_element_type=F32
    )


def mm(left, right, over_left=1, over_right=0):
    left = left if isinstance(left, tuple) else (left,)
    right = right if isinstance(right, tuple) else (right,)
    total = dot(left[0], right[0], over_left, over_right)
    if len(right) > 1:
        total = total + dot(left[0], right[1], over_left, over_right)
    if len(left) > 1:
        total = total + dot(left[1], right[0], over_left, over_right)
    return total


def exact_sum(ones, value):
    high = value.astype(BF)
    rest = value - high.astype(F32)
    mid = rest.astype(BF)
    low = (rest - mid.astype(F32)).astype(BF)
    return dot(ones, high) + dot(ones, mid) + dot(ones, low)


def step_orders():
    row = lax.broadcasted_iota(jnp.int32, (ST, ST), 0)
    col = lax.broadcasted_iota(jnp.int32, (ST, ST), 1)
    order = lambda i: 2 * (i & (CH - 1)) + (i >> 6)
    return order(row), order(col)


def sees():
    row = lax.broadcasted_iota(jnp.int32, (CH, ST), 0)
    col = lax.broadcasted_iota(jnp.int32, (CH, ST), 1)
    return (col & (CH - 1)) <= row


def twice(value):
    return jnp.concatenate([value, value], axis=0)


def log_decays(router, par):
    lane = lax.broadcasted_iota(jnp.int32, (CH, LANES), 1)
    pre = router + par[2:3]
    soft = jnp.maximum(pre, 0.0) + jnp.log1p(jnp.exp(-jnp.abs(pre)))
    decay = -jnp.exp(par[1:2]) * soft
    row = lax.broadcasted_iota(jnp.int32, (CH, CH), 0)
    col = lax.broadcasted_iota(jnp.int32, (CH, CH), 1)
    below = jnp.where(col <= row, 1.0, 0.0).astype(BF)
    total = exact_sum(below, jnp.where(lane == 2, decay, 0.0))
    return decay, total


def gate_columns(router, par):
    strength = jax.nn.sigmoid(router)
    decay, total = log_decays(router, par)
    beta = jnp.concatenate([strength[:, 0:1], strength[:, 1:2]], axis=0)
    doubled = twice(total)
    g_col = doubled[:, 2:3]
    g_row = doubled.T[2:3, :]
    g_last = total[CH - 1 : CH, 2:3]
    return beta, g_col, g_row, g_last, decay


def seen_decay(g_col, g_row, visible):
    return jnp.where(visible, jnp.exp(jnp.where(visible, g_col[:CH] - g_row, 0.0)), 0.0)


def unit(value):
    scale = lax.rsqrt(jnp.sum(value * value, axis=-1, keepdims=True) + EPS_UNIT)
    return value * scale, scale


def taps_sum(window, weight, start):
    total = weight[0:1] * window[pl.ds(start + 5, CH), :]
    for tap in range(1, 4):
        total = total + weight[tap : tap + 1] * window[pl.ds(start + 5 + tap, CH), :]
    return total


def fill_window(window, proj_ref, halo_ref, is_first):
    width = window.shape[1]
    edge = halo_ref[0, :, :width].astype(F32)[HALO - 8 :]
    window[0:8, :] = jnp.where(is_first, 0.0, edge)
    window[8:, :] = proj_ref[0, :, :width].astype(F32)


def prep_kernel(
    count, proj_ref, halo_ref, router_ref, taps_ref, par_ref,
    solve_ref, wmat_ref, umat_ref, seen_ref, q_ref, k_ref, window,
):
    fill_window(window, proj_ref, halo_ref, pl.program_id(0) == 0)
    weight = taps_ref[...]
    par = par_ref[...]
    o_row, o_col = step_orders()
    strict = o_row > o_col
    eye = jnp.where(o_row == o_col, 1.0, 0.0)
    visible = sees()
    many = range(count)
    lower, rights = [], []
    for n in many:
        conv = taps_sum(window, weight, n * CH)
        act = conv * jax.nn.sigmoid(conv)
        q = unit(act[:, 0:128])[0].astype(BF)
        k = jnp.concatenate(
            [unit(act[:, 128:256])[0], unit(act[:, 256:384])[0]], axis=0
        ).astype(BF)
        v = jnp.concatenate([act[:, 384:512], act[:, 512:640]], axis=0).astype(BF)
        beta, g_col, g_row, _, _ = gate_columns(
            router_ref[0, n * CH : (n + 1) * CH, :], par
        )
        gaps = seen_decay(g_col, g_row, visible)
        lower.append(jnp.where(strict, beta * twice(gaps) * dot(k, k, 1, 1), 0.0))
        kf = k.astype(F32)
        rights.append(
            jnp.concatenate([beta * jnp.exp(g_col) * kf, beta * v.astype(F32)], axis=1)
        )
        seen_ref[0, n] = gaps * dot(q, k, 1, 1)
        q_ref[0, n] = q
        k_ref[0, n] = k
    inverse = [eye - jnp.where((o_row >> 1) == (o_col >> 1), part, 0.0) for part in lower]
    for level in range(1, 7):
        at = ((o_row >> level) ^ (o_col >> level)) == 1
        parts = [halves(jnp.where(at, part, 0.0)) for part in lower]
        known = [halves(value) for value in inverse]
        inner = [halves(mm(parts[n], known[n])) for n in many]
        inverse = [inverse[n] - mm(known[n], inner[n]) for n in many]
    for n in many:
        solve_ref[0, n] = inverse[n]
        both = mm(halves(inverse[n]), halves(rights[n]))
        wmat_ref[0, n] = both[:, :128]
        umat_ref[0, n] = both[:, 128:]


def head_norm(mixed):
    return lax.rsqrt(jnp.mean(mixed * mixed, axis=-1, keepdims=True) + EPS_NORM)


def scan_kernel(
    n_micro, count, wmat_ref, umat_ref, seen_ref, q_ref, k_ref, router_ref, gate_ref, par_ref,
    out_ref, mixed_ref, news_ref, state_ref, state,
):
    @pl.when(pl.program_id(0) == 0)
    def _():
        state[...] = jnp.zeros_like(state)

    par = par_ref[...]
    now = [state[m] for m in range(n_micro)]
    for n in range(count):
        rows = slice(n * CH, (n + 1) * CH)
        for m in range(n_micro):
            _, g_col, _, g_last, _ = gate_columns(router_ref[m, rows, :], par)
            held = halves(now[m])
            state_ref[m, n] = now[m]
            news = umat_ref[m, n] - mm(halves(wmat_ref[m, n]), held)
            news_ref[m, n] = news
            news_h = halves(news)
            ends = halves(jnp.exp(g_last - g_col) * k_ref[m, n].astype(F32))
            now[m] = jnp.exp(g_last) * now[m] + mm(ends, news_h, 0, 0)
            mixed = jnp.exp(g_col[:CH]) * mm(q_ref[m, n], held) + mm(halves(seen_ref[m, n]), news_h)
            mixed_ref[m, n] = mixed
            gate = gate_ref[m, rows, :].astype(F32)
            tok = out_ref.shape[2]
            at = slice(n * CH % tok, n * CH % tok + CH)
            out_ref[n * CH // tok, m, at, :] = (
                mixed * head_norm(mixed) * par[0:1] * (gate * jax.nn.sigmoid(gate))
            ).astype(BF)
    for m in range(n_micro):
        state[m] = now[m]


def scan_back_kernel(
    n_micro, count, wmat_ref, seen_ref, q_ref, k_ref, router_ref, gate_ref, par_ref, mixed_ref, d_out_ref,
    d_mixed_ref, d_news_ref, d_state_ref, d_gate_ref, gain_ref, state,
):
    @pl.when(pl.program_id(0) == 0)
    def _():
        state[...] = jnp.zeros_like(state)
        gain_ref[...] = jnp.zeros_like(gain_ref)

    par = par_ref[...]
    now = [state[m] for m in range(n_micro)]
    gain = jnp.zeros((1, LANES), F32)
    for n in reversed(range(count)):
        rows = slice(n * CH, (n + 1) * CH)
        for m in range(n_micro):
            _, g_col, _, g_last, _ = gate_columns(router_ref[m, rows, :], par)
            mixed = mixed_ref[m, n]
            gate = gate_ref[m, rows, :].astype(F32)
            tok = d_out_ref.shape[2]
            at = slice(n * CH % tok, n * CH % tok + CH)
            d_out = d_out_ref[n * CH // tok, m, at, :].astype(F32)
            scale = head_norm(mixed)
            normed = mixed * scale
            sig = jax.nn.sigmoid(gate)
            silu = gate * sig
            gain = gain + jnp.sum(d_out * normed * silu, axis=0, keepdims=True)
            d_gate = d_out * normed * par[0:1] * (sig * (1.0 + gate * (1.0 - sig)))
            d_gate_ref[m, rows, :] = d_gate.astype(BF)
            d_normed = d_out * par[0:1] * silu
            d_mixed = scale * d_normed - mixed * scale**3 * jnp.mean(
                d_normed * mixed, axis=-1, keepdims=True
            )
            d_mixed_ref[m, n] = d_mixed
            d_mixed_h = halves(d_mixed)
            d_state_ref[m, n] = now[m]
            ends = halves(jnp.exp(g_last - g_col) * k_ref[m, n].astype(F32))
            d_news = mm(halves(seen_ref[m, n]), d_mixed_h, 0, 0) + mm(ends, halves(now[m]))
            d_news_ref[m, n] = d_news
            q_eff = halves(jnp.exp(g_col[:CH]) * q_ref[m, n].astype(F32))
            now[m] = (
                jnp.exp(g_last) * now[m]
                + mm(q_eff, d_mixed_h, 0, 0)
                - mm(halves(wmat_ref[m, n]), halves(d_news), 0, 0)
            )
    gain_ref[0:1, :] += gain
    for m in range(n_micro):
        state[m] = now[m]


def in_step(chains):
    while chains:
        chains = [chain for chain in chains if next(chain, chain) is not chain]


def unit_back(grad, value, scale):
    return scale * grad - value * scale**3 * jnp.sum(grad * value, axis=-1, keepdims=True)


def grads_kernel(
    count, proj_ref, halo_ref, router_ref, taps_ref, par_ref, solve_ref, seen_ref, news_ref, state_ref,
    d_mixed_ref, d_news_ref, d_state_ref, d_gate_ref,
    d_ext_ref, g_taps_ref, g_par_ref, window, d_window,
):
    step = pl.program_id(1)
    size = count * CH
    fill_window(window, proj_ref, halo_ref, step == pl.num_programs(1) - 1)

    @pl.when((step == 0) & (pl.program_id(0) == 0))
    def _():
        g_taps_ref[...] = jnp.zeros_like(g_taps_ref)
        g_par_ref[...] = jnp.zeros_like(g_par_ref)

    @pl.when(step == 0)
    def _():
        d_window[size:, :] = jnp.zeros((8, d_window.shape[1]), F32)

    @pl.when(step > 0)
    def _():
        d_window[size:, :] = d_window[0:8, :]

    weight = taps_ref[...]
    par = par_ref[...]
    o_row, o_col = step_orders()
    strict = o_row > o_col
    visible = sees()
    row = lax.broadcasted_iota(jnp.int32, (CH, CH), 0)
    col = lax.broadcasted_iota(jnp.int32, (CH, CH), 1)
    above = jnp.where(col >= row, 1.0, 0.0).astype(BF)
    lane = lax.broadcasted_iota(jnp.int32, (CH, LANES), 1)
    last = lax.broadcasted_iota(jnp.int32, (CH, LANES), 0) == CH - 1
    sums = [jnp.zeros((1, LANES), F32), jnp.zeros((1, LANES), F32)]

    def one(n):
        rows = slice(n * CH, (n + 1) * CH)
        conv = taps_sum(window, weight, n * CH)
        sig = jax.nn.sigmoid(conv)
        act = conv * sig
        qn, q_scale = unit(act[:, 0:128])
        k0n, k0_scale = unit(act[:, 128:256])
        k1n, k1_scale = unit(act[:, 256:384])
        q = qn.astype(BF)
        k = jnp.concatenate([k0n, k1n], axis=0).astype(BF)
        kf, qf = k.astype(F32), q.astype(F32)
        router = router_ref[0, rows, :]
        yield
        d_right = mm(halves(solve_ref[0, n]), halves(d_news_ref[0, n]), 0, 0)
        beta, g_col, g_row, g_last, decay = gate_columns(router, par)
        gaps = seen_decay(g_col, g_row, visible)
        yield
        ratio = jnp.where(strict, twice(gaps), 0.0)
        grown = jnp.exp(g_col)
        left = jnp.exp(g_last - g_col)
        gram = dot(k, k, 1, 1)
        state = state_ref[0, n]
        state_h = halves(state)
        news = news_ref[0, n]
        news_h = halves(news)
        d_mixed_h = halves(d_mixed_ref[0, n])
        d_state = d_state_ref[0, n]
        d_seen = mm(d_mixed_h, news_h, 1, 1)
        yield
        d_q_grown = grown[:CH] * mm(d_mixed_h, state_h, 1, 1)
        d_right_h = halves(d_right)
        d_lower = jnp.where(strict, -mm(d_right_h, news_h, 1, 1), 0.0)
        yield
        d_ends = left * mm(news_h, halves(d_state), 1, 1)
        d_pre = (1.0 - beta) * jnp.sum(d_right * news, axis=-1, keepdims=True)
        d_v = beta * d_right
        yield
        d_grown_k = -beta * mm(d_right_h, state_h, 1, 1)
        d_scores = halves(d_seen * gaps)
        seen_both = d_seen * seen_ref[0, n]
        yield
        d_q = d_q_grown + mm(d_scores, k)
        d_k = grown * d_grown_k
        d_gram = beta * ratio * d_lower
        both = d_gram * gram
        d_g = jnp.sum(both, axis=-1, keepdims=True) + jnp.sum(d_k * kf, axis=-1, keepdims=True)
        d_g_row = -jnp.sum(both, axis=0, keepdims=True)
        yield
        d_k = d_k + mm(halves(d_gram + d_gram.T), k) + d_ends
        d_g_q = jnp.sum(seen_both + d_q_grown * qf, axis=-1, keepdims=True)
        yield
        d_k = d_k + mm(d_scores, q, 0, 0)
        d_g_row = d_g_row - jnp.sum(seen_both, axis=0, keepdims=True)
        ends_sum = jnp.sum(d_ends * kf, axis=-1, keepdims=True)
        d_g = d_g - ends_sum
        d_last = jnp.sum(ends_sum, axis=0, keepdims=True) + jnp.exp(g_last) * jnp.sum(
            jnp.sum(d_state * state, axis=-1, keepdims=True), axis=0, keepdims=True
        )
        d_g_rows = jnp.broadcast_to(d_g_row, (LANES, ST)).T
        d_g_tok = d_g_q + d_g[:CH] + d_g[CH:] + d_g_rows[:CH] + d_g_rows[CH:]
        d_g_tok = d_g_tok + jnp.where(last, d_last, 0.0)
        yield
        d_decay = exact_sum(above, d_g_tok)
        yield
        d_soft = -jnp.exp(par[1:2]) * jax.nn.sigmoid(router + par[2:3]) * d_decay
        d_router = jnp.where(
            lane == 0,
            d_pre[:CH],
            jnp.where(lane == 1, d_pre[CH:], jnp.where(lane == 2, d_soft, 0.0)),
        )
        width = window.shape[1]
        d_ext_ref[0, rows, width : width + LANES] = d_gate_ref[0, rows, :]
        d_ext_ref[0, rows, width + LANES :] = d_router.astype(BF)
        sums[0] += jnp.sum(jnp.where(lane == 2, d_decay * decay, 0.0), axis=0, keepdims=True)
        sums[1] += jnp.sum(jnp.where(lane == 2, d_soft, 0.0), axis=0, keepdims=True)
        d_act = jnp.concatenate(
            [
                unit_back(d_q, act[:, 0:128], q_scale),
                unit_back(d_k[:CH], act[:, 128:256], k0_scale),
                unit_back(d_k[CH:], act[:, 256:384], k1_scale),
                d_v[:CH],
                d_v[CH:],
            ],
            axis=1,
        )
        d_window[rows, :] = d_act * (sig * (1.0 + conv * (1.0 - sig)))

    in_step([one(n) for n in range(count)])
    g_alog, g_dt = sums
    g_par_ref[1:2, :] += g_alog
    g_par_ref[2:3, :] += g_dt
    for n in range(count):
        start = n * CH
        here = d_window[pl.ds(start, CH), :]
        total = weight[3:4] * here
        for tap in range(3):
            total = total + weight[tap : tap + 1] * d_window[pl.ds(start + 3 - tap, CH), :]
        d_ext_ref[0, pl.ds(start, CH), : total.shape[1]] = total.astype(BF)
        for tap in range(4):
            g_taps_ref[tap : tap + 1, :] += jnp.sum(
                here * window[pl.ds(start + 5 + tap, CH), :], axis=0, keepdims=True
            )


def params(*semantics):
    return pltpu.CompilerParams(dimension_semantics=semantics, vmem_limit_bytes=VMEM_BYTES)


def small_params(*semantics):
    return pltpu.CompilerParams(dimension_semantics=semantics, vmem_limit_bytes=SMALL_BYTES)


def cost(chunks, per_chunk):
    return pl.CostEstimate(
        flops=int(chunks * per_chunk * 1.1e9), transcendentals=0, bytes_accessed=1 << 20
    )


def launch(kernel, in_specs, earlier, onto=(), first_out=0, **options):
    n_in = len(in_specs)
    others = list(earlier) + list(onto)

    def body(*refs):
        kernel(*refs[:n_in], *refs[n_in + len(others) :])

    specs = list(in_specs) + [pl.BlockSpec(memory_space=pl.ANY)] * len(others)
    at = n_in + len(earlier)
    aliases = {at + n: first_out + n for n in range(len(onto))}
    called = pl.pallas_call(body, in_specs=specs, input_output_aliases=aliases, **options)
    return lambda *operands: called(*operands, *others)


def fence(value, *earlier):
    earlier = [other for other in earlier if other is not None]
    if not earlier:
        return value
    anywhere = pl.BlockSpec(memory_space=pl.ANY)
    return pl.pallas_call(
        lambda *refs: None,
        in_specs=[anywhere] * (1 + len(earlier)),
        out_specs=anywhere,
        out_shape=jax.ShapeDtypeStruct(value.shape, value.dtype),
        input_output_aliases={0: 0},
        name="fence",
    )(value, *earlier)


def whole(shape):
    return pl.BlockSpec(shape, lambda *_: (0,) * len(shape))


def prepare(at, projected, router, taps, par, width, onto=(), earlier=(), count=8):
    n_micro, length, full = projected.shape
    chunks = length // CH
    size = count * CH
    per = lambda *tail: pl.BlockSpec((1, count) + tail, lambda i: (at, i, 0, 0))
    made = lambda kind, *tail: jax.ShapeDtypeStruct((n_micro, chunks) + tail, kind)
    return launch(
        partial(prep_kernel, count),
        [
            pl.BlockSpec((1, size, full), lambda i: (at, i, 0)),
            pl.BlockSpec((1, HALO, full), lambda i: (at, jnp.maximum(i * (size // HALO) - 1, 0), 0)),
            pl.BlockSpec((1, size, LANES), lambda i: (at, i, 0)),
            whole(taps.shape),
            whole(par.shape),
        ],
        earlier,
        onto,
        grid=(length // size,),
        out_specs=[per(ST, ST), per(ST, 128), per(ST, 128), per(CH, ST), per(CH, 128), per(ST, 128)],
        out_shape=[
            made(F32, ST, ST), made(F32, ST, 128), made(F32, ST, 128), made(F32, CH, ST),
            made(BF, CH, 128), made(BF, ST, 128),
        ],
        scratch_shapes=[pltpu.VMEM((size + 8, width), F32)],
        compiler_params=params("arbitrary"),
        cost_estimate=cost(chunks, 0.75),
        name="mixer_prepare",
    )(projected, projected, router, taps, par)


def scan_states(at, prep, router, projected, par, gate_at, n_tok, onto=(), earlier=(), count=4):
    _, wmat, umat, seen, q, k = prep
    n_micro, chunks = wmat.shape[:2]
    length = chunks * CH
    size = count * CH
    per = lambda *tail: pl.BlockSpec((1, count) + tail, lambda i: (at, i, 0, 0))
    made = lambda kind, *tail: jax.ShapeDtypeStruct((n_micro, chunks) + tail, kind)
    return launch(
        partial(scan_kernel, 1, count),
        [
            per(ST, 128), per(ST, 128), per(CH, ST), per(CH, 128), per(ST, 128),
            pl.BlockSpec((1, size, LANES), lambda i: (at, i, 0)),
            pl.BlockSpec((1, size, 128), lambda i: (at, i, gate_at)),
            whole(par.shape),
        ],
        earlier,
        onto,
        1,
        grid=(chunks // count,),
        out_specs=[
            pl.BlockSpec((size // n_tok, 1, n_tok, 128), lambda i: (i, 0, 0, 0)),
            per(CH, 128), per(ST, 128), per(128, 128),
        ],
        out_shape=[
            jax.ShapeDtypeStruct((length // n_tok, 1, n_tok, 128), BF),
            made(F32, CH, 128), made(F32, ST, 128), made(F32, 128, 128),
        ],
        scratch_shapes=[pltpu.VMEM((1, 128, 128), F32)],
        compiler_params=params("arbitrary"),
        cost_estimate=cost(chunks, 0.5),
        name="mixer_scan",
    )(wmat, umat, seen, q, k, router, projected, par)


def scan_back(prep, router, projected, par, gate_at, mixed, d_out, earlier=(), count=4):
    _, wmat, _, seen, q, k = prep
    n_micro, chunks = wmat.shape[:2]
    length = chunks * CH
    size = count * CH
    blocks = chunks // count
    n_tok = d_out.shape[2]
    per = lambda *tail: pl.BlockSpec((n_micro, count) + tail, lambda i: (0, blocks - 1 - i, 0, 0))
    made = lambda kind, *tail: jax.ShapeDtypeStruct((n_micro, chunks) + tail, kind)
    return launch(
        partial(scan_back_kernel, n_micro, count),
        [
            per(ST, 128), per(CH, ST), per(CH, 128), per(ST, 128),
            pl.BlockSpec((n_micro, size, LANES), lambda i: (0, blocks - 1 - i, 0)),
            pl.BlockSpec((n_micro, size, 128), lambda i: (0, blocks - 1 - i, gate_at)),
            whole(par.shape),
            per(CH, 128),
            pl.BlockSpec(
                (size // n_tok, n_micro, n_tok, 128), lambda i: (blocks - 1 - i, 0, 0, 0)
            ),
        ],
        earlier,
        grid=(blocks,),
        out_specs=[
            per(CH, 128), per(ST, 128), per(128, 128),
            pl.BlockSpec((n_micro, size, 128), lambda i: (0, blocks - 1 - i, 0)),
            whole((8, LANES)),
        ],
        out_shape=[
            made(F32, CH, 128), made(F32, ST, 128), made(F32, 128, 128),
            jax.ShapeDtypeStruct((n_micro, length, 128), BF),
            jax.ShapeDtypeStruct((8, LANES), F32),
        ],
        scratch_shapes=[pltpu.VMEM((n_micro, 128, 128), F32)],
        compiler_params=params("arbitrary"),
        cost_estimate=cost(n_micro * chunks, 0.4),
        name="mixer_scan_back",
    )(wmat, seen, q, k, router, projected, par, mixed, d_out)


def mixer_grads(
    prep, router, projected, taps, par, width, news, state, d_mixed, d_news, d_state, d_gate,
    earlier=(), count=4,
):
    solve, _, _, seen, _, _ = prep
    n_micro, chunks = solve.shape[:2]
    length = chunks * CH
    size = count * CH
    blocks = chunks // count
    full = projected.shape[2]
    per = lambda *tail: pl.BlockSpec((1, count) + tail, lambda m, i: (m, blocks - 1 - i, 0, 0))
    rows = lambda n: pl.BlockSpec((1, size, n), lambda m, i: (m, blocks - 1 - i, 0))
    before = lambda m, i: (m, jnp.maximum((blocks - 1 - i) * (size // HALO) - 1, 0), 0)
    return launch(
        partial(grads_kernel, count),
        [
            rows(full), pl.BlockSpec((1, HALO, full), before), rows(LANES),
            whole(taps.shape), whole(par.shape),
            per(ST, ST), per(CH, ST), per(ST, 128), per(128, 128),
            per(CH, 128), per(ST, 128), per(128, 128), rows(LANES),
        ],
        earlier,
        grid=(n_micro, blocks),
        out_specs=[rows(width + 2 * LANES), whole((8, width)), whole((8, LANES))],
        out_shape=[
            jax.ShapeDtypeStruct((n_micro, length, width + 2 * LANES), BF),
            jax.ShapeDtypeStruct((8, width), F32),
            jax.ShapeDtypeStruct((8, LANES), F32),
        ],
        scratch_shapes=[pltpu.VMEM((size + 8, width), F32), pltpu.VMEM((size + 8, width), F32)],
        compiler_params=params("arbitrary", "arbitrary"),
        cost_estimate=cost(n_micro * chunks, 1.0),
        name="mixer_grads",
    )(projected, projected, router, taps, par, solve, seen, news, state, d_mixed, d_news, d_state, d_gate)


def project_kernel(x_ref, gain_ref, weight_ref, router_weight_ref, normed_ref, out_ref, router_ref):
    per, _, n_tok, model = x_ref.shape
    x = x_ref[:, 0].reshape(per * n_tok, model).astype(F32)
    scale = lax.rsqrt(jnp.mean(x * x, axis=-1, keepdims=True) + EPS_NORM)
    normed = (x * scale * gain_ref[...]).astype(BF)
    normed_ref[0] = normed
    out_ref[0] = dot(normed, weight_ref[...]).astype(BF)
    router_ref[0] = dot(normed, router_weight_ref[...])


def project(x, gain, weight, router_weight, earlier=(), size=512):
    n_seq, n_micro, n_tok, model = x.shape
    length = n_seq * n_tok
    full = weight.shape[1]
    blocks = pl.BlockSpec((size // n_tok, 1, n_tok, model), lambda m, i: (i, m, 0, 0))
    rows = lambda n: pl.BlockSpec((1, size, n), lambda m, i: (m, i, 0))
    return launch(
        project_kernel,
        [blocks, whole((1, model)), whole(weight.shape), whole(router_weight.shape)],
        earlier,
        grid=(n_micro, length // size),
        out_specs=[rows(model), rows(full), rows(LANES)],
        out_shape=[
            jax.ShapeDtypeStruct((n_micro, length, model), BF),
            jax.ShapeDtypeStruct((n_micro, length, full), BF),
            jax.ShapeDtypeStruct((n_micro, length, LANES), F32),
        ],
        compiler_params=params("arbitrary", "arbitrary"),
        cost_estimate=cost(n_micro * length // CH, 0.35),
        name="project",
    )(x, gain[None], weight, router_weight)


def input_grads_kernel(normed_ref, d_ext_ref, w_ext_ref, gain_ref, out_ref, lines_ref):
    total = dot(normed_ref[0], d_ext_ref[0], 0, 0)
    for m in range(1, normed_ref.shape[0]):
        total = total + dot(normed_ref[m], d_ext_ref[m], 0, 0)
    full = out_ref.shape[1]
    out_ref[...] = total[:, :full].astype(BF)
    norm = jnp.sum(total * w_ext_ref[...].astype(F32), axis=1, keepdims=True)
    lane = lax.broadcasted_iota(jnp.int32, (total.shape[0], LANES), 1)
    tail = jnp.where(lane == 3, norm, total[:, full:])
    lines = tail.T[:8]
    row = lax.broadcasted_iota(jnp.int32, lines.shape, 0)
    lines_ref[...] = jnp.where(row == 3, lines / gain_ref[...], lines)


def input_grads(normed, d_ext, w_ext, gain, full, earlier=(), size=256):
    n_micro, length, model = normed.shape
    wide = d_ext.shape[2]
    return launch(
        input_grads_kernel,
        [
            pl.BlockSpec((n_micro, length, size), lambda i: (0, 0, i)),
            whole(d_ext.shape),
            pl.BlockSpec((size, wide), lambda i: (i, 0)),
            pl.BlockSpec((1, size), lambda i: (0, i)),
        ],
        earlier,
        grid=(model // size,),
        out_specs=[
            pl.BlockSpec((size, full), lambda i: (i, 0)),
            pl.BlockSpec((8, size), lambda i: (0, i)),
        ],
        out_shape=[
            jax.ShapeDtypeStruct((model, full), BF),
            jax.ShapeDtypeStruct((8, model), F32),
        ],
        compiler_params=params("arbitrary"),
        cost_estimate=cost(1, 7.0),
        name="input_grads",
    )(normed, d_ext, w_ext, gain[None])


def place_heads_kernel(n_heads, copies, slots, cut, lines, where, *refs):
    parts, out_ref, small_ref = refs[:-2], refs[-2], refs[-1]
    for j, part in enumerate(parts):
        at = where[0] ^ j
        for slot in range(slots):
            for h in range(n_heads):
                to = (slot * n_heads + h) * LANES
                value = part[h * copies, :cut, slot * LANES : (slot + 1) * LANES]
                out_ref[at, :, to : to + LANES] = value.astype(F32)
        for s in range(part.shape[0]):
            high = part[s, cut : cut + lines].astype(F32)
            low = part[s, cut + lines : cut + 2 * lines].astype(F32)
            for r in range(len(parts)):

                @pl.when(at == r)
                def _(s=s, r=r, value=high + low):
                    small_ref[s, r * lines : (r + 1) * lines] = value


def place_heads(where, parts, n_heads, slots, cut, lines):
    n_seq, rows, full = parts[0].shape
    n_parts = len(parts)
    shape = (n_parts, cut, full * n_heads)
    small = (n_seq, n_parts * lines, full)
    grad, values = pl.pallas_call(
        partial(place_heads_kernel, n_heads, n_seq // n_heads, slots, cut, lines),
        grid_spec=pltpu.PrefetchScalarGridSpec(
            num_scalar_prefetch=1,
            grid=(1,),
            in_specs=[pl.BlockSpec(part.shape, lambda i, where: (0, 0, 0)) for part in parts],
            out_specs=[
                pl.BlockSpec(shape, lambda i, where: (0, 0, 0)),
                pl.BlockSpec(small, lambda i, where: (0, 0, 0)),
            ],
        ),
        out_shape=[jax.ShapeDtypeStruct(shape, F32), jax.ShapeDtypeStruct(small, F32)],
        compiler_params=small_params("arbitrary"),
        cost_estimate=cost(1, 3.0),
        name="place_heads",
    )(where, *parts)
    return grad.reshape(-1, full * n_heads), values


def pack_kernel(lines, own_ref, got_ref, small_ref, out_ref):
    n_seq, cut, full = own_ref.shape
    rows = out_ref.shape[1]
    tail = list(halves(small_ref[...]))
    if rows > cut + 2 * lines:
        tail.append(jnp.zeros((rows - cut - 2 * lines, full), BF))
    tail = jnp.concatenate(tail, axis=0)
    for s in range(n_seq):
        out_ref[s, :cut] = (own_ref[s].astype(F32) + got_ref[s].astype(F32)).astype(BF)
        out_ref[s, cut:] = tail


def pack(own, got, small, rows, earlier=()):
    n_seq, cut, full = own.shape
    return launch(
        partial(pack_kernel, small.shape[0]),
        [whole(own.shape), whole(got.shape), whole(small.shape)],
        earlier,
        grid=(1,),
        out_specs=whole((n_seq, rows, full)),
        out_shape=jax.ShapeDtypeStruct((n_seq, rows, full), BF),
        compiler_params=small_params("arbitrary"),
        cost_estimate=cost(1, 1.5),
        name="pack",
    )(own, got, small)


def place_units_kernel(unit_cut, unit_pad, n_seq, where, *refs):
    parts, out_ref = refs[:-1], refs[-1]
    n_row = len(parts)
    group = unit_cut * n_row
    hidden = group * n_seq
    for block in range(hidden // LANES):
        low = (block * LANES // group) * unit_pad // LANES * LANES
        high = ((block * LANES + LANES - 1) // group + 1) * unit_pad
        high = min(n_seq * unit_pad, -(-high // LANES) * LANES)
        col = lax.broadcasted_iota(jnp.int32, (high - low, LANES), 1) + block * LANES
        row = lax.broadcasted_iota(jnp.int32, (high - low, LANES), 0) + low
        inner = lax.rem(col, group)
        owner = lax.div(inner, unit_cut)
        unit = lax.div(col, group) * unit_pad + lax.rem(inner, unit_cut)
        total = [0.0, 0.0]
        for j, part in enumerate(parts):
            chosen = jnp.where((unit == row) & (owner == (where[0] ^ j)), 1.0, 0.0).astype(BF)
            for half in range(2):
                at = half * n_seq * unit_pad
                total[half] = total[half] + dot(part[:, at + low : at + high], chosen)
        for half in range(2):
            to = half * hidden + block * LANES
            out_ref[:, to : to + LANES] = total[half]


def place_units(where, parts, unit_cut, unit_pad, n_seq):
    rows = parts[0].shape[0]
    shape = (rows, 2 * unit_cut * n_seq * len(parts))
    return pl.pallas_call(
        partial(place_units_kernel, unit_cut, unit_pad, n_seq),
        grid_spec=pltpu.PrefetchScalarGridSpec(
            num_scalar_prefetch=1,
            grid=(1,),
            in_specs=[pl.BlockSpec(part.shape, lambda i, where: (0, 0)) for part in parts],
            out_specs=pl.BlockSpec(shape, lambda i, where: (0, 0)),
        ),
        out_shape=jax.ShapeDtypeStruct(shape, F32),
        compiler_params=small_params("arbitrary"),
        cost_estimate=cost(1, 5.0),
        name="place_units",
    )(where, *parts)


def place_rows_kernel(where, *refs):
    parts, out_ref = refs[:-1], refs[-1]
    for j, part in enumerate(parts):
        out_ref[where[0] ^ j] = part[...].astype(F32)


def place_down_kernel(unit_pad, left, where, *refs):
    parts, out_ref = refs[:-1], refs[-1]
    _, keep, model = out_ref.shape
    n_units = parts[0].shape[1] - left
    rest = model - n_units
    step = unit_pad * rest // n_units
    for j, part in enumerate(parts):
        at = where[0] ^ j
        out_ref[at, :, :n_units] = part[:keep, left:].astype(F32)
        for b in range(n_units // rest):
            have = min(step, keep - b * step)
            if have > 0:
                value = part[unit_pad : unit_pad + have, left + b * rest : left + (b + 1) * rest]
                out_ref[at, b * step : b * step + have, n_units:] = value.astype(F32)


def place_rows(where, parts, shape, kernel=place_rows_kernel):
    return pl.pallas_call(
        kernel,
        grid_spec=pltpu.PrefetchScalarGridSpec(
            num_scalar_prefetch=1,
            grid=(1,),
            in_specs=[pl.BlockSpec(part.shape, lambda i, where: (0, 0)) for part in parts],
            out_specs=pl.BlockSpec((len(parts),) + shape, lambda i, where: (0, 0, 0)),
        ),
        out_shape=jax.ShapeDtypeStruct((len(parts),) + shape, F32),
        compiler_params=small_params("arbitrary"),
        cost_estimate=cost(1, 2.0),
        name="place_rows",
    )(where, *parts).reshape(-1, shape[1])


def place_down(where, parts, unit_pad, left, shape):
    return place_rows(where, parts, shape, partial(place_down_kernel, unit_pad, left))


def feed_kernel(n_seq, n_parts, d_top_ref, w_ref, *refs):
    part_refs, (mid_ref, act_ref, d_gu_ref, down_ref), d_mid_refs = (
        refs[:-4 - n_parts], refs[-4 - n_parts : -n_parts], refs[-n_parts:]
    )
    per_step = len(part_refs) // n_parts
    n_tok = part_refs[0].shape[0]
    for j in range(n_parts):

        @pl.when(pl.program_id(0) == j)
        def _(j=j):
            for m in range(per_step):
                mid_ref[m * n_tok : (m + 1) * n_tok] = part_refs[j * per_step + m][...]

    n_units = act_ref.shape[1]
    model = mid_ref.shape[1]
    per = n_units // n_seq

    @pl.when(pl.program_id(0) == 0)
    def _():
        lines = w_ref[:, 2 * n_units :].reshape(n_seq, model // n_seq, n_units)
        rest = model - n_units
        step = per * rest // n_units
        for s in range(n_seq):
            down_ref[s * per : (s + 1) * per, :n_units] = lines[s, :per]
            for b in range(n_units // rest):
                at = s * per + b * step
                down_ref[at : at + step, n_units:] = lines[s, per:, b * rest : (b + 1) * rest]

    w_gate = w_ref[:, :n_units]
    w_up = w_ref[:, n_units : 2 * n_units]
    mid = mid_ref[...]
    gate = dot(mid, w_gate)
    up = dot(mid, w_up)
    d_act = dot(d_top_ref[...], down_ref[...], 1, 1)
    sig = jax.nn.sigmoid(gate)
    silu = gate * sig
    act_ref[...] = (silu * up).astype(BF)
    d_gate = (d_act * up * sig * (1.0 + gate * (1.0 - sig))).astype(BF)
    d_up = (d_act * silu).astype(BF)
    d_gu_ref[0] = d_gate
    d_gu_ref[1] = d_up
    d_mid = (dot(d_gate, w_gate, 1, 1) + dot(d_up, w_up, 1, 1)).astype(BF)
    for j, d_mid_ref in enumerate(d_mid_refs):

        @pl.when(pl.program_id(0) == j)
        def _(d_mid_ref=d_mid_ref):
            d_mid_ref[...] = d_mid


def feed(mid, d_top, weights, n_units, n_seq, n_parts):
    tokens, model = d_top.shape
    size = tokens // n_parts
    rows = lambda n: pl.BlockSpec((size, n), lambda i: (i, 0))
    return pl.pallas_call(
        partial(feed_kernel, n_seq, n_parts),
        grid=(n_parts,),
        in_specs=[rows(model), whole(weights.shape)] + [whole(part.shape) for part in mid],
        out_specs=[
            rows(model), rows(n_units), pl.BlockSpec((2, size, n_units), lambda i: (0, i, 0)),
            whole((n_units, model)),
        ] + [whole((size, model))] * n_parts,
        out_shape=[
            jax.ShapeDtypeStruct((tokens, model), BF),
            jax.ShapeDtypeStruct((tokens, n_units), BF),
            jax.ShapeDtypeStruct((2, tokens, n_units), BF),
            jax.ShapeDtypeStruct((n_units, model), BF),
        ] + [jax.ShapeDtypeStruct((size, model), BF)] * n_parts,
        compiler_params=params("arbitrary"),
        cost_estimate=cost(1, 14.0),
        name="feed",
    )(d_top, weights, *mid)


def times_kernel(left_ref, right_ref, *out_refs):
    value = dot(left_ref[...], right_ref[...]).astype(BF)
    for j, out_ref in enumerate(out_refs):

        @pl.when(pl.program_id(0) == j)
        def _(out_ref=out_ref):
            out_ref[...] = value


def times(left, right, n_parts, earlier=()):
    tokens, inner = left.shape
    size = tokens // n_parts
    return launch(
        times_kernel,
        [pl.BlockSpec((size, inner), lambda i: (i, 0)), whole(right.shape)],
        earlier,
        grid=(n_parts,),
        out_specs=[whole((size, right.shape[1]))] * n_parts,
        out_shape=[jax.ShapeDtypeStruct((size, right.shape[1]), BF)] * n_parts,
        compiler_params=small_params("arbitrary"),
        cost_estimate=cost(1, 3.0),
        name="times",
    )(left, right)


def feed_grads(mid, d_gu, act, d_top, n_seq, earlier=(), size=512):
    tokens, model = mid.shape
    n_units = d_gu.shape[2]
    shard, unit_pad = model // n_seq, n_units // n_seq
    per = size // shard

    def body(mid_ref, d_gu_ref, act_ref, d_top_ref, out_ref):
        mid = mid_ref[...]
        g_down = dot(act_ref[...], d_top_ref[...], 0, 0).astype(BF)
        for half in range(2):
            value = dot(mid, d_gu_ref[half], 0, 0).astype(BF)
            out_ref[:, half * n_units : (half + 1) * n_units] = value
        rest = model - n_units
        step = unit_pad * rest // n_units
        for part in range(per):
            at, rows = part * shard, g_down[part * unit_pad : (part + 1) * unit_pad]
            out_ref[at : at + unit_pad, 2 * n_units :] = rows[:, :n_units]
            for b in range(n_units // rest):
                to = 2 * n_units + b * rest
                out_ref[at + unit_pad : at + shard, to : to + rest] = rows[
                    b * step : (b + 1) * step, n_units:
                ]

    return launch(
        body,
        [
            pl.BlockSpec((tokens, size), lambda i: (0, i)), whole(d_gu.shape),
            pl.BlockSpec((tokens, per * unit_pad), lambda i: (0, i)), whole(d_top.shape),
        ],
        earlier,
        grid=(model // size,),
        out_specs=pl.BlockSpec((size, 3 * n_units), lambda i: (i, 0)),
        out_shape=jax.ShapeDtypeStruct((model, 3 * n_units), BF),
        compiler_params=params("arbitrary"),
        cost_estimate=cost(1, 7.0),
        name="feed_grads",
    )(mid, d_gu, act, d_top)


def place_pieces_kernel(order, where, *refs):
    parts, out_ref = refs[:-1], refs[-1]
    for j, part in enumerate(parts):
        for n in range(part.shape[0]):
            at = n if order is None else where[1] ^ order[n]
            out_ref[at, where[0] ^ j] = part[n]


def place_pieces(where, parts, order=None):
    n_seq, cut, width = parts[0].shape
    shape = (n_seq, len(parts), cut, width)
    return pl.pallas_call(
        partial(place_pieces_kernel, order),
        grid_spec=pltpu.PrefetchScalarGridSpec(
            num_scalar_prefetch=1,
            grid=(1,),
            in_specs=[pl.BlockSpec(part.shape, lambda i, where: (0, 0, 0)) for part in parts],
            out_specs=pl.BlockSpec(shape, lambda i, where: (0, 0, 0, 0)),
        ),
        out_shape=jax.ShapeDtypeStruct(shape, BF),
        compiler_params=small_params("arbitrary"),
        cost_estimate=cost(1, 2.0),
        name="place_pieces",
    )(where, *parts).reshape(-1, width)


def middle_kernel(copies, gated_ref, x_ref, w_ref, gain_ref, residual_ref, normed_ref, gated_out_ref):
    n_heads = gated_ref.shape[0] // copies
    total = x_ref[0].astype(F32)
    for h in range(n_heads):
        part = gated_ref[h * copies, 0]
        gated_out_ref[0, :, h * LANES : (h + 1) * LANES] = part
        total = total + dot(part, w_ref[h * LANES : (h + 1) * LANES])
    scale = lax.rsqrt(jnp.mean(total * total, axis=-1, keepdims=True) + EPS_NORM)
    residual_ref[0] = total
    normed_ref[0] = (total * scale * gain_ref[...]).astype(BF)


def middle(at, gated, x, w_out, gain, copies):
    _, n_tok, model = x.shape
    n_seq = gated.shape[0]
    rows = pl.BlockSpec((1, n_tok, model), lambda i: (0, 0, 0))
    made = lambda kind: jax.ShapeDtypeStruct((1, n_tok, model), kind)
    return pl.pallas_call(
        partial(middle_kernel, copies),
        grid=(1,),
        in_specs=[
            pl.BlockSpec((n_seq, 1, n_tok, LANES), lambda i: (0, 0, 0, 0)),
            pl.BlockSpec((1, n_tok, model), lambda i: (at, 0, 0)),
            whole(w_out.shape), whole((1, model)),
        ],
        out_specs=[rows] * 3,
        out_shape=[made(F32), made(BF), made(BF)],
        compiler_params=params("arbitrary"),
        cost_estimate=cost(1, 2.0),
        name="middle",
    )(gated, x, w_out, gain[None])


def input_back_kernel(d_ext_ref, w_ref, out_ref):
    value = dot(d_ext_ref[0], w_ref[...], 1, 1).astype(BF)
    per, _, n_tok, _ = out_ref.shape
    for part in range(per):
        out_ref[part, 0] = value[part * n_tok : (part + 1) * n_tok]


def input_back(d_ext, w_ext, n_tok, size=512):
    n_micro, length, wide = d_ext.shape
    model = w_ext.shape[0]
    per = size // n_tok
    return pl.pallas_call(
        input_back_kernel,
        grid=(n_micro, length // size),
        in_specs=[pl.BlockSpec((1, size, wide), lambda m, s: (m, s, 0)), whole(w_ext.shape)],
        out_specs=pl.BlockSpec((per, 1, n_tok, model), lambda m, s: (s, m, 0, 0)),
        out_shape=jax.ShapeDtypeStruct((length // n_tok, n_micro, n_tok, model), BF),
        compiler_params=params("arbitrary", "arbitrary"),
        cost_estimate=cost(1, 7.0),
        name="input_back",
    )(d_ext, w_ext)


def bottom_kernel(d_in_ref, d_residual_ref, x_ref, gain_ref, out_ref):
    x = x_ref[0].astype(F32)
    scale = lax.rsqrt(jnp.mean(x * x, axis=-1, keepdims=True) + EPS_NORM)
    d_normed = d_in_ref[...].astype(F32) * gain_ref[...]
    out_ref[0] = (
        d_residual_ref[...]
        + scale * d_normed
        - x * scale**3 * jnp.mean(d_normed * x, axis=-1, keepdims=True)
    )


def bottom(d_in, d_residual, x, gain, earlier=()):
    n_micro, n_tok, model = x.shape
    rows = pl.BlockSpec((n_tok, model), lambda m: (m, 0))
    block = pl.BlockSpec((1, n_tok, model), lambda m: (m, 0, 0))
    return launch(
        bottom_kernel,
        [rows, rows, block, whole((1, model))],
        earlier,
        grid=(n_micro,),
        out_specs=block,
        out_shape=jax.ShapeDtypeStruct((n_micro, n_tok, model), F32),
        compiler_params=small_params("arbitrary"),
        cost_estimate=cost(1, 2.0),
        name="bottom",
    )(d_in, d_residual, x, gain[None])


def turn_kernel(
    own_ref, got_ref, d_top_ref, residual_ref, w_ref, gain_ref, d_residual_ref, d_low_ref, d_sent_ref, norm_ref
):
    @pl.when(pl.program_id(0) == 0)
    def _():
        norm_ref[...] = jnp.zeros_like(norm_ref)

    residual = residual_ref[...]
    scale = lax.rsqrt(jnp.mean(residual * residual, axis=-1, keepdims=True) + EPS_NORM)
    d_mid = own_ref[...].astype(F32) + got_ref[...].astype(F32)
    norm_ref[0:1, :] += jnp.sum(d_mid * residual * scale, axis=0, keepdims=True)
    d_normed = d_mid * gain_ref[...]
    d_residual = (
        d_top_ref[...]
        + scale * d_normed
        - residual * scale**3 * jnp.mean(d_normed * residual, axis=-1, keepdims=True)
    )
    d_residual_ref[...] = d_residual
    d_low = d_residual.astype(BF)
    d_low_ref[...] = d_low
    d_gated = dot(d_low, w_ref[...], 1, 1).astype(BF)
    for h in range(d_sent_ref.shape[0]):
        d_sent_ref[h, 0] = d_gated[:, h * LANES : (h + 1) * LANES]


def turn(own, got, d_top, residual, w_out, gain, n_micro):
    tokens, model = own.shape
    n_tok = tokens // n_micro
    n_heads = model // LANES
    rows = pl.BlockSpec((n_tok, model), lambda m: (m, 0))
    return pl.pallas_call(
        turn_kernel,
        grid=(n_micro,),
        in_specs=[rows, rows, rows, rows, whole(w_out.shape), whole((1, model))],
        out_specs=[
            rows, rows,
            pl.BlockSpec((n_heads, 1, n_tok, LANES), lambda m: (0, m, 0, 0)),
            whole((8, model)),
        ],
        out_shape=[
            jax.ShapeDtypeStruct((tokens, model), F32),
            jax.ShapeDtypeStruct((tokens, model), BF),
            jax.ShapeDtypeStruct((n_heads, n_micro, n_tok, LANES), BF),
            jax.ShapeDtypeStruct((8, model), F32),
        ],
        compiler_params=params("arbitrary"),
        cost_estimate=cost(1, 5.0),
        name="turn",
    )(own, got, d_top, residual, w_out, gain[None])


def pick(stacked, at, axis=0):
    return lax.dynamic_index_in_dim(stacked, at, axis, False, allow_negative_indices=False)


def exchange(value, axis, bit):
    count = lax.axis_size(axis)
    return lax.ppermute(value, axis, [(i, i ^ bit) for i in range(count)])


def bits(axis):
    count = lax.axis_size(axis)
    return [1 << b for b in range(count.bit_length() - 1)]


def row_gather(value):
    parts = {0: value}
    for bit in reversed(bits("row")):
        parts.update({j ^ bit: exchange(part, "row", bit) for j, part in parts.items()})
    return [parts[j] for j in range(len(parts))]


def row_gather_steps(value):
    parts = {0: value}
    for bit in reversed(bits("row")):
        got = {j ^ bit: exchange(part, "row", bit) for j, part in parts.items()}
        parts.update(got)
        earlier = yield list(got.values())
        if earlier:
            parts = {j: fence(part, *earlier) for j, part in parts.items()}
    return [parts[j] for j in range(len(parts))]


def seq_scatter_steps(parts):
    mine = lax.axis_index("seq")
    for bit in reversed(bits("seq")):
        parts = parts.reshape((2, bit) + parts.shape[1:])
        side = (mine & bit) // bit
        got = exchange(pick(parts, 1 - side).astype(BF), "seq", bit)
        yield got
        parts = pick(parts, side).astype(F32) + got.astype(F32)
    return parts[0].astype(BF)


def seq_gather_steps(value):
    parts, order = value[None], [0]
    for n, bit in enumerate(reversed(bits("seq"))):
        parts = jnp.concatenate([parts, exchange(parts, "seq", bit)], axis=0)
        order = order + [place ^ bit for place in order]
        if n + 1 < len(bits("seq")):
            sent = yield parts
            parts = parts if sent is None else sent
    return parts, order


def finish(steps, value=None):
    try:
        steps.send(value)
        while True:
            next(steps)
    except StopIteration as end:
        return end.value


def row_scatter_halves(parts):
    parts = dict(enumerate(parts))
    for bit in bits("row"):
        got = {j ^ bit: exchange(parts[j].astype(BF), "row", bit) for j in parts if j & bit}
        if len(got) == 1:
            return parts[0], got[0]
        parts = {j: parts[j].astype(F32) + part.astype(F32) for j, part in got.items()}


def ring():
    count, mine = lax.axis_size("seq"), lax.axis_index("seq")
    order = list(range(0, count, 2)) + list(range(1, count, 2))[::-1]
    half = mine >> 1
    place = jnp.where((mine & 1) == 0, half, count - 1 - half)

    def owner(k):
        at = (place + (k % count)) & (count - 1)
        return jnp.where(at < count // 2, 2 * at, 2 * count - 1 - 2 * at)

    ahead = [(order[i], order[(i + 1) % count]) for i in range(count)]
    behind = [(b, a) for a, b in ahead]
    return count, owner, ahead, behind


def ring_gather(value, earlier):
    count, owner, ahead, behind = ring()
    blocks = jnp.zeros((count,) + value.shape, value.dtype)
    put = lambda blocks, block, k: lax.dynamic_update_index_in_dim(
        blocks, block, owner(k), 0, allow_negative_indices=False
    )
    blocks = put(blocks, value, 0)
    there, back = value, value
    for k in range(1, count // 2):
        there = lax.ppermute(there, "seq", ahead)
        back = lax.ppermute(back, "seq", behind)
        if k in earlier:
            there = fence(there, *earlier[k])
        blocks = put(put(blocks, there, -k), back, k)
    cut = value.shape[1] // 2
    there = lax.ppermute(there[:, :cut], "seq", ahead)
    back = lax.ppermute(back[:, cut:], "seq", behind)
    return put(blocks, jnp.concatenate([there, back], axis=1), count // 2)


def matmul(spec, left, right, kind=F32):
    return jnp.einsum(spec, left, right, preferred_element_type=F32).astype(kind)


def local(
    tokens,
    cotangent,
    row_lengths,
    norm1_gain,
    w_in,
    w_router,
    conv_weight,
    a_log,
    dt_bias,
    head_gain,
    w_out,
    norm2_gain,
    w_gu,
    w_down,
):
    n_seq, n_row = lax.axis_size("seq"), lax.axis_size("row")
    seq, row = lax.axis_index("seq"), lax.axis_index("row")
    n_micro, _, n_tok, model = tokens.shape
    micros = list(range(n_micro))
    n_heads = a_log.shape[0]
    head_dim = head_gain.shape[0]
    n_taps, conv_width = conv_weight.shape
    slots = w_in.shape[1] // (n_heads * head_dim)
    width = conv_width // n_heads
    full = slots * head_dim
    length = n_tok * n_seq
    copies = n_seq // n_heads
    head = seq // copies
    gate_at = slots - 1

    def to_heads(value):
        return lax.all_to_all(jnp.repeat(value, copies, axis=0), "seq", 0, 0, tiled=True)

    def seq_parts(value):
        return lax.all_to_all(value, "seq", 0, 0, tiled=True)

    def from_heads(value):
        got = lax.all_to_all(value, "seq", 0, 0, tiled=True)
        return got if copies == 1 else got[::copies]

    def in_order(parts, axis):
        stacked = jnp.stack(parts)
        return jnp.concatenate([pick(stacked, row ^ j) for j in range(n_row)], axis=axis)

    where = jnp.stack([row, seq]).astype(jnp.int32)

    cut = w_in.shape[0] // n_row
    w_piece = pick(w_in.reshape(n_row, cut, slots, n_heads, head_dim), row)
    w_got = to_heads(w_piece.transpose(2, 0, 1, 3).reshape(n_heads, cut, full))
    w_head = place_pieces(where, row_gather(w_got))
    w_rt = pick(w_router.reshape(model, -1, n_heads), head, 2)
    n_rt = w_rt.shape[1]
    w_rt = jnp.pad(w_rt, ((0, 0), (0, LANES - n_rt)))
    w_ext = jnp.concatenate([w_head, w_rt], axis=1)
    taps = pick(conv_weight.reshape(n_taps, gate_at, n_heads, head_dim), head, 2)
    taps = jnp.pad(taps.reshape(n_taps, width), ((0, 8 - n_taps), (0, 0)))
    par = jnp.concatenate(
        [
            head_gain[None],
            jnp.broadcast_to(lax.dynamic_index_in_dim(a_log, head, 0), (1, LANES)),
            jnp.broadcast_to(lax.dynamic_index_in_dim(dt_bias, head, 0), (1, LANES)),
            jnp.zeros((5, LANES), F32),
        ]
    )
    position = seq * n_tok + jnp.arange(n_tok, dtype=jnp.int32)
    live = (position[None, :] < row_lengths[:, :1]).astype(F32)[:, :, None]
    d_top = (cotangent[:, 0].astype(F32) * live).reshape(-1, model)
    d_rows = jnp.concatenate(row_gather(d_top.astype(BF)), axis=0)

    out_cut = w_out.shape[0] // n_row
    out_piece = lax.dynamic_slice_in_dim(w_out, row * out_cut, out_cut, 0)
    out_steps = seq_gather_steps(out_piece)
    out_got = next(out_steps)

    x_all = ring_gather(
        tokens[:, 0], {n_seq // 4: [w_got], n_seq // 2 - 1: [w_ext, w_rt, taps, par, d_rows, out_got]}
    )

    shard = w_out.shape[0]
    hidden = w_gu.shape[1] // 2
    unit_cut = hidden // n_seq // n_row
    unit_pad = -(-unit_cut // 16) * 16
    n_units = unit_pad * n_seq
    gu_piece = pick(w_gu.reshape(shard, 2, n_seq, n_row, unit_cut), row, 3)
    gu_piece = jnp.pad(gu_piece, ((0, 0), (0, 0), (0, 0), (0, unit_pad - unit_cut)))
    down_piece = lax.dynamic_slice_in_dim(w_down, row * unit_cut, unit_cut, 0)
    down_piece = jnp.pad(down_piece, ((0, unit_pad - unit_cut), (0, 0)))
    beside = down_piece[:, n_units:]
    beside = beside.reshape(n_units // beside.shape[1], -1, beside.shape[1])
    beside = jnp.concatenate(list(beside), axis=1)
    down_piece = jnp.concatenate([down_piece[:, :n_units], beside])
    weights = jnp.concatenate([gu_piece.reshape(shard, -1), down_piece], axis=1)
    weights = fence(weights, x_all)
    weights_all = lax.all_gather(weights, "seq", axis=0, tiled=True)

    normed_in, projected, router = project(x_all, norm1_gain, w_head, w_rt, [d_rows, weights])
    out_got = out_steps.send(fence(out_got, projected))
    prep, kept, sent = (), (), []
    for m in micros:
        prep = prepare(m, projected, router, taps, par, width, prep)
        if m == 0:
            out_got, order = finish(out_steps, fence(out_got, prep[0]))
        gated, *kept = scan_states(
            m, prep, router, projected, par, gate_at, n_tok, kept, sent[-1:]
        )
        sent.append(seq_parts(gated))
        if m == 0:
            full_out = place_pieces(where, row_gather(fence(out_got, gated)), order)

    middles = [middle(m, sent[m], tokens[:, 0], full_out, norm2_gain, copies) for m in micros]
    mid_rows = zip(*[row_gather(normed_mid[0]) for _, normed_mid, _ in middles])
    mid_rows = [part for parts in mid_rows for part in parts]
    residual = jnp.concatenate([value[0][0] for value in middles], axis=0)
    gated = jnp.concatenate([value[2][0] for value in middles], axis=0)
    mid_rows, act, d_gu, down, *d_mid = feed(
        mid_rows, d_rows, weights_all, n_units, n_seq, n_row
    )
    g_feed = feed_grads(mid_rows, d_gu, act, d_rows, n_seq)
    g_feed_sum = lax.psum_scatter(g_feed, "seq", scatter_dimension=0, tiled=True)
    d_mid_own, d_mid_got = row_scatter_halves(d_mid)

    def row_parts(value, axis):
        return [pick(value, row ^ j, axis) for j in range(n_row)]

    d_residual, d_low, d_sent, g_norm2 = turn(
        d_mid_own, fence(d_mid_got, g_feed), d_top, residual, full_out, norm2_gain, n_micro
    )
    d_gated = to_heads(d_sent)

    mlp = times(act, down, n_row, [d_sent])
    out_halves = row_scatter_halves(mlp)
    g_out_full = matmul("tc,td->cd", fence(gated, d_sent), d_low)
    g_out = g_out_full
    g_out = row_scatter_halves(row_parts(g_out.reshape(n_seq, n_row, out_cut, model), 1))

    mixed, news, state = kept
    d_mixed, d_news, d_state, d_gate_pre, g_head = scan_back(
        prep, router, projected, par, gate_at, mixed, d_gated
    )
    d_ext, g_taps, g_par = mixer_grads(
        prep, router, projected, taps, par, width,
        news, state, d_mixed, d_news, d_state, d_gate_pre, [g_out[1], out_halves[1]],
    )
    if copies > 1:
        mine = (seq % copies == 0).astype(F32)
        d_ext = d_ext * mine.astype(BF)
        g_taps, g_par, g_head = g_taps * mine, g_par * mine, g_head * mine
    d_in_part = input_back(d_ext, w_ext, n_tok).reshape(-1, model)
    d_in = lax.psum_scatter(d_in_part, "seq", scatter_dimension=0, tiled=True)
    g_in, in_lines = input_grads(normed_in, d_ext, w_ext, norm1_gain, full, [d_in_part])
    fill = lambda value: jnp.pad(value, ((0, 0), (0, full - value.shape[1])))
    scalars = jnp.concatenate([g_head[:1], g_par[1:2], g_par[2:3]], axis=1)
    vectors = jnp.concatenate([in_lines[: n_rt + 1], g_norm2[:1]]).reshape(-1, model // 2)
    small = jnp.concatenate([fill(vectors), fill(scalars), fill(g_taps[:n_taps])])
    n_vec = vectors.shape[0]
    lines = -(-small.shape[0] // n_row)
    small = jnp.pad(small, ((0, n_row * lines - small.shape[0]), (0, 0))).reshape(n_row, lines, full)

    g_out = g_out[0].astype(F32) + fence(g_out[1], d_in_part).astype(F32)
    g_out_steps = seq_scatter_steps(g_out)
    moment = next(g_out_steps)
    parts = row_parts(g_in.reshape(n_seq, n_row, cut, full), 1)
    parts = {j: fence(part, moment) if j & 1 else part for j, part in enumerate(parts)}
    smalls = dict(enumerate(row_parts(small, 0)))
    for bit in bits("row"):
        got = {j ^ bit: exchange(parts[j], "row", bit) for j in parts if j & bit}
        got_small = {j ^ bit: exchange(smalls[j], "row", bit) for j in smalls if j & bit}
        smalls = {j: smalls[j] + part for j, part in got_small.items()}
        if len(got) > 1:
            parts = {
                j: (parts[j].astype(F32) + part.astype(F32)).astype(BF) for j, part in got.items()
            }
    rows = cut + -(-2 * lines // 16) * 16
    g_in_got = seq_parts(pack(parts[0], got[0], smalls[0], rows, [next(g_out_steps)]))
    feed_steps = row_gather_steps(fence(g_feed_sum, got[0]))
    g_in_got = fence(g_in_got, *next(feed_steps), next(g_out_steps))
    in_steps = row_gather_steps(g_in_got)
    first_in = next(in_steps)
    g_out_sum = finish(g_out_steps)
    g_feed_all = finish(feed_steps)
    g_out_all = row_gather(g_out_sum)
    grad_out = place_rows(where, g_out_all, (out_cut, model))
    grad_down = place_down(where, g_feed_all, unit_pad, 2 * n_units, (unit_cut, model))
    grad_gu = place_units(where, g_feed_all, unit_cut, unit_pad, n_seq)
    g_in_all = finish(in_steps, [grad_gu, grad_down])
    grad_in, small = place_heads(where, g_in_all, n_heads, slots, cut, lines)
    before = [grad_in, grad_gu, grad_down, grad_out]
    grad_tokens = bottom(d_in, d_residual, tokens[:, 0], norm1_gain, before)[:, None]
    out = residual + out_halves[0].astype(F32) + out_halves[1].astype(F32)
    out = out.astype(BF).reshape(n_micro, 1, n_tok, model)
    total = jnp.sum(small[:, 2 * n_rt : n_vec + 1], axis=0)
    norms = total[:4, : model // 2].reshape(2, model)
    heads = small[::copies]
    conv_sum = heads[:, n_vec + 1 : n_vec + 1 + n_taps, :width]
    conv_sum = conv_sum.reshape(n_heads, n_taps, gate_at, head_dim)
    conv_sum = conv_sum.transpose(1, 2, 0, 3).reshape(n_taps, conv_width)
    router_sum = heads[:, : 2 * n_rt, : model // 2].reshape(n_heads, n_rt, model)
    router_sum = router_sum.transpose(2, 1, 0).reshape(model, n_rt * n_heads)
    return (
        out,
        grad_tokens,
        norms[0],
        grad_in,
        router_sum,
        conv_sum,
        heads[:, n_vec, LANES + 2],
        heads[:, n_vec, 2 * LANES + 2],
        total[4, :head_dim],
        grad_out,
        norms[1],
        grad_gu,
        grad_down,
    )


def solution(mesh):
    by_rows = P("seq", None)
    by_tokens = P(None, "row", "seq", None)
    return jax.shard_map(
        local,
        mesh=mesh,
        in_specs=(
            by_tokens, by_tokens, P(None, "row"), P(), by_rows, P(), P(), P(), P(), P(),
            by_rows, P(), by_rows, by_rows,
        ),
        out_specs=(
            by_tokens, by_tokens, P(), by_rows, P(), P(), P(), P(), P(),
            by_rows, P(), by_rows, by_rows,
        ),
        check_vma=False,
    )
```
